32 devices in a mesh: tensor: 4 (over x, core), dp: 8 (over z, y).
Axes of the slice: x: 2, y: 2, z: 4, core: 2. Of those that a mesh axis runs over, the one named last changes fastest.
Arguments:
- inputs: bfloat16 [16384, 768], P('dp'), may hold values from -6 to 6
- gain_attn: bfloat16 [768], replicated, may hold values from 0.25 to 1.75
- w_qkv: bfloat16 [3, 768, 768], P(None, None, 'tensor'), may hold values from -0.21875 to 0.21875
- w_out: bfloat16 [768, 768], P('tensor'), may hold values from -0.875 to 0.875
- gain_ffn: bfloat16 [768], replicated, may hold values from 0.25 to 1.75
- w_in: bfloat16 [768, 3072], P(None, 'tensor'), may hold values from -0.21875 to 0.21875
- w_back: bfloat16 [3072, 768], P('tensor'), may hold values from -0.109375 to 0.109375
- bias_table: bfloat16 [32, 12], P(None, 'tensor'), may hold values from -4 to 4
- lengths: int32 [32], P('dp'), may hold values from 51 to 512, as said below
- buckets: int32 [512, 512], replicated, may hold values from 0 to 31, as said below
- cotangent: bfloat16 [16384, 768], P('dp'), may hold values from -6 to 6
Outputs:
- mixed: bfloat16 [16384, 768], P('dp')
- grad_input: float32 [16384, 768], P('dp')
- grad_gain_attn: float32 [768], replicated
- grad_w_qkv: float32 [3, 768, 768], P(None, None, 'tensor')
- grad_w_out: float32 [768, 768], P('tensor')
- grad_gain_ffn: float32 [768], replicated
- grad_w_in: float32 [768, 3072], P(None, 'tensor')
- grad_w_back: float32 [3072, 768], P('tensor')
- grad_bias_table: float32 [32, 12], P(None, 'tensor')
The draws below stay inside these ranges and needn't reach their ends.
Inputs may be any that keep to these rules, and one draw needn't show every extreme that they name: `lengths`: every group of 4 consecutive documents holds one of 512 tokens. `buckets`: a function of j - i alone, never falling as |j - i| grows on either side of zero; larger when j > i than for the same |j - i| with j < i.
All inputs are finite; a program needn't handle non-finite values.
Results may differ from the reference program's by a relative error of at most 0.012.
Values may be sent and summed in bfloat16 or wider, within the bound.
No kernel may reach another device: no remote copies, remote signals or barrier semaphores. Data moves between devices by JAX's collectives and lax.ppermute only.
A program may use at most 192 MiB of HBM per device.

```python
import math
import jax
import jax.numpy as jnp
from jax import lax

D = 768
HEADS = 12
HD = 64
FF = 3072
BUCKETS = 32
SEQ = 512
DOCS_DEV = 4
DOCS = 32
TOKENS = 16384


def draw_lengths(key, part):
    key = jax.random.fold_in(key, 11)
    first_key, second_key = jax.random.split(key)
    drawn_len = jax.random.randint(first_key, (DOCS // DOCS_DEV, DOCS_DEV), SEQ // 10, SEQ + 1)
    chosen = jax.random.randint(second_key, (DOCS // DOCS_DEV, 1), 0, DOCS_DEV)
    is_full = jnp.arange(DOCS_DEV)[None, :] == chosen
    return jnp.where(is_full, SEQ, drawn_len).reshape(DOCS).astype(jnp.int32)


def draw_buckets(key, part):
    key = jax.random.fold_in(key, 23)
    exact_count = BUCKETS // 4
    half_count = BUCKETS // 2
    distance_row = jnp.arange(SEQ)
    steps_drawn = jax.random.randint(key, (2, SEQ), 0, SEQ)
    rising = ((steps_drawn < 3 * (half_count - exact_count)) & (distance_row[None, :] >= exact_count)).astype(jnp.int32)
    climbed = jnp.cumsum(rising, axis=1)
    far_bucket = jnp.minimum(exact_count + climbed, half_count - 1)
    far_bucket = jnp.where(distance_row[None, :] == SEQ - 1, half_count - 1, far_bucket)
    table = jnp.where(distance_row[None, :] < exact_count, distance_row[None, :], far_bucket).astype(jnp.int32)
    offsets = distance_row[None, :] - distance_row[:, None]
    distance = jnp.abs(offsets)
    side = (offsets > 0).astype(jnp.int32)
    inner = table[side, distance]
    return (inner + half_count * side).astype(jnp.int32)


def block_levels(key, dims, cuts, least, top_value):
    loudness = 1.0
    for dim, blocks in cuts:
        steps = jax.random.uniform(jax.random.fold_in(jax.random.fold_in(key, 6), dim), (blocks,), jnp.float32, least / len(cuts), top_value / len(cuts))
        loudness = loudness * jnp.repeat(jnp.exp(steps), dims[dim] // blocks).reshape((-1,) + (1,) * (len(dims) - 1 - dim))
    return loudness


def normal_values(stream_key, dims, spread, bound, cuts=(), kind=jnp.bfloat16):
    drawn = jax.random.normal(stream_key, dims, jnp.float32) * spread
    if len(cuts) > 0:
        drawn = block_levels(stream_key, dims, cuts, -0.22, 0.18) * drawn
    return jnp.clip(drawn, min=-bound, max=bound).astype(kind)


def setup_inputs(seed: int = 0) -> dict:
    arg_keys = jax.random.split(jax.random.key(seed), 12)
    return {
        "inputs": normal_values(arg_keys[0], (TOKENS, D), 1.0, 6.0, ((0, 8),)),
        "gain_attn": jnp.clip(1.0 + 0.15 * jax.random.normal(arg_keys[1], (D,), jnp.float32), 0.25, 1.75).astype(jnp.bfloat16),
        "w_qkv": normal_values(arg_keys[2], (3, D, D), D ** -0.5, 0.21875, ((2, 4),)),
        "w_out": normal_values(arg_keys[3], (D, D), (D // 16) ** -0.5, 0.875, ((0, 4),)),
        "gain_ffn": jnp.clip(1.0 + 0.15 * jax.random.normal(arg_keys[4], (D,), jnp.float32), 0.25, 1.75).astype(jnp.bfloat16),
        "w_in": normal_values(arg_keys[5], (D, FF), D ** -0.5, 0.21875, ((1, 4),)),
        "w_back": normal_values(arg_keys[6], (FF, D), FF ** -0.5, 0.109375, ((0, 4),)),
        "bias_table": normal_values(arg_keys[7], (BUCKETS, HEADS), 1.0, 4.0, ((1, 4),)),
        "lengths": draw_lengths(jax.random.fold_in(arg_keys[11], 71), 0),
        "buckets": draw_buckets(jax.random.fold_in(arg_keys[11], 71), 0),
        "cotangent": normal_values(arg_keys[10], (TOKENS, D), 1.0, 6.0, ((0, 8),)),
    }


@jax.custom_vjp
def low(v):
    return lax.optimization_barrier(v.astype(jnp.bfloat16)).astype(jnp.float32)

@jax.custom_vjp
def low_back(v):
    return v

def low_keep(v):
    return (low(v), None)

def low_pass(kept, grad):
    return (grad,)

def back_keep(v):
    return (v, None)

def back_low(kept, grad):
    return (low(grad),)
low.defvjp(low_keep, low_pass)
low_back.defvjp(back_keep, back_low)
epsilon = 1e-06
masked_score = -1000000000.0
gelu_coeff = 0.7978845608028654

def highest(first, second):
    return jnp.dot(first, second, precision=lax.Precision.HIGHEST)

def rms_norm(values, gain_vec):
    return values * lax.rsqrt(lax.optimization_barrier(jnp.mean(values * values, axis=-1, keepdims=True)) + epsilon) * gain_vec

def gelu_tanh(values):
    return 0.5 * values * (1.0 + jnp.tanh(gelu_coeff * (values + 0.044715 * values * values * values)))

def layer_forward(source, gain_attn, w_qkv, w_out, gain_ffn, w_in, w_back, bias_table, lengths, buckets):
    docs_here = lengths.shape[0]
    score_scale = 1.0 / math.sqrt(HD)
    normed = low(rms_norm(source, gain_attn))
    packed = low(low_back(jnp.einsum('td,cde->cte', normed, w_qkv, precision=lax.Precision.HIGHEST)))
    head_split = packed.reshape(3, docs_here, SEQ, HEADS, HD).transpose(0, 1, 3, 2, 4)
    relative = jnp.moveaxis(bias_table[buckets], -1, 0)
    positions = jnp.arange(SEQ)

    def one_document(pieces):
        doc_queries, doc_keys, doc_values, doc_length = pieces
        scores = jnp.einsum('hqe,hke->hqk', doc_queries, doc_keys, precision=lax.Precision.HIGHEST) * score_scale + relative
        scores = low_back(jnp.where(positions[None, None, :] < doc_length, scores, masked_score))
        shifted = jnp.exp(scores - lax.optimization_barrier(jnp.max(scores, axis=-1, keepdims=True)))
        softmax_probs = shifted / lax.optimization_barrier(jnp.sum(shifted, axis=-1, keepdims=True))
        return jnp.einsum('hqk,hke->hqe', low(softmax_probs), doc_values, precision=lax.Precision.HIGHEST)
    mixed_heads = lax.map(jax.checkpoint(one_document), (head_split[0], head_split[1], head_split[2], lengths))
    attended = low(low_back(mixed_heads.transpose(0, 2, 1, 3).reshape(docs_here * SEQ, HEADS * HD)))
    middle = source + low_back(highest(attended, w_out))
    normed_second = low(rms_norm(middle, gain_ffn))
    hidden = low(gelu_tanh(low_back(highest(normed_second, w_in))))
    return middle + highest(hidden, w_back)

def reference(inputs, gain_attn, w_qkv, w_out, gain_ffn, w_in, w_back, bias_table, lengths, buckets, cotangent):
    group_docs = math.gcd(DOCS, max(1, 4096 // SEQ))
    rounds = DOCS // group_docs
    weights = tuple((weight_arg.astype(jnp.float32) for weight_arg in (gain_attn, w_qkv, w_out, gain_ffn, w_in, w_back, bias_table)))
    sources = inputs.astype(jnp.float32).reshape(rounds, group_docs * SEQ, D)
    cotangents = cotangent.astype(jnp.float32).reshape(rounds, group_docs * SEQ, D)
    doc_lengths = lengths.reshape(rounds, group_docs).astype(jnp.int32)

    def group_step(totals, pieces):
        source, doc_length, incoming = pieces

        def forward(source_in, *params):
            return layer_forward(source_in, *params, doc_length, buckets)
        output, pullback = jax.vjp(forward, source, *weights)
        gradients = pullback(incoming)
        totals = jax.tree.map(jnp.add, totals, tuple(gradients[1:]))
        return (totals, (output.astype(jnp.bfloat16), gradients[0]))
    initial = tuple((jnp.zeros(weight_arg.shape, jnp.float32) for weight_arg in weights))
    totals, (outputs, grads_in) = lax.scan(group_step, initial, (sources, doc_lengths, cotangents))
    return (outputs.reshape(TOKENS, D), grads_in.reshape(TOKENS, D), totals[0], totals[1], totals[2], totals[3], totals[4], totals[5], totals[6])
```

```python
import functools
import math

import jax
import jax.numpy as jnp
from jax import lax
from jax.experimental import pallas as pl
from jax.experimental.pallas import tpu as pltpu
from jax.sharding import PartitionSpec as P

HD = 64
PAIR = 2 * HD
EPS = 1e-06
MASKED = -1000000000.0
GELU_C = 0.7978845608028654
GELU_A = 0.044715
VMEM_BYTES = 60 * 1024 * 1024

F32 = jnp.float32
BF16 = jnp.bfloat16


def dot_nn(a, b):
    return lax.dot_general(a, b, (((1,), (0,)), ((), ())), preferred_element_type=F32)


def dot_nt(a, b):
    return lax.dot_general(a, b, (((1,), (1,)), ((), ())), preferred_element_type=F32)


def dot_tn(a, b):
    return lax.dot_general(a, b, (((0,), (0,)), ((), ())), preferred_element_type=F32)


def params():
    return pltpu.CompilerParams(vmem_limit_bytes=VMEM_BYTES)


def whole(shape):
    return pl.BlockSpec(shape, lambda *_: (0,) * len(shape))


def norm_kernel(src_ref, gain_ref, out_ref):
    v = src_ref[...].astype(F32)
    r = lax.rsqrt(jnp.mean(v * v, axis=-1, keepdims=True) + EPS)
    out_ref[...] = (v * r * gain_ref[...]).astype(BF16)


def norm_rows(src, gain):
    rows, width = src.shape
    return pl.pallas_call(
        norm_kernel,
        grid=(4,),
        in_specs=[pl.BlockSpec((rows // 4, width), lambda i: (i, 0)), whole((1, width))],
        out_specs=pl.BlockSpec((rows // 4, width), lambda i: (i, 0)),
        out_shape=jax.ShapeDtypeStruct((rows, width), BF16),
        compiler_params=params(),
        name="norm_rows",
    )(src, gain)


def attn_fwd_kernel(docs, seq, len_ref, normed_ref, w_ref, u_ref, packed_ref, probs_ref, att_ref):
    packed = dot_nn(normed_ref[...], w_ref[:, : 3 * PAIR])
    lane = lax.broadcasted_iota(jnp.int32, (seq, PAIR), 1)
    scale = 1.0 / math.sqrt(HD)
    packed_ref[:, :PAIR] = (packed[:, :PAIR].astype(BF16).astype(F32) * scale).astype(BF16)
    packed_ref[:, PAIR:] = packed[:, PAIR:].astype(BF16)
    key_pos = lax.broadcasted_iota(jnp.int32, (seq, 1), 0)
    for head in range(2):
        row = jnp.broadcast_to(u_ref[0, head : head + 1, :], (seq, 2 * seq))
        rel = pltpu.roll(row, 0, 1, stride=1, stride_axis=0)[:, :seq]
        mine = (lane >= HD) if head else (lane < HD)
        for doc in range(docs):
            rows = slice(doc * seq, (doc + 1) * seq)
            q = packed_ref[rows, :PAIR]
            k = packed_ref[rows, PAIR : 2 * PAIR]
            v = packed_ref[rows, 2 * PAIR :]
            k = jnp.where(mine, k, jnp.zeros_like(k))
            scores = dot_nt(k, q) + rel
            scores = jnp.where(key_pos < len_ref[doc], scores, MASKED)
            top = jnp.max(scores, axis=0, keepdims=True)
            e = jnp.exp(scores - top)
            total = jnp.sum(e, axis=0, keepdims=True)
            p = (e * (1.0 / total)).astype(BF16)
            probs_ref[doc, head] = p
            vt = v.T[head * HD : (head + 1) * HD, :]
            o = dot_nn(vt, p)
            att_ref[rows, head * HD : (head + 1) * HD] = o.T.astype(BF16)


def attn_fwd(normed, w_half, u_half, lengths, docs, seq):
    rows, width = normed.shape
    pairs = u_half.shape[0]
    return pl.pallas_call(
        functools.partial(attn_fwd_kernel, docs, seq),
        grid=(pairs,),
        in_specs=[
            pl.BlockSpec(memory_space=pltpu.SMEM),
            whole((rows, width)),
            pl.BlockSpec((width, 4 * PAIR), lambda p: (0, p)),
            pl.BlockSpec((1, 2, 2 * seq), lambda p: (p, 0, 0)),
        ],
        out_specs=[
            pl.BlockSpec((rows, 3 * PAIR), lambda p: (0, p)),
            pl.BlockSpec((docs, 2, seq, seq), lambda p: (0, p, 0, 0)),
            pl.BlockSpec((rows, PAIR), lambda p: (0, p)),
        ],
        out_shape=[
            jax.ShapeDtypeStruct((rows, pairs * 3 * PAIR), BF16),
            jax.ShapeDtypeStruct((docs, 2 * pairs, seq, seq), BF16),
            jax.ShapeDtypeStruct((rows, pairs * PAIR), BF16),
        ],
        compiler_params=params(),
        name="attn_fwd",
    )(lengths, normed, w_half, u_half)


def fold_diagonals(g, seq):
    g = jnp.concatenate([g, jnp.zeros_like(g)], axis=1)
    n = seq
    while n > 8:
        n //= 2
        g = g[:n] + pltpu.roll(g[n:], 2 * seq - n, 1)
    while n > 1:
        n //= 2
        g = g[:n] + jnp.concatenate([g[n:, n:], g[n:, :n]], axis=1)
    return g


def attn_bwd_kernel(docs, seq, packed_ref, probs_ref, dout_ref, gp_ref, diag_ref):
    lane = lax.broadcasted_iota(jnp.int32, (seq, PAIR), 1)
    scale = 1.0 / math.sqrt(HD)
    sums = [None, None]
    for doc in range(docs):
        rows = slice(doc * seq, (doc + 1) * seq)
        q = packed_ref[rows, :PAIR]
        k = packed_ref[rows, PAIR : 2 * PAIR]
        v = packed_ref[rows, 2 * PAIR :]
        do = dout_ref[rows, :]
        kt = k.T
        dqs, dks, dvs = [], [], []
        for head in range(2):
            mine = (lane >= HD) if head else (lane < HD)
            vm = jnp.where(mine, v, jnp.zeros_like(v))
            dp = dot_nt(vm, do)
            p_low = probs_ref[doc, head]
            p = p_low.astype(F32)
            mean = jnp.sum(dp * p, axis=0, keepdims=True)
            ds = (p * (dp - mean)).astype(BF16)
            ds32 = ds.astype(F32)
            sums[head] = ds32 if sums[head] is None else sums[head] + ds32
            dvs.append(dot_nn(p_low, do))
            dks.append(dot_nn(ds, q))
            dqs.append(dot_nn(kt[head * HD : (head + 1) * HD, :], ds))
        dq = jnp.concatenate(dqs, axis=0).T * scale
        first = lane < HD
        gp_ref[rows, :PAIR] = dq.astype(BF16)
        gp_ref[rows, PAIR : 2 * PAIR] = jnp.where(first, dks[0], dks[1]).astype(BF16)
        gp_ref[rows, 2 * PAIR :] = jnp.where(first, dvs[0], dvs[1]).astype(BF16)
    for head in range(2):
        diag_ref[0, head : head + 1, :] = fold_diagonals(sums[head], seq)


def attn_bwd(packed, probs, dout, docs, seq):
    rows = packed.shape[0]
    pairs = packed.shape[1] // (3 * PAIR)
    return pl.pallas_call(
        functools.partial(attn_bwd_kernel, docs, seq),
        grid=(pairs,),
        in_specs=[
            pl.BlockSpec((rows, 3 * PAIR), lambda p: (0, p)),
            pl.BlockSpec((docs, 2, seq, seq), lambda p: (0, p, 0, 0)),
            pl.BlockSpec((rows, PAIR), lambda p: (0, p)),
        ],
        out_specs=[
            pl.BlockSpec((rows, 3 * PAIR), lambda p: (0, p)),
            pl.BlockSpec((1, 2, 2 * seq), lambda p: (p, 0, 0)),
        ],
        out_shape=[
            jax.ShapeDtypeStruct((rows, pairs * 3 * PAIR), BF16),
            jax.ShapeDtypeStruct((pairs, 2, 2 * seq), F32),
        ],
        compiler_params=params(),
        name="attn_bwd",
    )(packed, probs, dout)


CHUNK = 256


def out_proj_weight(w_ref):
    pairs = w_ref.shape[1] // (4 * PAIR)
    return jnp.concatenate(
        [w_ref[:, (4 * p + 3) * PAIR : (4 * p + 4) * PAIR] for p in range(pairs)], axis=1
    )


def ffn_half(step, normed_ref, cot_ref, w_in, w_back, acc_ref, gacc_ref, hid_ref, gpre_ref):
    rows = normed_ref.shape[0]
    for start in range(0, rows, CHUNK):
        at = slice(start, start + CHUNK)
        pre = dot_nn(normed_ref[at, :], w_in)
        ghid = dot_nt(cot_ref[at, :], w_back)
        sq = pre * pre
        t = jnp.tanh(GELU_C * (pre + GELU_A * sq * pre))
        half_t = 0.5 * (1.0 + t)
        hidden = (pre * half_t).astype(BF16)
        slope = half_t + 0.5 * pre * (1.0 - t * t) * (GELU_C * (1.0 + 3.0 * GELU_A * sq))
        gpre = (ghid * slope).astype(BF16)
        out = dot_nn(hidden, w_back)
        gnorm = dot_nt(gpre, w_in)
        if hid_ref is not None:
            hid_ref[at, :] = hidden
            gpre_ref[at, :] = gpre

        @pl.when(step == 0)
        def _():
            acc_ref[at, :] = out
            gacc_ref[at, :] = gnorm

        @pl.when(step != 0)
        def _():
            acc_ref[at, :] += out
            gacc_ref[at, :] += gnorm


def ffn_a_kernel(
    src_ref,
    att_own_ref,
    att_oth_ref,
    wa_own_ref,
    wa_oth_ref,
    gain_ref,
    cot_ref,
    in_a_ref,
    in_b_ref,
    back_a_ref,
    back_b_ref,
    middle_ref,
    normed_ref,
    acc_ref,
    gacc_ref,
    gback_ref,
    gin_ref,
    hid_ref,
    gpre_ref,
):
    step = pl.program_id(0)
    rows = src_ref.shape[0]

    @pl.when(step == 0)
    def _():
        wo_own = out_proj_weight(wa_own_ref)
        wo_oth = out_proj_weight(wa_oth_ref)
        for start in range(0, rows, CHUNK):
            at = slice(start, start + CHUNK)
            terms = dot_nt(att_own_ref[at, :], wo_own) + dot_nt(att_oth_ref[at, :], wo_oth)
            m = src_ref[at, :].astype(F32) + terms
            r = lax.rsqrt(jnp.mean(m * m, axis=-1, keepdims=True) + EPS)
            middle_ref[at, :] = m
            normed_ref[at, :] = (m * r * gain_ref[...]).astype(BF16)

    w_in = jnp.where(step == 0, in_a_ref[...], in_b_ref[...])
    w_back = jnp.where(step == 0, back_a_ref[...], back_b_ref[...])
    ffn_half(step, normed_ref, cot_ref, w_in, w_back, acc_ref, gacc_ref, hid_ref, gpre_ref)
    gback_ref[0] = dot_tn(hid_ref[...], cot_ref[...]).astype(BF16)
    gin_ref[0] = dot_tn(normed_ref[...], gpre_ref[...]).astype(BF16)


def ffn_a(src, att_own, att_oth, wa_own, wa_oth, gain, cot, in_a, in_b, back_a, back_b):
    rows, width = src.shape
    units = in_a.shape[1]
    args = (src, att_own, att_oth, wa_own, wa_oth, gain, cot, in_a, in_b, back_a, back_b)
    return pl.pallas_call(
        ffn_a_kernel,
        grid=(2,),
        in_specs=[whole(a.shape) for a in args],
        out_specs=[
            whole((rows, width)),
            whole((rows, width)),
            whole((rows, width)),
            whole((rows, width)),
            pl.BlockSpec((1, units, width), lambda i: (i, 0, 0)),
            pl.BlockSpec((1, width, units), lambda i: (i, 0, 0)),
        ],
        out_shape=[
            jax.ShapeDtypeStruct((rows, width), F32),
            jax.ShapeDtypeStruct((rows, width), BF16),
            jax.ShapeDtypeStruct((rows, width), F32),
            jax.ShapeDtypeStruct((rows, width), F32),
            jax.ShapeDtypeStruct((2, units, width), BF16),
            jax.ShapeDtypeStruct((2, width, units), BF16),
        ],
        scratch_shapes=[pltpu.VMEM((rows, units), BF16), pltpu.VMEM((rows, units), BF16)],
        compiler_params=params(),
        name="ffn_a",
    )(*args)


def ffn_b_kernel(
    middle_ref,
    normed_ref,
    acc_a_ref,
    gacc_a_ref,
    att_own_ref,
    wa_own_ref,
    wa_oth_ref,
    gain_ref,
    cot_ref,
    in_a_ref,
    in_b_ref,
    back_a_ref,
    back_b_ref,
    mixed_ref,
    gmid_ref,
    ggain_ref,
    gwout_ref,
    do_own_ref,
    do_oth_ref,
    acc_ref,
    gacc_ref,
    low_ref,
):
    step = pl.program_id(0)
    rows = middle_ref.shape[0]
    w_in = jnp.where(step == 0, in_a_ref[...], in_b_ref[...])
    w_back = jnp.where(step == 0, back_a_ref[...], back_b_ref[...])
    ffn_half(step, normed_ref, cot_ref, w_in, w_back, acc_ref, gacc_ref, None, None)

    @pl.when(step == 1)
    def _():
        wo_own = out_proj_weight(wa_own_ref)
        wo_oth = out_proj_weight(wa_oth_ref)
        ggain = jnp.zeros(ggain_ref.shape, F32)
        for start in range(0, rows, CHUNK):
            at = slice(start, start + CHUNK)
            m = middle_ref[at, :]
            mixed_ref[at, :] = (m + (acc_a_ref[at, :] + acc_ref[at, :])).astype(BF16)
            gnorm = gacc_a_ref[at, :] + gacc_ref[at, :]
            r = lax.rsqrt(jnp.mean(m * m, axis=-1, keepdims=True) + EPS)
            ggain = ggain + jnp.sum(gnorm * m * r, axis=0, keepdims=True)
            back = gain_ref[...] * gnorm
            inner = jnp.mean(back * m, axis=-1, keepdims=True)
            gm = cot_ref[at, :].astype(F32) + r * back - m * (r * r * r * inner)
            gmid_ref[at, :] = gm
            low = gm.astype(BF16)
            low_ref[at, :] = low
            do_own_ref[at, :] = dot_nn(low, wo_own).astype(BF16)
            do_oth_ref[at, :] = dot_nn(low, wo_oth).astype(BF16)
        ggain_ref[...] = ggain
        gwout_ref[...] = dot_tn(att_own_ref[...], low_ref[...]).astype(BF16)


def ffn_b(middle, normed, acc_a, gacc_a, att_own, wa_own, wa_oth, gain, cot, in_a, in_b, back_a, back_b):
    rows, width = middle.shape
    half = att_own.shape[1]
    args = (middle, normed, acc_a, gacc_a, att_own, wa_own, wa_oth, gain, cot, in_a, in_b, back_a, back_b)
    outs = [
        jax.ShapeDtypeStruct((rows, width), BF16),
        jax.ShapeDtypeStruct((rows, width), F32),
        jax.ShapeDtypeStruct((1, width), F32),
        jax.ShapeDtypeStruct((half, width), BF16),
        jax.ShapeDtypeStruct((rows, half), BF16),
        jax.ShapeDtypeStruct((rows, half), BF16),
    ]
    return pl.pallas_call(
        ffn_b_kernel,
        grid=(2,),
        in_specs=[whole(a.shape) for a in args],
        out_specs=[whole(o.shape) for o in outs],
        out_shape=outs,
        scratch_shapes=[
            pltpu.VMEM((rows, width), F32),
            pltpu.VMEM((rows, width), F32),
            pltpu.VMEM((rows, width), BF16),
        ],
        compiler_params=params(),
        name="ffn_b",
    )(*args)


def grad_qkv_kernel(normed_ref, gp_ref, out_ref):
    out_ref[...] = dot_tn(normed_ref[...], gp_ref[...]).astype(BF16)


def grad_qkv(normed, gp):
    rows, width = normed.shape
    pairs = gp.shape[1] // (3 * PAIR)
    return pl.pallas_call(
        grad_qkv_kernel,
        grid=(pairs,),
        in_specs=[whole((rows, width)), pl.BlockSpec((rows, 3 * PAIR), lambda p: (0, p))],
        out_specs=pl.BlockSpec((width, 3 * PAIR), lambda p: (0, p)),
        out_shape=jax.ShapeDtypeStruct((width, gp.shape[1]), BF16),
        compiler_params=params(),
        name="grad_qkv",
    )(normed, gp)


def grad_input_kernel(src_ref, gmid_ref, gain_ref, gp_own_ref, gp_oth_ref, wa_own_ref, wa_oth_ref, out_ref, ggain_ref):
    rows = src_ref.shape[0]
    pairs = wa_own_ref.shape[1] // (4 * PAIR)

    def weight(ref):
        return jnp.concatenate(
            [ref[:, 4 * p * PAIR : (4 * p + 3) * PAIR] for p in range(pairs)], axis=1
        )

    w_own, w_oth = weight(wa_own_ref), weight(wa_oth_ref)
    ggain = jnp.zeros(ggain_ref.shape, F32)
    for start in range(0, rows, CHUNK):
        at = slice(start, start + CHUNK)
        gnorm = dot_nt(gp_own_ref[at, :], w_own) + dot_nt(gp_oth_ref[at, :], w_oth)
        v = src_ref[at, :].astype(F32)
        r = lax.rsqrt(jnp.mean(v * v, axis=-1, keepdims=True) + EPS)
        ggain = ggain + jnp.sum(gnorm * v * r, axis=0, keepdims=True)
        back = gain_ref[...] * gnorm
        inner = jnp.mean(back * v, axis=-1, keepdims=True)
        out_ref[at, :] = gmid_ref[at, :] + r * back - v * (r * r * r * inner)
    ggain_ref[...] = ggain


def grad_input(src, gmid, gain, gp_own, gp_oth, wa_own, wa_oth):
    rows, width = src.shape
    args = (src, gmid, gain, gp_own, gp_oth, wa_own, wa_oth)
    return pl.pallas_call(
        grad_input_kernel,
        grid=(1,),
        in_specs=[whole(a.shape) for a in args],
        out_specs=[whole((rows, width)), whole((1, width))],
        out_shape=[
            jax.ShapeDtypeStruct((rows, width), F32),
            jax.ShapeDtypeStruct((1, width), F32),
        ],
        compiler_params=params(),
        name="grad_input",
    )(*args)


def swap(v, axis, size, bit):
    return lax.ppermute(v, axis, [(i, i ^ bit) for i in range(size)])


def ordered(flag, mine, other):
    return jnp.where(
        flag == 0,
        jnp.concatenate([mine, other], axis=0),
        jnp.concatenate([other, mine], axis=0),
    )


def sum_over_dp(cur, dp, me):
    stages = [1 << s for s in range(dp.bit_length() - 1)]
    for bit in stages:
        flag = (me // bit) % 2
        half = cur.shape[0] // 2
        send = lax.dynamic_slice_in_dim(cur, (1 - flag) * half, half, 0)
        keep = lax.dynamic_slice_in_dim(cur, flag * half, half, 0)
        got = swap(send, "dp", dp, bit)
        cur = (keep.astype(F32) + got.astype(F32)).astype(BF16)
    for bit in reversed(stages):
        flag = (me // bit) % 2
        cur = ordered(flag, cur, swap(cur, "dp", dp, bit))
    return cur.astype(F32)


def per_device(dp, inputs, gain_attn, w_qkv, w_out, gain_ffn, w_in, w_back, bias_table, lengths, buckets, cotangent):
    t = lax.axis_index("tensor")
    me = lax.axis_index("dp")
    core = t % 2
    width = inputs.shape[1]
    rows = inputs.shape[0] // 2
    seq = buckets.shape[0]
    docs = lengths.shape[0] // 2
    heads = bias_table.shape[1]
    table_rows = bias_table.shape[0]
    cols = heads * HD
    pairs = heads

    src = lax.dynamic_slice_in_dim(inputs, core * rows, rows, 0)
    cot = lax.dynamic_slice_in_dim(cotangent, core * rows, rows, 0)
    lens = lax.dynamic_slice_in_dim(lengths, core * docs, docs, 0)
    gain_one = gain_attn.astype(F32).reshape(1, width)
    gain_two = gain_ffn.astype(F32).reshape(1, width)

    attn_w = jnp.concatenate([w_qkv[0], w_qkv[1], w_qkv[2], w_out.T], axis=1)

    def from_core(v):
        return swap(v, "tensor", 4, 1)

    def from_x(v):
        flag = me % 2
        half = v.shape[0] // 2
        part = lax.dynamic_slice_in_dim(v, flag * half, half, 0)
        part = swap(part, "tensor", 4, 2)
        return ordered(flag, part, swap(part, "dp", dp, 1))

    attn_c = from_core(attn_w)
    in_c = from_core(w_in)
    back_c = from_core(w_back)
    attn_x = from_x(attn_w)
    attn_xc = from_core(attn_x)
    in_x = from_x(w_in)
    in_xc = from_core(in_x)
    back_x = from_x(w_back)
    back_xc = from_core(back_x)

    def by_pair(a, b):
        both = jnp.stack([a.reshape(width, 4, heads, HD), b.reshape(width, 4, heads, HD)], axis=2)
        both = both.reshape(width, 4, pairs, PAIR).transpose(0, 2, 1, 3)
        return both.reshape(width, pairs * 4 * PAIR)

    wa_own = by_pair(attn_w, attn_c)
    wa_oth = by_pair(attn_x, attn_xc)

    diag_bucket = jnp.concatenate([buckets[:, 0], buckets[0, :1], buckets[0, 1:][::-1]])
    one_hot = diag_bucket[:, None] == jnp.arange(table_rows)[None, :]
    table_all = lax.all_gather(bias_table.T.astype(F32), "tensor", tiled=False)
    along = jnp.sum(
        jnp.where(one_hot[None, None], table_all[:, :, None, :], 0.0), axis=-1
    )

    def along_of(first, second):
        picked = jnp.stack(
            [
                lax.dynamic_index_in_dim(along, first, 0, keepdims=False),
                lax.dynamic_index_in_dim(along, second, 0, keepdims=False),
            ]
        )
        return picked.reshape(pairs, 2, 2 * seq)

    chip = t // 2
    u_own = along_of(2 * chip + core, 2 * chip + 1 - core)
    u_oth = along_of(2 * (1 - chip) + core, 2 * (1 - chip) + 1 - core)

    normed = norm_rows(src, gain_one)
    packed_own, probs_own, att_own = attn_fwd(normed, wa_own, u_own, lens, docs, seq)
    packed_oth, probs_oth, att_oth = attn_fwd(normed, wa_oth, u_oth, lens, docs, seq)
    middle, normed2, acc_a, gacc_a, gback, gin = ffn_a(
        src, att_own, att_oth, wa_own, wa_oth, gain_two, cot, w_in, in_c, w_back, back_c
    )

    def sum_core(mine, other):
        return (mine.astype(F32) + from_core(other).astype(F32)).astype(BF16)

    grad_w_back = sum_over_dp(sum_core(gback[0], gback[1]), dp, me)
    grad_w_in = sum_over_dp(sum_core(gin[0], gin[1]), dp, me)
    mixed, gmid, ggain_two, gwout, do_own, do_oth = ffn_b(
        middle, normed2, acc_a, gacc_a, att_own, wa_own, wa_oth, gain_two, cot, in_x, in_xc, back_x, back_xc
    )
    grad_w_out = sum_over_dp(sum_core(gwout[:cols], gwout[cols:]), dp, me)
    gp_own, diag_own = attn_bwd(packed_own, probs_own, do_own, docs, seq)
    gqkv = grad_qkv(normed, gp_own)
    gqkv = gqkv.reshape(width, pairs, 3, PAIR).transpose(0, 2, 1, 3).reshape(width, 3, 2 * cols)
    gq_mine = gqkv[:, :, :cols].reshape(width, 3 * cols)
    gq_other = gqkv[:, :, cols:].reshape(width, 3 * cols)
    grad_w_qkv = sum_over_dp(sum_core(gq_mine, gq_other), dp, me)
    grad_w_qkv = grad_w_qkv.reshape(width, 3, cols).transpose(1, 0, 2)
    gp_oth, _ = attn_bwd(packed_oth, probs_oth, do_oth, docs, seq)
    gsrc, ggain_one = grad_input(src, gmid, gain_one, gp_own, gp_oth, wa_own, wa_oth)

    diag = diag_own.reshape(2 * heads, 2 * seq)
    table = jnp.sum(jnp.where(one_hot[None], diag[:, :, None], 0.0), axis=1)
    table = ordered(0, table[:heads], table[heads:])
    table_sum = table[:heads] + from_core(table[heads:])
    small = jnp.concatenate([ggain_one, ggain_two], axis=1)
    small = small + from_core(small)
    small = jnp.concatenate([small.reshape(-1), table_sum.reshape(-1)])
    for s in range(dp.bit_length() - 1):
        small = small + swap(small, "dp", dp, 1 << s)
    grad_gain_attn = small[:width]
    grad_gain_ffn = small[width : 2 * width]
    grad_table = small[2 * width :].reshape(heads, table_rows).T

    mixed_all = ordered(core, mixed, from_core(mixed))
    grad_in_all = ordered(core, gsrc, from_core(gsrc))
    return (
        mixed_all,
        grad_in_all,
        grad_gain_attn,
        grad_w_qkv,
        grad_w_out,
        grad_gain_ffn,
        grad_w_in,
        grad_w_back,
        grad_table,
    )


def solution(mesh):
    return jax.shard_map(
        functools.partial(per_device, mesh.shape["dp"]),
        mesh=mesh,
        in_specs=(
            P("dp", None),
            P(),
            P(None, None, "tensor"),
            P("tensor", None),
            P(),
            P(None, "tensor"),
            P("tensor", None),
            P(None, "tensor"),
            P("dp"),
            P(),
            P("dp", None),
        ),
        out_specs=(
            P("dp", None),
            P("dp", None),
            P(),
            P(None, None, "tensor"),
            P("tensor", None),
            P(),
            P(None, "tensor"),
            P("tensor", None),
            P(None, "tensor"),
        ),
        check_vma=False,
    )
```

```python
import functools
import math

import jax
import jax.numpy as jnp
from jax import lax
from jax.experimental import pallas as pl
from jax.experimental.pallas import tpu as pltpu
from jax.sharding import PartitionSpec as P

HD = 64
PAIR = 2 * HD
EPS = 1e-06
MASKED = -1000000000.0
GELU_C = 0.7978845608028654
GELU_A = 0.044715
CHUNK = 256
VMEM_BYTES = 60 * 1024 * 1024

F32 = jnp.float32
BF16 = jnp.bfloat16


def dot_nn(a, b):
    return lax.dot_general(a, b, (((1,), (0,)), ((), ())), preferred_element_type=F32)


def dot_nt(a, b):
    return lax.dot_general(a, b, (((1,), (1,)), ((), ())), preferred_element_type=F32)


def dot_tn(a, b):
    return lax.dot_general(a, b, (((0,), (0,)), ((), ())), preferred_element_type=F32)


def whole(shape):
    return pl.BlockSpec(shape, lambda *_: (0,) * len(shape))


def shape_of(shape, dtype):
    return jax.ShapeDtypeStruct(shape, dtype)


def call(kernel, name, token, args, in_specs, outs, out_specs, grid=(1,), scratch=(), aliases=None):
    n_in, n_out = len(args), len(outs)

    def body(token_ref, *refs):
        del token_ref
        kernel(*refs[:n_in], *refs[n_in + 1 :])

    anywhere = pl.BlockSpec(memory_space=pl.ANY)
    res = pl.pallas_call(
        body,
        grid=grid,
        in_specs=[anywhere] + list(in_specs),
        out_specs=[anywhere] + list(out_specs),
        scratch_shapes=list(scratch),
        out_shape=[shape_of(token.shape, token.dtype)] + list(outs),
        input_output_aliases={0: 0, **(aliases or {})},
        compiler_params=pltpu.CompilerParams(vmem_limit_bytes=VMEM_BYTES),
        name=name,
    )(token, *args)
    return res[1:], res[0]


def rms_rows(v):
    return lax.rsqrt(jnp.mean(v * v, axis=-1, keepdims=True) + EPS)


def doc_rows(seq, width, docs, doc):
    return pl.BlockSpec((seq, width), lambda i: (lax.axis_index("core") * docs + doc, 0))


BIAS_ROWS = 16


def assemble(first_ref, second_ref, w_ref, width):
    cols = width // 4
    heads = cols // HD
    sources = [(first_ref, h) for h in range(heads)] + [(second_ref, h) for h in range(heads)]
    for p in range(heads):
        for part in range(3):
            for i in range(2):
                ref, head = sources[2 * p + i]
                src = part * cols + head * HD
                dst = (3 * p + part) * PAIR + i * HD
                w_ref[dst : dst + HD, :] = ref[src : src + HD, :]


def bias_along(first_ref, second_ref, left_ref, right_ref, u_ref, width):
    seq = left_ref.shape[0]
    left = left_ref[...].astype(F32).T[:1, :]
    right = right_ref[...].astype(F32).T[PAIR - 1 :, :]
    bucket = jnp.concatenate([left, pltpu.roll(right, 1, 1)], axis=1)
    index = lax.broadcasted_iota(jnp.int32, (PAIR, 2 * seq), 0).astype(F32)
    one_hot = (index == bucket).astype(BF16)
    heads = width // 4 // HD
    for at, ref in ((0, first_ref), (heads, second_ref)):
        u = dot_nn(ref[width:, :PAIR], one_hot)
        u_ref[at : at + heads, :] = u[:heads]


def attn_fwd_kernel(
    first, doc, docs, seq, len_ref, src_ref, gains_ref, *refs
):
    step = pl.program_id(0)
    if first:
        first_ref, second_ref, left_ref, right_ref, w_ref, u_ref, *refs = refs
    else:
        w_ref, u_ref, *refs = refs
    normed_ref, packed_ref, probs_ref, att_ref = refs

    @pl.when(step == 0)
    def _():
        if first:
            assemble(first_ref, second_ref, w_ref, src_ref.shape[1])
            bias_along(first_ref, second_ref, left_ref, right_ref, u_ref, src_ref.shape[1])
        for start in range(0, src_ref.shape[0], CHUNK):
            at = slice(start, start + CHUNK)
            v = src_ref[at, :].astype(F32)
            normed_ref[at, :] = (v * rms_rows(v) * gains_ref[:1, :]).astype(BF16)

    at = pl.multiple_of(step * 3 * PAIR, 3 * PAIR)
    packed = dot_nt(normed_ref[...], w_ref[pl.ds(at, 3 * PAIR), :])
    lane = lax.broadcasted_iota(jnp.int32, (seq, PAIR), 1)
    scale = 1.0 / math.sqrt(HD)
    packed_ref[:, :PAIR] = (packed[:, :PAIR].astype(BF16).astype(F32) * scale).astype(BF16)
    packed_ref[:, PAIR:] = packed[:, PAIR:].astype(BF16)
    key_pos = lax.broadcasted_iota(jnp.int32, (seq, 1), 0)
    length = len_ref[lax.axis_index("core") * docs + doc]
    for head in range(2):
        row = jnp.broadcast_to(u_ref[pl.ds(2 * step + head, 1), :], (seq, 2 * seq))
        rel = pltpu.roll(row, 0, 1, stride=1, stride_axis=0)[:, :seq]
        mine = (lane >= HD) if head else (lane < HD)
        q = packed_ref[:, :PAIR]
        k = packed_ref[:, PAIR : 2 * PAIR]
        v = packed_ref[:, 2 * PAIR :]
        k = jnp.where(mine, k, jnp.zeros_like(k))
        scores = dot_nt(k, q) + rel
        scores = jnp.where(key_pos < length, scores, MASKED)
        top = jnp.max(scores, axis=0, keepdims=True)
        e = jnp.exp(scores - top)
        total = jnp.sum(e, axis=0, keepdims=True)
        p = (e * (1.0 / total)).astype(BF16)
        probs_ref[head] = p
        vt = v.T[head * HD : (head + 1) * HD, :]
        o = dot_nn(vt, p)
        att_ref[:, head * HD : (head + 1) * HD] = o.T.astype(BF16)


def attn_fwd(ids, lengths, inputs, gains, weights, buckets, doc, docs):
    seq = buckets.shape[0]
    width = inputs.shape[1]
    pairs = width // (4 * HD)
    first = doc == 0
    specs = [pl.BlockSpec(memory_space=pltpu.SMEM), doc_rows(seq, width, docs, doc), whole(gains.shape)]
    args = (lengths, inputs, gains) + tuple(weights)
    specs += [whole(w.shape) for w in weights]
    outs, out_specs = [], []
    if first:
        last = seq // PAIR - 1
        args += (buckets, buckets)
        specs += [
            pl.BlockSpec((seq, PAIR), lambda p: (0, 0)),
            pl.BlockSpec((seq, PAIR), lambda p: (0, last)),
        ]
        outs = [shape_of((pairs * 3 * PAIR, width), BF16), shape_of((2 * pairs, 2 * seq), F32)]
        out_specs = [whole(o.shape) for o in outs]
    outs += [
        shape_of((seq, width), BF16),
        shape_of((seq, pairs * 3 * PAIR), BF16),
        shape_of((2 * pairs, seq, seq), BF16),
        shape_of((seq, pairs * PAIR), BF16),
    ]
    out_specs += [
        whole((seq, width)),
        pl.BlockSpec((seq, 3 * PAIR), lambda p: (0, p)),
        pl.BlockSpec((2, seq, seq), lambda p: (p, 0, 0)),
        pl.BlockSpec((seq, PAIR), lambda p: (0, p)),
    ]
    return call(
        functools.partial(attn_fwd_kernel, first, doc, docs, seq),
        "attn_fwd",
        ids,
        args,
        specs,
        outs,
        out_specs,
        grid=(pairs,),
    )


def ffn_kernel(
    src_ref, att_own_ref, att_oth_ref, wo_a_ref, wo_b_ref, wo_x_ref, wo_xc_ref, gains_ref, cot_ref,
    in_a_ref, in_b_ref, back_a_ref, back_b_ref,
    middle_ref, normed_ref, gsend_ref, hsend_ref, hid_ref, gpre_ref, acc_ref, gacc_ref,
):
    rows, width = src_ref.shape
    cols = width // 4
    step = pl.program_id(0)

    @pl.when(step == 0)
    def _():
        swapped = lax.axis_index("x") != 0
        wo_own = jnp.concatenate([wo_a_ref[...], wo_b_ref[...]], axis=0)
        wo_oth = jnp.concatenate([wo_x_ref[...], wo_xc_ref[...]], axis=0)
        wo_0 = jnp.where(swapped, wo_oth, wo_own)
        wo_1 = jnp.where(swapped, wo_own, wo_oth)
        for start in range(0, rows, CHUNK):
            at = slice(start, start + CHUNK)
            own, oth = att_own_ref[at, :], att_oth_ref[at, :]
            terms = dot_nn(jnp.where(swapped, oth, own), wo_0) + dot_nn(jnp.where(swapped, own, oth), wo_1)
            m = src_ref[at, :].astype(F32) + terms
            middle_ref[at, :] = m
            normed_ref[at, :] = (m * rms_rows(m) * gains_ref[1:, :]).astype(BF16)

    w_in = jnp.where(step == 0, in_a_ref[...], in_b_ref[...])
    w_back = jnp.where(step == 0, back_a_ref[...], back_b_ref[...])
    for start in range(0, rows, CHUNK):
        at = slice(start, start + CHUNK)
        pre = dot_nn(normed_ref[at, :], w_in)
        ghid = dot_nt(cot_ref[at, :], w_back)
        sq = pre * pre
        t = jnp.tanh(GELU_C * (pre + GELU_A * sq * pre))
        half_t = 0.5 * (1.0 + t)
        hidden = (pre * half_t).astype(BF16)
        slope = half_t + 0.5 * pre * (1.0 - t * t) * (GELU_C * (1.0 + 3.0 * GELU_A * sq))
        gpre = (ghid * slope).astype(BF16)
        out = dot_nn(hidden, w_back)
        gnorm = dot_nt(gpre, w_in)
        hid_ref[at, :] = hidden
        gpre_ref[at, :] = gpre

        @pl.when(step == 0)
        def _():
            acc_ref[at, :] = out
            gacc_ref[at, :] = gnorm

        @pl.when(step != 0)
        def _():
            hsend_ref[at, :] = (acc_ref[at, :] + out).astype(BF16)
            gsend_ref[at, :] = (gacc_ref[at, :] + gnorm).astype(BF16)


def ffn(ids, inputs, att_own, att_oth, wos, gains, cotangent, w_ins, w_backs, doc, docs):
    seq = att_own.shape[0]
    width = inputs.shape[1]
    units = w_ins[0].shape[1]
    mine = doc_rows(seq, width, docs, doc)
    outs = [
        shape_of((seq, width), F32),
        shape_of((seq, width), BF16),
        shape_of((seq, width), BF16),
        shape_of((seq, width), BF16),
        shape_of((seq, 2 * units), BF16),
        shape_of((seq, 2 * units), BF16),
    ]
    return call(
        ffn_kernel,
        "ffn",
        ids,
        (inputs, att_own, att_oth) + wos + (gains, cotangent) + w_ins + w_backs,
        [mine, whole(att_own.shape), whole(att_oth.shape)]
        + [whole(w.shape) for w in wos]
        + [whole(gains.shape), mine]
        + [whole(w.shape) for w in w_ins + w_backs],
        outs,
        [whole(o.shape) for o in outs[:4]] + [pl.BlockSpec((seq, units), lambda i: (0, i))] * 2,
        grid=(2,),
        scratch=[pltpu.VMEM((seq, width), F32), pltpu.VMEM((seq, width), F32)],
    )


def grad_back_kernel(docs, *refs):
    hid_refs, cot_ref, out_refs = refs[:docs], refs[docs], refs[docs + 1 :]
    hid = jnp.concatenate([r[...] for r in hid_refs], axis=0)
    units = out_refs[0].shape[0]
    for i in range(2):
        out_refs[i][...] = dot_tn(hid[:, i * units : (i + 1) * units], cot_ref[...]).astype(BF16)


def grad_back(ids, hids, cotangent, docs):
    seq, both = hids[0].shape
    width = cotangent.shape[1]
    outs = [shape_of((both // 2, width), BF16)] * 2
    return call(
        functools.partial(grad_back_kernel, docs),
        "grad_back",
        ids,
        tuple(hids) + (cotangent,),
        [whole(h.shape) for h in hids] + [pl.BlockSpec((docs * seq, width), lambda i: (lax.axis_index("core"), 0))],
        outs,
        [whole(o.shape) for o in outs],
    )


def grad_in_kernel(docs, *refs):
    normed_refs, gpre_refs, out_refs = refs[:docs], refs[docs : 2 * docs], refs[2 * docs :]
    normed = jnp.concatenate([r[...] for r in normed_refs], axis=0)
    gpre = jnp.concatenate([r[...] for r in gpre_refs], axis=0)
    units = out_refs[0].shape[1]
    for i in range(2):
        out_refs[i][...] = dot_tn(normed, gpre[:, i * units : (i + 1) * units]).astype(BF16)


def grad_in(ids, normeds, gpres, docs):
    width = normeds[0].shape[1]
    units = gpres[0].shape[1] // 2
    outs = [shape_of((width, units), BF16)] * 2
    args = tuple(normeds) + tuple(gpres)
    return call(
        functools.partial(grad_in_kernel, docs),
        "grad_in",
        ids,
        args,
        [whole(a.shape) for a in args],
        outs,
        [whole(o.shape) for o in outs],
    )


def fold_diagonals(g, seq):
    g = jnp.concatenate([g, jnp.zeros_like(g)], axis=1)
    n = seq
    while n > 8:
        n //= 2
        g = g[:n] + pltpu.roll(g[n:], 2 * seq - n, 1)
    while n > 1:
        n //= 2
        g = g[:n] + jnp.concatenate([g[n:, n:], g[n:, :n]], axis=1)
    return g


def attn_bwd_kernel(
    seq, middle_ref, gown_ref, goth_ref, gains_ref, cot_ref, wo_a_ref, wo_b_ref, w_ref, packed_ref, probs_ref,
    gmid_ref, low_ref, ggain_ref, gp_ref, nsend_ref, diag_ref, dout_ref, acc_ref,
):
    step = pl.program_id(0)
    pairs = pl.num_programs(0)

    @pl.when(step == 0)
    def _():
        wo_own = jnp.concatenate([wo_a_ref[...], wo_b_ref[...]], axis=0)
        ggain = jnp.zeros(ggain_ref.shape, F32)
        for start in range(0, seq, CHUNK):
            at = slice(start, start + CHUNK)
            m = middle_ref[at, :]
            gnorm = gown_ref[at, :].astype(F32) + goth_ref[at, :].astype(F32)
            r = rms_rows(m)
            ggain = ggain + jnp.sum(gnorm * m * r, axis=0, keepdims=True)
            back = gains_ref[1:, :] * gnorm
            inner = jnp.mean(back * m, axis=-1, keepdims=True)
            gm = cot_ref[at, :].astype(F32) + r * back - m * (r * r * r * inner)
            gmid_ref[at, :] = gm
            low = gm.astype(BF16)
            low_ref[at, :] = low
            dout = dot_nt(low, wo_own).astype(BF16)
            for p in range(dout_ref.shape[0]):
                dout_ref[p, at, :] = dout[:, p * PAIR : (p + 1) * PAIR]
        ggain_ref[...] = ggain

    lane = lax.broadcasted_iota(jnp.int32, (seq, PAIR), 1)
    scale = 1.0 / math.sqrt(HD)
    q = packed_ref[:, :PAIR]
    k = packed_ref[:, PAIR : 2 * PAIR]
    v = packed_ref[:, 2 * PAIR :]
    do = dout_ref[step]
    kt = k.T
    dqs, dks, dvs = [], [], []
    for head in range(2):
        mine = (lane >= HD) if head else (lane < HD)
        vm = jnp.where(mine, v, jnp.zeros_like(v))
        dp = dot_nt(vm, do)
        p_low = probs_ref[head]
        p = p_low.astype(F32)
        mean = jnp.sum(dp * p, axis=0, keepdims=True)
        ds = (p * (dp - mean)).astype(BF16)
        diag_ref[0, head : head + 1, :] = fold_diagonals(ds.astype(F32), seq)
        dvs.append(dot_nn(p_low, do))
        dks.append(dot_nn(ds, q))
        dqs.append(dot_nn(kt[head * HD : (head + 1) * HD, :], ds))
    dq = jnp.concatenate(dqs, axis=0).T * scale
    first = lane < HD
    gp_ref[:, :PAIR] = dq.astype(BF16)
    gp_ref[:, PAIR : 2 * PAIR] = jnp.where(first, dks[0], dks[1]).astype(BF16)
    gp_ref[:, 2 * PAIR :] = jnp.where(first, dvs[0], dvs[1]).astype(BF16)
    terms = dot_nn(gp_ref[...], w_ref[...])

    @pl.when(step == 0)
    def _():
        acc_ref[...] = terms

    @pl.when(step != 0)
    def _():
        acc_ref[...] += terms

    @pl.when(step == pairs - 1)
    def _():
        nsend_ref[...] = acc_ref[...].astype(BF16)


def attn_bwd(ids, middle, gown, goth, gains, cotangent, wo_a, wo_b, w_own, packed, probs, doc, docs):
    seq, width = middle.shape
    pairs = packed.shape[1] // (3 * PAIR)
    mine = doc_rows(seq, width, docs, doc)
    outs = [
        shape_of((seq, width), F32),
        shape_of((seq, width), BF16),
        shape_of((1, width), F32),
        shape_of(packed.shape, BF16),
        shape_of((seq, width), BF16),
        shape_of((pairs, 2, 2 * seq), F32),
    ]
    return call(
        functools.partial(attn_bwd_kernel, seq),
        "attn_bwd",
        ids,
        (middle, gown, goth, gains, cotangent, wo_a, wo_b, w_own, packed, probs),
        [whole(middle.shape), whole(gown.shape), whole(goth.shape), whole(gains.shape), mine]
        + [whole(wo_a.shape), whole(wo_b.shape)]
        + [
            pl.BlockSpec((3 * PAIR, width), lambda p: (p, 0)),
            pl.BlockSpec((seq, 3 * PAIR), lambda p: (0, p)),
            pl.BlockSpec((2, seq, seq), lambda p: (p, 0, 0)),
        ],
        outs,
        [
            whole((seq, width)),
            whole((seq, width)),
            whole((1, width)),
            pl.BlockSpec((seq, 3 * PAIR), lambda p: (0, p)),
            whole((seq, width)),
            pl.BlockSpec((1, 2, 2 * seq), lambda p: (p, 0, 0)),
        ],
        grid=(pairs,),
        scratch=[pltpu.VMEM((pairs, seq, PAIR), BF16), pltpu.VMEM((seq, width), F32)],
    )


def grad_attn_kernel(docs, pairs, *refs):
    groups = [refs[i * docs : (i + 1) * docs] for i in range(4)]
    (out_ref,) = refs[4 * docs :]
    normed, gp, low, att = (jnp.concatenate([r[...] for r in g], axis=0) for g in groups)
    step = pl.program_id(0)
    width = out_ref.shape[0] // 2
    cols = width // 4
    heads = cols // HD
    core = lax.axis_index("core")
    grads = dot_tn(gp, normed).astype(BF16)
    outer = dot_tn(att, low).astype(BF16)
    for p in range(pairs):

        @pl.when(step == p)
        def _(p=p):
            for i in range(2):
                head = 2 * p + i
                base = (core if head < heads else 1 - core) * width + (head % heads) * HD
                for part in range(3):
                    piece = grads[part * PAIR + i * HD : part * PAIR + (i + 1) * HD, :]
                    out_ref[pl.ds(pl.multiple_of(base + part * cols, HD), HD), :] = piece
                piece = outer[i * HD : (i + 1) * HD, :]
                out_ref[pl.ds(pl.multiple_of(base + 3 * cols, HD), HD), :] = piece


def grad_attn(ids, normeds, gps, lows, atts, docs):
    seq, width = normeds[0].shape
    pairs = atts[0].shape[1] // PAIR
    outs = [shape_of((2 * width, width), BF16)]
    return call(
        functools.partial(grad_attn_kernel, docs, pairs),
        "grad_attn",
        ids,
        tuple(normeds) + tuple(gps) + tuple(lows) + tuple(atts),
        [whole((seq, width))] * docs
        + [pl.BlockSpec((seq, 3 * PAIR), lambda p: (0, p))] * docs
        + [whole((seq, width))] * docs
        + [pl.BlockSpec((seq, PAIR), lambda p: (0, p))] * docs,
        outs,
        [whole((2 * width, width))],
        grid=(pairs,),
    )


def grad_input_kernel(docs, src_ref, gains_ref, *refs):
    gmid_refs, own_refs, oth_refs = (refs[i * docs : (i + 1) * docs] for i in range(3))
    full_ref, send_ref, ggain_ref = refs[3 * docs :]
    seq = gmid_refs[0].shape[0]
    ggain = jnp.zeros(ggain_ref.shape, F32)
    for doc in range(docs):
        for start in range(0, seq, CHUNK):
            here = slice(start, start + CHUNK)
            at = slice(doc * seq + start, doc * seq + start + CHUNK)
            gnorm = own_refs[doc][here, :].astype(F32) + oth_refs[doc][here, :].astype(F32)
            v = src_ref[at, :].astype(F32)
            r = rms_rows(v)
            ggain = ggain + jnp.sum(gnorm * v * r, axis=0, keepdims=True)
            back = gains_ref[:1, :] * gnorm
            inner = jnp.mean(back * v, axis=-1, keepdims=True)
            out = gmid_refs[doc][here, :] + r * back - v * (r * r * r * inner)
            full_ref[at, :] = out
            send_ref[at, :] = out
    ggain_ref[...] = ggain


def grad_input(ids, inputs, gains, gmids, owns, oths, docs):
    seq, width = gmids[0].shape
    rows = docs * seq
    mine = pl.BlockSpec((rows, width), lambda i: (lax.axis_index("core"), 0))
    return call(
        functools.partial(grad_input_kernel, docs),
        "grad_input",
        ids,
        (inputs, gains) + tuple(gmids) + tuple(owns) + tuple(oths),
        [mine, whole(gains.shape)] + [whole((seq, width))] * (3 * docs),
        [shape_of((2 * rows, width), F32), shape_of((rows, width), F32), shape_of((1, width), F32)],
        [mine, whole((rows, width)), whole((1, width))],
    )


def mix_kernel(docs, *refs):
    middle_refs, own_refs, oth_refs = (refs[i * docs : (i + 1) * docs] for i in range(3))
    full_ref, send_ref = refs[3 * docs :]
    seq = middle_refs[0].shape[0]
    for doc in range(docs):
        at = slice(doc * seq, (doc + 1) * seq)
        terms = own_refs[doc][...].astype(F32) + oth_refs[doc][...].astype(F32)
        out = (middle_refs[doc][...] + terms).astype(BF16)
        full_ref[at, :] = out
        send_ref[at, :] = out


def mix(ids, middles, owns, oths, docs):
    seq, width = middles[0].shape
    rows = docs * seq
    return call(
        functools.partial(mix_kernel, docs),
        "mix",
        ids,
        tuple(middles) + tuple(owns) + tuple(oths),
        [whole((seq, width))] * (3 * docs),
        [shape_of((2 * rows, width), BF16), shape_of((rows, width), BF16)],
        [pl.BlockSpec((rows, width), lambda i: (lax.axis_index("core"), 0)), whole((rows, width))],
    )


def place_kernel(full_ref, got_ref, out_ref):
    out_ref[...] = got_ref[...]


def place(ids, full, got):
    rows, width = got.shape
    steps = 4
    part = rows // steps
    return call(
        place_kernel,
        "place",
        ids,
        (full, got),
        [pl.BlockSpec(memory_space=pl.ANY), pl.BlockSpec((part, width), lambda i: (i, 0))],
        [shape_of(full.shape, full.dtype)],
        [pl.BlockSpec((part, width), lambda i: ((1 - lax.axis_index("core")) * steps + i, 0))],
        grid=(steps,),
        aliases={1: 1},
    )


def gate(ids, *arrays):
    anywhere = [pl.BlockSpec(memory_space=pl.ANY)] * len(arrays)
    shapes = [shape_of(v.shape, v.dtype) for v in arrays]
    aliases = {i + 1: i + 1 for i in range(len(arrays))}
    return call(lambda *refs: None, "gate", ids, arrays, anywhere, shapes, anywhere, aliases=aliases)


def need(ids, *arrays):
    anywhere = pl.BlockSpec(memory_space=pl.ANY)
    return call(lambda *refs: None, "need", ids, arrays, [anywhere] * len(arrays), [], [])[1]


def sum_core_kernel(a_ref, b_ref, c_ref, d_ref, ab_ref, cd_ref):
    ab_ref[...] = (a_ref[...].astype(F32) + b_ref[...].astype(F32)).astype(BF16)
    cd_ref[...] = (c_ref[...].astype(F32) + d_ref[...].astype(F32)).astype(BF16)


def sum_core(ids, a, b, c, d):
    steps = 4
    specs = [pl.BlockSpec((v.shape[0] // steps, v.shape[1]), lambda i: (i, 0)) for v in (a, b, c, d)]
    return call(
        sum_core_kernel,
        "sum_core",
        ids,
        (a, b, c, d),
        specs,
        [shape_of(a.shape, BF16), shape_of(c.shape, BF16)],
        [specs[0], specs[2]],
        grid=(steps,),
    )


def widen_kernel(*refs):
    half = len(refs) // 2
    for src, dst in zip(refs[:half], refs[half:]):
        dst[...] = src[...].astype(F32)


def widen(ids, *arrays):
    steps = 4
    specs = [pl.BlockSpec((v.shape[0] // steps, v.shape[1]), lambda i: (i, 0)) for v in arrays]
    return call(
        widen_kernel, "widen", ids, arrays, specs, [shape_of(v.shape, F32) for v in arrays], specs, grid=(steps,)
    )


def sum_kernel(got_ref, out_ref):
    rows = out_ref.shape[0]
    parts = got_ref.shape[0] // rows
    total = got_ref[:rows, :].astype(F32)
    for i in range(1, parts):
        total = total + got_ref[i * rows : (i + 1) * rows, :].astype(F32)
    out_ref[...] = total.astype(BF16)


def sum_parts(token, got, dp):
    width = got.shape[1]
    rows = got.shape[0] // (2 * dp)
    if rows % 16:
        total = jnp.sum(got.reshape(2 * dp, rows, width).astype(F32), axis=0).astype(BF16)
        return [jnp.tile(total, (dp, 1))], token
    return call(
        sum_kernel,
        "sum_parts",
        token,
        (got,),
        [whole(got.shape)],
        [shape_of((dp * rows, width), BF16)],
        [pl.BlockSpec((rows, width), lambda i: (i, 0))],
        grid=(dp,),
    )


def region(always, fn, ids):
    outs = jax.eval_shape(fn, ids)
    return lax.cond(always, fn, lambda _: jax.tree.map(lambda o: jnp.zeros(o.shape, o.dtype), outs), ids)


def per_device(dp, inputs, gain_attn, w_qkv, w_out, gain_ffn, w_in, w_back, bias_table, lengths, buckets, cotangent):
    width = inputs.shape[1]
    seq = buckets.shape[0]
    docs = lengths.shape[0] // 2
    table_rows, heads = bias_table.shape
    gains = jnp.stack([gain_attn, gain_ffn]).astype(F32)
    ids = jnp.zeros((8, 128), F32)

    def from_core(v):
        return lax.ppermute(v, "core", [(0, 1), (1, 0)])

    def from_x(v):
        return lax.ppermute(v, "x", [(0, 1), (1, 0)])

    def scatter(v):
        return lax.all_to_all(v, ("core", "dp"), 0, 0, tiled=True)

    def spread(v):
        return lax.all_to_all(v, "dp", 0, 0, tiled=True)

    bias = jnp.pad(bias_table.T, ((0, BIAS_ROWS - heads), (0, width - table_rows)))
    attn_w = jnp.concatenate([w_qkv.transpose(0, 2, 1).reshape(-1, width), bias], axis=0)
    attn_w = jnp.concatenate([attn_w[: 3 * width // 4], w_out, attn_w[3 * width // 4 :]], axis=0)
    attn_c = from_core(attn_w)
    wo_x = from_x(w_out)
    wo_c = from_core(w_out)
    in_c = from_core(w_in)
    back_c = from_core(w_back)

    every = range(docs)
    normed, packed, probs, att, att_x = [], [], [], [], []
    for doc in every:
        if doc == 0:
            (w_own, u, n, a, b, c), ids = attn_fwd(
                ids, lengths, inputs, gains, (attn_w, attn_c), buckets, doc, docs
            )
            (wo_x,), ids = gate(ids, wo_x)
            wo_xc = from_core(wo_x)
        else:
            (n, a, b, c), ids = attn_fwd(ids, lengths, inputs, gains, (w_own, u), buckets, doc, docs)
        normed.append(n)
        packed.append(a)
        probs.append(b)
        att.append(c)
        att_x.append(from_x(c))

    middle, normed2, gown, hown, hid, gpre, goth, hoth = [], [], [], [], [], [], [], []
    for doc in every:
        res, ids = ffn(
            ids, inputs, att[doc], att_x[doc], (w_out, wo_c, wo_x, wo_xc), gains, cotangent,
            (w_in, in_c), (w_back, back_c), doc, docs,
        )
        for group, r in zip((middle, normed2, gown, hown, hid, gpre), res):
            group.append(r)
        if doc + 1 < docs:
            ids = need(ids, att_x[doc + 1])
        (send,), ids = gate(ids, res[2])
        goth.append(from_x(send))
    always = lengths[0] > 0

    def ffn_grads(ids):
        (gback, gback_c), ids = grad_back(ids, hid, cotangent, docs)
        gback_c = from_core(gback_c)
        (gin, gin_c), ids = grad_in(ids, normed2, gpre, docs)
        (gback, gin), ids = sum_core(ids, gback, gback_c, gin, from_core(gin_c))
        return ids, gback, gin

    ids, gback, gin = region(always, ffn_grads, ids)
    ids = need(ids, *goth)
    (gback, gin), ids = gate(ids, gback, gin)
    gback, gin = lax.psum((gback, gin), "dp")

    def back_of(doc, ids):
        res, ids = attn_bwd(
            ids, middle[doc], gown[doc], goth[doc], gains, cotangent, w_out, wo_c, w_own, packed[doc], probs[doc],
            doc, docs,
        )
        return ids, res

    def attention_back(ids):
        ids, first = back_of(0, ids)
        noth = [from_x(first[4])]

        def others(ids):
            results = [first]
            for doc in range(1, docs):
                ids, res = back_of(doc, ids)
                results.append(res)
            gp, low = [r[3] for r in results], [r[1] for r in results]
            (gattn,), ids = grad_attn(ids, normed, gp, low, att, docs)
            return ids, results[1:], gattn

        ids, results, gattn = region(always, others, ids)
        gmid, low, ggain_two, gp, nown, diag = zip(first, *results)
        ids = need(ids, noth[0])
        for doc in range(1, docs):
            (send,), ids = gate(ids, nown[doc])
            noth.append(from_x(send))
        (gattn,), ids = gate(ids, gattn)
        gattn = scatter(gattn)
        hoth = []
        for doc in every:
            (send,), ids = gate(ids, hown[doc])
            hoth.append(from_x(send))
        (gsrc, gsrc_send, ggain_one), ids = grad_input(ids, inputs, gains, gmid, nown, noth, docs)
        gsrc_got = from_core(gsrc_send)

        diag_bucket = jnp.concatenate([buckets[:, 0], buckets[:1, -1], buckets[:-1, -1]])
        one_hot = (diag_bucket[:, None] == jnp.arange(table_rows)[None, :]).astype(F32)
        diag = sum(diag).reshape(2 * heads, 2 * seq)
        table = lax.dot_general(
            diag, one_hot, (((1,), (0,)), ((), ())), precision=lax.Precision.HIGHEST, preferred_element_type=F32
        )
        ggain_two = sum(ggain_two)
        small = jnp.concatenate([ggain_one.reshape(-1), ggain_two.reshape(-1), table[:heads].reshape(-1)])
        small_send = jnp.concatenate([ggain_one.reshape(-1), ggain_two.reshape(-1), table[heads:].reshape(-1)])
        small = small + from_core(small_send)
        for s in range(dp.bit_length() - 1):
            small = small + lax.ppermute(small, "dp", [(i, i ^ (1 << s)) for i in range(dp)])
        grad_gain_attn, grad_gain_ffn = small[:width], small[width : 2 * width]
        grad_table = small[2 * width :].reshape(heads, table_rows).T
        (gattn,), ids = sum_parts(ids, gattn, dp)
        gattn = spread(gattn)
        (gsrc,), ids = place(ids, gsrc, gsrc_got)
        (mixed, mixed_send), ids = mix(ids, middle, hown, hoth, docs)
        ids = need(ids, grad_gain_attn, grad_gain_ffn, grad_table)
        (mixed,), ids = place(ids, mixed, from_core(mixed_send))
        part = 3 * width // 4
        gattn = gattn.astype(F32)
        grad_w_qkv = gattn[:part].reshape(3, width // 4, width).transpose(0, 2, 1)
        grad_w_out = gattn[part:]
        return ids, mixed, gsrc, grad_gain_attn, grad_w_qkv, grad_w_out, grad_gain_ffn, grad_table

    ids, mixed, gsrc, grad_gain_attn, grad_w_qkv, grad_w_out, grad_gain_ffn, grad_table = region(
        always, attention_back, ids
    )
    (grad_w_back, grad_w_in), ids = widen(ids, gback, gin)
    return (
        mixed,
        gsrc,
        grad_gain_attn,
        grad_w_qkv,
        grad_w_out,
        grad_gain_ffn,
        grad_w_in,
        grad_w_back,
        grad_table,
    )


def solution(mesh):
    dp = mesh.shape["dp"]
    devices = mesh.devices.reshape(mesh.shape["tensor"] // 2, 2, dp)
    mesh = jax.sharding.Mesh(devices, ("x", "core", "dp"))
    return jax.shard_map(
        functools.partial(per_device, dp),
        mesh=mesh,
        in_specs=(
            P("dp", None),
            P(),
            P(None, None, ("x", "core")),
            P(("x", "core"), None),
            P(),
            P(None, ("x", "core")),
            P(("x", "core"), None),
            P(None, ("x", "core")),
            P("dp"),
            P(),
            P("dp", None),
        ),
        out_specs=(
            P("dp", None),
            P("dp", None),
            P(),
            P(None, None, ("x", "core")),
            P(("x", "core"), None),
            P(),
            P(None, ("x", "core")),
            P(("x", "core"), None),
            P(None, ("x", "core")),
        ),
        check_vma=False,
    )
```

```python
import functools
import math

import jax
import jax.numpy as jnp
from jax import lax
from jax.experimental import pallas as pl
from jax.experimental.pallas import tpu as pltpu
from jax.sharding import PartitionSpec as P

HD = 64
PAIR = 2 * HD
EPS = 1e-06
MASKED = -1000000000.0
GELU_C = 0.7978845608028654
GELU_A = 0.044715
CHUNK = 256
VMEM_BYTES = 18 * 1024 * 1024

F32 = jnp.float32
BF16 = jnp.bfloat16


def dot_nn(a, b):
    return lax.dot_general(a, b, (((1,), (0,)), ((), ())), preferred_element_type=F32)


def dot_nt(a, b):
    return lax.dot_general(a, b, (((1,), (1,)), ((), ())), preferred_element_type=F32)


def dot_tn(a, b):
    return lax.dot_general(a, b, (((0,), (0,)), ((), ())), preferred_element_type=F32)


def whole(shape):
    return pl.BlockSpec(shape, lambda *_: (0,) * len(shape))


def shape_of(shape, dtype):
    return jax.ShapeDtypeStruct(shape, dtype)


def call(kernel, name, token, args, in_specs, outs, out_specs, grid=(1,), scratch=(), aliases=None):
    n_in, n_out = len(args), len(outs)

    def body(token_ref, *refs):
        del token_ref
        kernel(*refs[:n_in], *refs[n_in + 1 :])

    anywhere = pl.BlockSpec(memory_space=pl.ANY)
    res = pl.pallas_call(
        body,
        grid=grid,
        in_specs=[anywhere] + list(in_specs),
        out_specs=[anywhere] + list(out_specs),
        scratch_shapes=list(scratch),
        out_shape=[shape_of(token.shape, token.dtype)] + list(outs),
        input_output_aliases={0: 0, **(aliases or {})},
        compiler_params=pltpu.CompilerParams(vmem_limit_bytes=VMEM_BYTES),
        name=name,
    )(token, *args)
    return res[1:], res[0]


def rms_rows(v):
    return lax.rsqrt(jnp.mean(v * v, axis=-1, keepdims=True) + EPS)


def doc_rows(seq, width, docs, doc):
    return pl.BlockSpec((seq, width), lambda i: (lax.axis_index("core") * docs + doc, 0))


BIAS_ROWS = 16


def assemble(first_ref, second_ref, w_ref, width):
    cols = width // 4
    heads = cols // HD
    sources = [(first_ref, h) for h in range(heads)] + [(second_ref, h) for h in range(heads)]
    for p in range(heads):
        for part in range(3):
            for i in range(2):
                ref, head = sources[2 * p + i]
                src = part * cols + head * HD
                dst = (3 * p + part) * PAIR + i * HD
                w_ref[dst : dst + HD, :] = ref[src : src + HD, :]


def bias_along(first_ref, second_ref, left_ref, right_ref, u_ref, width):
    seq = left_ref.shape[0]
    left = left_ref[...].astype(F32).T[:1, :]
    right = right_ref[...].astype(F32).T[PAIR - 1 :, :]
    bucket = jnp.concatenate([left, pltpu.roll(right, 1, 1)], axis=1)
    index = lax.broadcasted_iota(jnp.int32, (PAIR, 2 * seq), 0).astype(F32)
    one_hot = (index == bucket).astype(BF16)
    heads = width // 4 // HD
    for at, ref in ((0, first_ref), (heads, second_ref)):
        u = dot_nn(ref[width:, :PAIR], one_hot)
        u_ref[at : at + heads, :] = u[:heads]


def attn_fwd_kernel(
    first, doc, docs, seq, len_ref, src_ref, gains_ref, *refs
):
    step = pl.program_id(0)
    if first:
        first_ref, second_ref, left_ref, right_ref, w_ref, u_ref, *refs = refs
    else:
        w_ref, u_ref, *refs = refs
    normed_ref, packed_ref, probs_ref, att_ref = refs

    @pl.when(step == 0)
    def _():
        if first:
            assemble(first_ref, second_ref, w_ref, src_ref.shape[1])
            bias_along(first_ref, second_ref, left_ref, right_ref, u_ref, src_ref.shape[1])
        for start in range(0, src_ref.shape[0], CHUNK):
            at = slice(start, start + CHUNK)
            v = src_ref[at, :].astype(F32)
            normed_ref[at, :] = (v * rms_rows(v) * gains_ref[:1, :]).astype(BF16)

    at = pl.multiple_of(step * 3 * PAIR, 3 * PAIR)
    packed = dot_nt(normed_ref[...], w_ref[pl.ds(at, 3 * PAIR), :])
    lane = lax.broadcasted_iota(jnp.int32, (seq, PAIR), 1)
    scale = 1.0 / math.sqrt(HD)
    packed_ref[:, :PAIR] = (packed[:, :PAIR].astype(BF16).astype(F32) * scale).astype(BF16)
    packed_ref[:, PAIR:] = packed[:, PAIR:].astype(BF16)
    key_pos = lax.broadcasted_iota(jnp.int32, (seq, 1), 0)
    length = len_ref[lax.axis_index("core") * docs + doc]
    for head in range(2):
        row = jnp.broadcast_to(u_ref[pl.ds(2 * step + head, 1), :], (seq, 2 * seq))
        rel = pltpu.roll(row, 0, 1, stride=1, stride_axis=0)[:, :seq]
        mine = (lane >= HD) if head else (lane < HD)
        q = packed_ref[:, :PAIR]
        k = packed_ref[:, PAIR : 2 * PAIR]
        v = packed_ref[:, 2 * PAIR :]
        k = jnp.where(mine, k, jnp.zeros_like(k))
        scores = dot_nt(k, q) + rel
        scores = jnp.where(key_pos < length, scores, MASKED)
        top = jnp.max(scores, axis=0, keepdims=True)
        e = jnp.exp(scores - top)
        total = jnp.sum(e, axis=0, keepdims=True)
        p = (e * (1.0 / total)).astype(BF16)
        probs_ref[head] = p
        vt = v.T[head * HD : (head + 1) * HD, :]
        o = dot_nn(vt, p)
        att_ref[:, head * HD : (head + 1) * HD] = o.T.astype(BF16)


def attn_fwd(ids, lengths, inputs, gains, weights, buckets, doc, docs):
    seq = buckets.shape[0]
    width = inputs.shape[1]
    pairs = width // (4 * HD)
    first = doc == 0
    specs = [pl.BlockSpec(memory_space=pltpu.SMEM), doc_rows(seq, width, docs, doc), whole(gains.shape)]
    args = (lengths, inputs, gains) + tuple(weights)
    specs += [whole(w.shape) for w in weights]
    outs, out_specs = [], []
    if first:
        last = seq // PAIR - 1
        args += (buckets, buckets)
        specs += [
            pl.BlockSpec((seq, PAIR), lambda p: (0, 0)),
            pl.BlockSpec((seq, PAIR), lambda p: (0, last)),
        ]
        outs = [shape_of((pairs * 3 * PAIR, width), BF16), shape_of((2 * pairs, 2 * seq), F32)]
        out_specs = [whole(o.shape) for o in outs]
    outs += [
        shape_of((seq, width), BF16),
        shape_of((seq, pairs * 3 * PAIR), BF16),
        shape_of((2 * pairs, seq, seq), BF16),
        shape_of((seq, pairs * PAIR), BF16),
    ]
    out_specs += [
        whole((seq, width)),
        pl.BlockSpec((seq, 3 * PAIR), lambda p: (0, p)),
        pl.BlockSpec((2, seq, seq), lambda p: (p, 0, 0)),
        pl.BlockSpec((seq, PAIR), lambda p: (0, p)),
    ]
    return call(
        functools.partial(attn_fwd_kernel, first, doc, docs, seq),
        "attn_fwd",
        ids,
        args,
        specs,
        outs,
        out_specs,
        grid=(pairs,),
    )


TILE = 256


def ffn_kernel(first, *refs):
    (
        src_ref, att_own_ref, att_oth_ref, wo_a_ref, wo_b_ref, wo_x_ref, wo_xc_ref, gains_ref, cot_ref,
        in_a_ref, in_b_ref, back_a_ref, back_b_ref, *refs,
    ) = refs
    if not first:
        gback_a_in, gback_b_in, gin_a_in, gin_b_in, *refs = refs
    (
        middle_ref, gsend_ref, hsend_ref, gback_a_ref, gback_b_ref, gin_a_ref, gin_b_ref,
        normed_ref, normed_t_ref, acc_ref, gacc_ref,
    ) = refs
    rows = src_ref.shape[0]
    step = pl.program_id(0)
    half = pl.num_programs(0) // 2

    @pl.when(step == 0)
    def _():
        swapped = lax.axis_index("x") != 0
        wo_own = jnp.concatenate([wo_a_ref[...], wo_b_ref[...]], axis=0)
        wo_oth = jnp.concatenate([wo_x_ref[...], wo_xc_ref[...]], axis=0)
        wo_0 = jnp.where(swapped, wo_oth, wo_own)
        wo_1 = jnp.where(swapped, wo_own, wo_oth)
        for start in range(0, rows, CHUNK):
            at = slice(start, start + CHUNK)
            own, oth = att_own_ref[at, :], att_oth_ref[at, :]
            terms = dot_nn(jnp.where(swapped, oth, own), wo_0) + dot_nn(jnp.where(swapped, own, oth), wo_1)
            m = src_ref[at, :].astype(F32) + terms
            middle_ref[at, :] = m
            normed = (m * rms_rows(m) * gains_ref[1:, :]).astype(BF16)
            normed_ref[at, :] = normed
            normed_t_ref[:, at] = normed.T
        acc_ref[...] = jnp.zeros(acc_ref.shape, F32)
        gacc_ref[...] = jnp.zeros(gacc_ref.shape, F32)

    mine = step < half
    w_in = jnp.where(mine, in_a_ref[...], in_b_ref[...])
    w_back = jnp.where(mine, back_a_ref[...], back_b_ref[...])
    hiddens, gpres = [], []
    for start in range(0, rows, 2 * CHUNK):
        at = slice(start, start + 2 * CHUNK)
        pre = dot_nn(normed_ref[at, :], w_in)
        ghid = dot_nt(cot_ref[at, :], w_back)
        sq = pre * pre
        t = jnp.tanh(pre * (GELU_C + (GELU_C * GELU_A) * sq))
        half_t = 0.5 + 0.5 * t
        act = pre * half_t
        hidden = act.astype(BF16)
        slope = half_t + (act * (1.0 - t)) * (GELU_C + (3.0 * GELU_C * GELU_A) * sq)
        gpre = (ghid * slope).astype(BF16)
        acc_ref[at, :] += dot_nn(hidden, w_back)
        gacc_ref[at, :] += dot_nt(gpre, w_in)
        hiddens.append(hidden)
        gpres.append(gpre)
    gback = dot_tn(jnp.concatenate(hiddens, axis=0), cot_ref[...])
    gin = dot_nn(normed_t_ref[...], jnp.concatenate(gpres, axis=0))

    @pl.when(mine)
    def _():
        if first:
            gback_a_ref[...] = gback.astype(BF16)
            gin_a_ref[...] = gin.astype(BF16)
        else:
            gback_a_ref[...] = (gback + gback_a_in[...].astype(F32)).astype(BF16)
            gin_a_ref[...] = (gin + gin_a_in[...].astype(F32)).astype(BF16)

    @pl.when(jnp.logical_not(mine))
    def _():
        if first:
            gback_b_ref[...] = gback.astype(BF16)
            gin_b_ref[...] = gin.astype(BF16)
        else:
            gback_b_ref[...] = (gback + gback_b_in[...].astype(F32)).astype(BF16)
            gin_b_ref[...] = (gin + gin_b_in[...].astype(F32)).astype(BF16)

    @pl.when(step == 2 * half - 1)
    def _():
        hsend_ref[...] = acc_ref[...].astype(BF16)
        gsend_ref[...] = gacc_ref[...].astype(BF16)


def ffn(ids, inputs, att_own, att_oth, wos, gains, cotangent, w_ins, w_backs, grads, doc, docs):
    seq = att_own.shape[0]
    width = inputs.shape[1]
    units = w_ins[0].shape[1]
    tiles = units // TILE
    mine = doc_rows(seq, width, docs, doc)

    def first_half(i):
        return jnp.minimum(i, tiles - 1)

    def second_half(i):
        return jnp.maximum(i - tiles, 0)

    def back_spec(of):
        return pl.BlockSpec((TILE, width), lambda i: (of(i), 0))

    def in_spec(of):
        return pl.BlockSpec((width, TILE), lambda i: (0, of(i)))

    grad_specs = [back_spec(first_half), back_spec(second_half), in_spec(first_half), in_spec(second_half)]
    outs = [
        shape_of((seq, width), F32),
        shape_of((seq, width), BF16),
        shape_of((seq, width), BF16),
        shape_of((units, width), BF16),
        shape_of((units, width), BF16),
        shape_of((width, units), BF16),
        shape_of((width, units), BF16),
    ]
    return call(
        functools.partial(ffn_kernel, grads is None),
        "ffn",
        ids,
        (inputs, att_own, att_oth) + wos + (gains, cotangent) + w_ins + w_backs + tuple(grads or ()),
        [mine, whole(att_own.shape), whole(att_oth.shape)]
        + [whole(w.shape) for w in wos]
        + [whole(gains.shape), mine]
        + [in_spec(first_half), in_spec(second_half), back_spec(first_half), back_spec(second_half)]
        + (grad_specs if grads else []),
        outs,
        [whole(o.shape) for o in outs[:3]] + grad_specs,
        grid=(2 * tiles,),
        scratch=[
            pltpu.VMEM((seq, width), BF16),
            pltpu.VMEM((width, seq), BF16),
            pltpu.VMEM((seq, width), F32),
            pltpu.VMEM((seq, width), F32),
        ],
    )


def fold_diagonals(g, seq):
    g = jnp.concatenate([g, jnp.zeros_like(g)], axis=1)
    n = seq
    while n > 8:
        n //= 2
        g = g[:n] + pltpu.roll(g[n:], 2 * seq - n, 1)
    while n > 1:
        n //= 2
        g = g[:n] + jnp.concatenate([g[n:, n:], g[n:, :n]], axis=1)
    return g


def attn_bwd_kernel(
    seq, middle_ref, gown_ref, goth_ref, gains_ref, cot_ref, wo_a_ref, wo_b_ref, w_ref, packed_ref, probs_ref,
    gmid_ref, low_ref, ggain_ref, gp_ref, nsend_ref, diag_ref, dout_ref, acc_ref,
):
    step = pl.program_id(0)
    pairs = pl.num_programs(0)

    @pl.when(step == 0)
    def _():
        wo_own = jnp.concatenate([wo_a_ref[...], wo_b_ref[...]], axis=0)
        ggain = jnp.zeros(ggain_ref.shape, F32)
        for start in range(0, seq, CHUNK):
            at = slice(start, start + CHUNK)
            m = middle_ref[at, :]
            gnorm = gown_ref[at, :].astype(F32) + goth_ref[at, :].astype(F32)
            r = rms_rows(m)
            ggain = ggain + jnp.sum(gnorm * m * r, axis=0, keepdims=True)
            back = gains_ref[1:, :] * gnorm
            inner = jnp.mean(back * m, axis=-1, keepdims=True)
            gm = cot_ref[at, :].astype(F32) + r * back - m * (r * r * r * inner)
            gmid_ref[at, :] = gm
            low = gm.astype(BF16)
            low_ref[at, :] = low
            dout = dot_nt(low, wo_own).astype(BF16)
            for p in range(dout_ref.shape[0]):
                dout_ref[p, at, :] = dout[:, p * PAIR : (p + 1) * PAIR]
        ggain_ref[...] = ggain

    lane = lax.broadcasted_iota(jnp.int32, (seq, PAIR), 1)
    scale = 1.0 / math.sqrt(HD)
    q = packed_ref[:, :PAIR]
    k = packed_ref[:, PAIR : 2 * PAIR]
    v = packed_ref[:, 2 * PAIR :]
    do = dout_ref[step]
    kt = k.T
    dqs, dks, dvs = [], [], []
    for head in range(2):
        mine = (lane >= HD) if head else (lane < HD)
        vm = jnp.where(mine, v, jnp.zeros_like(v))
        dp = dot_nt(vm, do)
        p_low = probs_ref[head]
        p = p_low.astype(F32)
        mean = jnp.sum(dp * p, axis=0, keepdims=True)
        ds = (p * (dp - mean)).astype(BF16)
        diag_ref[0, head : head + 1, :] = fold_diagonals(ds.astype(F32), seq)
        dvs.append(dot_nn(p_low, do))
        dks.append(dot_nn(ds, q))
        dqs.append(dot_nn(kt[head * HD : (head + 1) * HD, :], ds))
    dq = jnp.concatenate(dqs, axis=0).T * scale
    first = lane < HD
    gp_ref[:, :PAIR] = dq.astype(BF16)
    gp_ref[:, PAIR : 2 * PAIR] = jnp.where(first, dks[0], dks[1]).astype(BF16)
    gp_ref[:, 2 * PAIR :] = jnp.where(first, dvs[0], dvs[1]).astype(BF16)
    terms = dot_nn(gp_ref[...], w_ref[...])

    @pl.when(step == 0)
    def _():
        acc_ref[...] = terms

    @pl.when(step != 0)
    def _():
        acc_ref[...] += terms

    @pl.when(step == pairs - 1)
    def _():
        nsend_ref[...] = acc_ref[...].astype(BF16)


def attn_bwd(ids, middle, gown, goth, gains, cotangent, wo_a, wo_b, w_own, packed, probs, doc, docs):
    seq, width = middle.shape
    pairs = packed.shape[1] // (3 * PAIR)
    mine = doc_rows(seq, width, docs, doc)
    outs = [
        shape_of((seq, width), F32),
        shape_of((seq, width), BF16),
        shape_of((1, width), F32),
        shape_of(packed.shape, BF16),
        shape_of((seq, width), BF16),
        shape_of((pairs, 2, 2 * seq), F32),
    ]
    return call(
        functools.partial(attn_bwd_kernel, seq),
        "attn_bwd",
        ids,
        (middle, gown, goth, gains, cotangent, wo_a, wo_b, w_own, packed, probs),
        [whole(middle.shape), whole(gown.shape), whole(goth.shape), whole(gains.shape), mine]
        + [whole(wo_a.shape), whole(wo_b.shape)]
        + [
            pl.BlockSpec((3 * PAIR, width), lambda p: (p, 0)),
            pl.BlockSpec((seq, 3 * PAIR), lambda p: (0, p)),
            pl.BlockSpec((2, seq, seq), lambda p: (p, 0, 0)),
        ],
        outs,
        [
            whole((seq, width)),
            whole((seq, width)),
            whole((1, width)),
            pl.BlockSpec((seq, 3 * PAIR), lambda p: (0, p)),
            whole((seq, width)),
            pl.BlockSpec((1, 2, 2 * seq), lambda p: (p, 0, 0)),
        ],
        grid=(pairs,),
        scratch=[pltpu.VMEM((pairs, seq, PAIR), BF16), pltpu.VMEM((seq, width), F32)],
    )


def grad_attn_kernel(docs, pairs, *refs):
    groups = [refs[i * docs : (i + 1) * docs] for i in range(4)]
    (out_ref,) = refs[4 * docs :]
    normed, gp, low, att = (jnp.concatenate([r[...] for r in g], axis=0) for g in groups)
    step = pl.program_id(0)
    width = out_ref.shape[0] // 2
    cols = width // 4
    heads = cols // HD
    core = lax.axis_index("core")
    grads = dot_tn(gp, normed).astype(BF16)
    outer = dot_tn(att, low).astype(BF16)
    for p in range(pairs):

        @pl.when(step == p)
        def _(p=p):
            for i in range(2):
                head = 2 * p + i
                base = (core if head < heads else 1 - core) * width + (head % heads) * HD
                for part in range(3):
                    piece = grads[part * PAIR + i * HD : part * PAIR + (i + 1) * HD, :]
                    out_ref[pl.ds(pl.multiple_of(base + part * cols, HD), HD), :] = piece
                piece = outer[i * HD : (i + 1) * HD, :]
                out_ref[pl.ds(pl.multiple_of(base + 3 * cols, HD), HD), :] = piece


def grad_attn(ids, normeds, gps, lows, atts, docs):
    seq, width = normeds[0].shape
    pairs = atts[0].shape[1] // PAIR
    outs = [shape_of((2 * width, width), BF16)]
    return call(
        functools.partial(grad_attn_kernel, docs, pairs),
        "grad_attn",
        ids,
        tuple(normeds) + tuple(gps) + tuple(lows) + tuple(atts),
        [whole((seq, width))] * docs
        + [pl.BlockSpec((seq, 3 * PAIR), lambda p: (0, p))] * docs
        + [whole((seq, width))] * docs
        + [pl.BlockSpec((seq, PAIR), lambda p: (0, p))] * docs,
        outs,
        [whole((2 * width, width))],
        grid=(pairs,),
    )


def grad_input_kernel(docs, src_ref, gains_ref, *refs):
    gmid_refs, own_refs, oth_refs = (refs[i * docs : (i + 1) * docs] for i in range(3))
    full_ref, send_ref, ggain_ref = refs[3 * docs :]
    seq = gmid_refs[0].shape[0]
    ggain = jnp.zeros(ggain_ref.shape, F32)
    for doc in range(docs):
        for start in range(0, seq, CHUNK):
            here = slice(start, start + CHUNK)
            at = slice(doc * seq + start, doc * seq + start + CHUNK)
            gnorm = own_refs[doc][here, :].astype(F32) + oth_refs[doc][here, :].astype(F32)
            v = src_ref[at, :].astype(F32)
            r = rms_rows(v)
            ggain = ggain + jnp.sum(gnorm * v * r, axis=0, keepdims=True)
            back = gains_ref[:1, :] * gnorm
            inner = jnp.mean(back * v, axis=-1, keepdims=True)
            out = gmid_refs[doc][here, :] + r * back - v * (r * r * r * inner)
            full_ref[at, :] = out
            send_ref[at, :] = out
    ggain_ref[...] = ggain


def grad_input(ids, inputs, gains, gmids, owns, oths, docs):
    seq, width = gmids[0].shape
    rows = docs * seq
    mine = pl.BlockSpec((rows, width), lambda i: (lax.axis_index("core"), 0))
    return call(
        functools.partial(grad_input_kernel, docs),
        "grad_input",
        ids,
        (inputs, gains) + tuple(gmids) + tuple(owns) + tuple(oths),
        [mine, whole(gains.shape)] + [whole((seq, width))] * (3 * docs),
        [shape_of((2 * rows, width), F32), shape_of((rows, width), F32), shape_of((1, width), F32)],
        [mine, whole((rows, width)), whole((1, width))],
    )


def mix_kernel(docs, *refs):
    middle_refs, own_refs, oth_refs = (refs[i * docs : (i + 1) * docs] for i in range(3))
    full_ref, send_ref = refs[3 * docs :]
    seq = middle_refs[0].shape[0]
    for doc in range(docs):
        at = slice(doc * seq, (doc + 1) * seq)
        terms = own_refs[doc][...].astype(F32) + oth_refs[doc][...].astype(F32)
        out = (middle_refs[doc][...] + terms).astype(BF16)
        full_ref[at, :] = out
        send_ref[at, :] = out


def mix(ids, middles, owns, oths, docs):
    seq, width = middles[0].shape
    rows = docs * seq
    return call(
        functools.partial(mix_kernel, docs),
        "mix",
        ids,
        tuple(middles) + tuple(owns) + tuple(oths),
        [whole((seq, width))] * (3 * docs),
        [shape_of((2 * rows, width), BF16), shape_of((rows, width), BF16)],
        [pl.BlockSpec((rows, width), lambda i: (lax.axis_index("core"), 0)), whole((rows, width))],
    )


def place_kernel(full_ref, got_ref, out_ref):
    out_ref[...] = got_ref[...]


def place(ids, full, got):
    rows, width = got.shape
    steps = 4
    part = rows // steps
    return call(
        place_kernel,
        "place",
        ids,
        (full, got),
        [pl.BlockSpec(memory_space=pl.ANY), pl.BlockSpec((part, width), lambda i: (i, 0))],
        [shape_of(full.shape, full.dtype)],
        [pl.BlockSpec((part, width), lambda i: ((1 - lax.axis_index("core")) * steps + i, 0))],
        grid=(steps,),
        aliases={1: 1},
    )


def gate(ids, *arrays):
    anywhere = [pl.BlockSpec(memory_space=pl.ANY)] * len(arrays)
    shapes = [shape_of(v.shape, v.dtype) for v in arrays]
    aliases = {i + 1: i + 1 for i in range(len(arrays))}
    return call(lambda *refs: None, "gate", ids, arrays, anywhere, shapes, anywhere, aliases=aliases)


def need(ids, *arrays):
    anywhere = pl.BlockSpec(memory_space=pl.ANY)
    return call(lambda *refs: None, "need", ids, arrays, [anywhere] * len(arrays), [], [])[1]


def sum_core_kernel(a_ref, b_ref, c_ref, d_ref, ab_ref, cd_ref):
    ab_ref[...] = (a_ref[...].astype(F32) + b_ref[...].astype(F32)).astype(BF16)
    cd_ref[...] = (c_ref[...].astype(F32) + d_ref[...].astype(F32)).astype(BF16)


def sum_core(ids, a, b, c, d):
    steps = 4
    specs = [pl.BlockSpec((v.shape[0] // steps, v.shape[1]), lambda i: (i, 0)) for v in (a, b, c, d)]
    return call(
        sum_core_kernel,
        "sum_core",
        ids,
        (a, b, c, d),
        specs,
        [shape_of(a.shape, BF16), shape_of(c.shape, BF16)],
        [specs[0], specs[2]],
        grid=(steps,),
    )


def widen_kernel(*refs):
    half = len(refs) // 2
    for src, dst in zip(refs[:half], refs[half:]):
        dst[...] = src[...].astype(F32)


def widen_attn(ids, total):
    steps = 4
    width = total.shape[1]
    part = total.shape[0] // (4 * steps)
    specs = [
        pl.BlockSpec((3 * part, width), lambda i: (i, 0)),
        pl.BlockSpec((part, width), lambda i: (3 * steps + i, 0)),
    ]
    return call(
        widen_kernel,
        "widen_attn",
        ids,
        (total, total),
        specs,
        [shape_of((12 * part, width), F32), shape_of((4 * part, width), F32)],
        [pl.BlockSpec((n * part, width), lambda i: (i, 0)) for n in (3, 1)],
        grid=(steps,),
    )


def widen(ids, *arrays):
    steps = 4
    specs = [pl.BlockSpec((v.shape[0] // steps, v.shape[1]), lambda i: (i, 0)) for v in arrays]
    return call(
        widen_kernel, "widen", ids, arrays, specs, [shape_of(v.shape, F32) for v in arrays], specs, grid=(steps,)
    )


def sum_kernel(got_ref, out_ref):
    rows = out_ref.shape[0]
    parts = got_ref.shape[0] // rows
    total = got_ref[:rows, :].astype(F32)
    for i in range(1, parts):
        total = total + got_ref[i * rows : (i + 1) * rows, :].astype(F32)
    out_ref[...] = total.astype(BF16)


def sum_parts(token, got, dp):
    width = got.shape[1]
    rows = got.shape[0] // (2 * dp)
    if rows % 16:
        total = jnp.sum(got.reshape(2 * dp, rows, width).astype(F32), axis=0).astype(BF16)
        return [jnp.tile(total, (dp, 1))], token
    return call(
        sum_kernel,
        "sum_parts",
        token,
        (got,),
        [whole(got.shape)],
        [shape_of((dp * rows, width), BF16)],
        [pl.BlockSpec((rows, width), lambda i: (i, 0))],
        grid=(dp,),
    )


def region(always, fn, ids):
    outs = jax.eval_shape(fn, ids)
    return lax.cond(always, fn, lambda _: jax.tree.map(lambda o: jnp.zeros(o.shape, o.dtype), outs), ids)


def per_device(dp, inputs, gain_attn, w_qkv, w_out, gain_ffn, w_in, w_back, bias_table, lengths, buckets, cotangent):
    width = inputs.shape[1]
    seq = buckets.shape[0]
    docs = lengths.shape[0] // 2
    table_rows, heads = bias_table.shape
    gains = jnp.stack([gain_attn, gain_ffn]).astype(F32)
    ids = jnp.zeros((8, 128), F32)

    def from_core(v):
        return lax.ppermute(v, "core", [(0, 1), (1, 0)])

    def from_x(v):
        return lax.ppermute(v, "x", [(0, 1), (1, 0)])

    def scatter(v):
        return lax.all_to_all(v, ("core", "dp"), 0, 0, tiled=True)

    def spread(v):
        return lax.all_to_all(v, "dp", 0, 0, tiled=True)

    bias = jnp.pad(bias_table.T, ((0, BIAS_ROWS - heads), (0, width - table_rows)))
    attn_w = jnp.concatenate([w_qkv.transpose(0, 2, 1).reshape(-1, width), bias], axis=0)
    attn_w = jnp.concatenate([attn_w[: 3 * width // 4], w_out, attn_w[3 * width // 4 :]], axis=0)
    attn_c = from_core(attn_w)
    wo_x = from_x(w_out)
    wo_c = from_core(w_out)
    in_c = from_core(w_in)
    back_c = from_core(w_back)

    every = range(docs)
    normed, packed, probs, att, att_x = [], [], [], [], []
    for doc in every:
        if doc == 0:
            (w_own, u, n, a, b, c), ids = attn_fwd(
                ids, lengths, inputs, gains, (attn_w, attn_c), buckets, doc, docs
            )
            (wo_x,), ids = gate(ids, wo_x)
            wo_xc = from_core(wo_x)
        else:
            (n, a, b, c), ids = attn_fwd(ids, lengths, inputs, gains, (w_own, u), buckets, doc, docs)
        normed.append(n)
        packed.append(a)
        probs.append(b)
        att.append(c)
        att_x.append(from_x(c))

    middle, gown, hown, goth, grads = [], [], [], [], None
    for doc in every:
        (m, g, h, *grads), ids = ffn(
            ids, inputs, att[doc], att_x[doc], (w_out, wo_c, wo_x, wo_xc), gains, cotangent,
            (w_in, in_c), (w_back, back_c), grads, doc, docs,
        )
        middle.append(m)
        hown.append(h)
        if doc + 1 < docs:
            ids = need(ids, att_x[doc + 1])
        (g,), ids = gate(ids, g)
        gown.append(g)
        goth.append(from_x(g))
    always = lengths[0] > 0

    def ffn_grads(ids):
        gback, gback_c, gin, gin_c = grads
        return sum_core(ids, gback, from_core(gback_c), gin, from_core(gin_c))[::-1]

    ids = need(ids, goth[0])
    ids, (gback, gin) = region(always, ffn_grads, ids)
    gback, gin = lax.psum((gback, gin), "dp")

    def back_of(doc, ids):
        res, ids = attn_bwd(
            ids, middle[doc], gown[doc], goth[doc], gains, cotangent, w_out, wo_c, w_own, packed[doc], probs[doc],
            doc, docs,
        )
        return ids, res

    ids, first = back_of(0, ids)
    ids = need(ids, *goth[1:])

    def attention_back(ids):
        (nown_0,), ids = gate(ids, first[4])
        noth = [from_x(nown_0)]

        def others(ids):
            results = [first]
            for doc in range(1, docs):
                ids, res = back_of(doc, ids)
                results.append(res)
            gp, low = [r[3] for r in results], [r[1] for r in results]
            (gattn,), ids = grad_attn(ids, normed, gp, low, att, docs)
            return ids, results[1:], gattn

        ids, results, gattn = region(always, others, ids)
        gmid, low, ggain_two, gp, nown, diag = zip(first, *results)
        ids = need(ids, noth[0])
        nown = [nown_0] + list(nown[1:])
        for doc in range(1, docs):
            (nown[doc],), ids = gate(ids, nown[doc])
            noth.append(from_x(nown[doc]))
        (gattn,), ids = gate(ids, gattn)
        gattn = scatter(gattn)
        hsent, hoth = [], []
        for doc in every:
            (send,), ids = gate(ids, hown[doc])
            hsent.append(send)
            hoth.append(from_x(send))
        (gsrc, gsrc_send, ggain_one), ids = grad_input(ids, inputs, gains, gmid, nown, noth, docs)
        gsrc_got = from_core(gsrc_send)

        (gsrc,), ids = place(ids, gsrc, gsrc_got)
        ids = need(ids, *hoth)
        (gattn,), ids = sum_parts(ids, gattn, dp)
        return ids, gattn, gsrc, ggain_one, ggain_two, diag, hsent, hoth

    ids, gattn, gsrc, ggain_one, ggain_two, diag, hsent, hoth = region(always, attention_back, ids)
    gattn = spread(gattn)
    diag_bucket = jnp.concatenate([buckets[:, 0], buckets[:1, -1], buckets[:-1, -1]])
    one_hot = (diag_bucket[:, None] == jnp.arange(table_rows)[None, :]).astype(F32)
    diag = sum(diag).reshape(2 * heads, 2 * seq)
    table = lax.dot_general(
        diag, one_hot, (((1,), (0,)), ((), ())), precision=lax.Precision.HIGHEST, preferred_element_type=F32
    )
    ggain_two = sum(ggain_two)
    small = jnp.concatenate([ggain_one.reshape(-1), ggain_two.reshape(-1), table[:heads].reshape(-1)])
    small_send = jnp.concatenate([ggain_one.reshape(-1), ggain_two.reshape(-1), table[heads:].reshape(-1)])
    small = small + from_core(small_send)
    for s in range(dp.bit_length() - 1):
        small = small + lax.ppermute(small, "dp", [(i, i ^ (1 << s)) for i in range(dp)])
    grad_gain_attn, grad_gain_ffn = small[:width], small[width : 2 * width]
    grad_table = small[2 * width :].reshape(heads, table_rows).T
    (mixed, mixed_send), ids = mix(ids, middle, hsent, hoth, docs)
    ids = need(ids, grad_gain_attn, grad_gain_ffn, grad_table)
    mixed_got = from_core(mixed_send)
    (grad_w_back, grad_w_in), ids = widen(ids, gback, gin)
    (mixed,), ids = place(ids, mixed, mixed_got)
    (grad_w_qkv, grad_w_out), ids = widen_attn(ids, gattn)
    grad_w_qkv = grad_w_qkv.reshape(3, width // 4, width).transpose(0, 2, 1)
    return (
        mixed,
        gsrc,
        grad_gain_attn,
        grad_w_qkv,
        grad_w_out,
        grad_gain_ffn,
        grad_w_in,
        grad_w_back,
        grad_table,
    )


def solution(mesh):
    dp = mesh.shape["dp"]
    devices = mesh.devices.reshape(mesh.shape["tensor"] // 2, 2, dp)
    mesh = jax.sharding.Mesh(devices, ("x", "core", "dp"))
    return jax.shard_map(
        functools.partial(per_device, dp),
        mesh=mesh,
        in_specs=(
            P("dp", None),
            P(),
            P(None, None, ("x", "core")),
            P(("x", "core"), None),
            P(),
            P(None, ("x", "core")),
            P(("x", "core"), None),
            P(None, ("x", "core")),
            P("dp"),
            P(),
            P("dp", None),
        ),
        out_specs=(
            P("dp", None),
            P("dp", None),
            P(),
            P(None, None, ("x", "core")),
            P(("x", "core"), None),
            P(),
            P(None, ("x", "core")),
            P(("x", "core"), None),
            P(None, ("x", "core")),
        ),
        check_vma=False,
    )
```

```python
import functools
import math

import jax
import jax.numpy as jnp
from jax import lax
from jax.experimental import pallas as pl
from jax.experimental.pallas import tpu as pltpu
from jax.sharding import PartitionSpec as P

HD = 64
PAIR = 2 * HD
EPS = 1e-06
MASKED = -1000000000.0
GELU_C = 0.7978845608028654
GELU_A = 0.044715
CHUNK = 256
VMEM_BYTES = 18 * 1024 * 1024

F32 = jnp.float32
BF16 = jnp.bfloat16


def dot_nn(a, b):
    return lax.dot_general(a, b, (((1,), (0,)), ((), ())), preferred_element_type=F32)


def dot_nt(a, b):
    return lax.dot_general(a, b, (((1,), (1,)), ((), ())), preferred_element_type=F32)


def dot_tn(a, b):
    return lax.dot_general(a, b, (((0,), (0,)), ((), ())), preferred_element_type=F32)


def whole(shape):
    return pl.BlockSpec(shape, lambda *_: (0,) * len(shape))


def shape_of(shape, dtype):
    return jax.ShapeDtypeStruct(shape, dtype)


def call(kernel, name, token, args, in_specs, outs, out_specs, grid=(1,), scratch=(), aliases=None, vmem=VMEM_BYTES):
    n_in, n_out = len(args), len(outs)

    def body(token_ref, *refs):
        del token_ref
        kernel(*refs[:n_in], *refs[n_in + 1 :])

    anywhere = pl.BlockSpec(memory_space=pl.ANY)
    res = pl.pallas_call(
        body,
        grid=grid,
        in_specs=[anywhere] + list(in_specs),
        out_specs=[anywhere] + list(out_specs),
        scratch_shapes=list(scratch),
        out_shape=[shape_of(token.shape, token.dtype)] + list(outs),
        input_output_aliases={0: 0, **(aliases or {})},
        compiler_params=pltpu.CompilerParams(vmem_limit_bytes=vmem),
        name=name,
    )(token, *args)
    return res[1:], res[0]


def rms_rows(v):
    return lax.rsqrt(jnp.mean(v * v, axis=-1, keepdims=True) + EPS)


def doc_rows(seq, width, docs, doc):
    return pl.BlockSpec((seq, width), lambda i: (lax.axis_index("core") * docs + doc, 0))


BIAS_ROWS = 16


def assemble(first_ref, second_ref, w_ref, width):
    cols = width // 4
    heads = cols // HD
    sources = [(first_ref, h) for h in range(heads)] + [(second_ref, h) for h in range(heads)]
    for p in range(heads):
        for part in range(3):
            for i in range(2):
                ref, head = sources[2 * p + i]
                src = part * cols + head * HD
                dst = (3 * p + part) * PAIR + i * HD
                w_ref[dst : dst + HD, :] = ref[src : src + HD, :]


def bias_along(first_ref, second_ref, left_ref, right_ref, u_ref, width):
    seq = left_ref.shape[0]
    left = left_ref[...].astype(F32).T[:1, :]
    right = right_ref[...].astype(F32).T[PAIR - 1 :, :]
    bucket = jnp.concatenate([left, pltpu.roll(right, 1, 1)], axis=1)
    index = lax.broadcasted_iota(jnp.int32, (PAIR, 2 * seq), 0).astype(F32)
    one_hot = (index == bucket).astype(BF16)
    heads = width // 4 // HD
    for at, ref in ((0, first_ref), (heads, second_ref)):
        u = dot_nn(ref[width:, :PAIR], one_hot)
        u_ref[at : at + heads, :] = u[:heads]


def attn_fwd_kernel(
    first, doc, docs, seq, len_ref, src_ref, gains_ref, *refs
):
    step = pl.program_id(0)
    if first:
        first_ref, second_ref, left_ref, right_ref, w_ref, u_ref, *refs = refs
    else:
        w_ref, u_ref, *refs = refs
    normed_ref, packed_ref, probs_ref, att_ref = refs

    @pl.when(step == 0)
    def _():
        if first:
            assemble(first_ref, second_ref, w_ref, src_ref.shape[1])
            bias_along(first_ref, second_ref, left_ref, right_ref, u_ref, src_ref.shape[1])
        for start in range(0, src_ref.shape[0], CHUNK):
            at = slice(start, start + CHUNK)
            v = src_ref[at, :].astype(F32)
            normed_ref[at, :] = (v * rms_rows(v) * gains_ref[:1, :]).astype(BF16)

    at = pl.multiple_of(step * 3 * PAIR, 3 * PAIR)
    packed = dot_nt(normed_ref[...], w_ref[pl.ds(at, 3 * PAIR), :])
    lane = lax.broadcasted_iota(jnp.int32, (seq, PAIR), 1)
    scale = 1.0 / math.sqrt(HD)
    packed_ref[:, :PAIR] = (packed[:, :PAIR].astype(BF16).astype(F32) * scale).astype(BF16)
    packed_ref[:, PAIR:] = packed[:, PAIR:].astype(BF16)
    key_pos = lax.broadcasted_iota(jnp.int32, (seq, 1), 0)
    length = len_ref[lax.axis_index("core") * docs + doc]
    for head in range(2):
        row = jnp.broadcast_to(u_ref[pl.ds(2 * step + head, 1), :], (seq, 2 * seq))
        rel = pltpu.roll(row, 0, 1, stride=1, stride_axis=0)[:, :seq]
        mine = (lane >= HD) if head else (lane < HD)
        q = packed_ref[:, :PAIR]
        k = packed_ref[:, PAIR : 2 * PAIR]
        v = packed_ref[:, 2 * PAIR :]
        k = jnp.where(mine, k, jnp.zeros_like(k))
        scores = dot_nt(k, q) + rel
        scores = jnp.where(key_pos < length, scores, MASKED)
        top = jnp.max(scores, axis=0, keepdims=True)
        e = jnp.exp(scores - top)
        total = jnp.sum(e, axis=0, keepdims=True)
        p = (e * (1.0 / total)).astype(BF16)
        probs_ref[head] = p
        vt = v.T[head * HD : (head + 1) * HD, :]
        o = dot_nn(vt, p)
        att_ref[:, head * HD : (head + 1) * HD] = o.T.astype(BF16)


def attn_fwd(ids, lengths, inputs, gains, weights, buckets, doc, docs):
    seq = buckets.shape[0]
    width = inputs.shape[1]
    pairs = width // (4 * HD)
    first = doc == 0
    specs = [pl.BlockSpec(memory_space=pltpu.SMEM), doc_rows(seq, width, docs, doc), whole(gains.shape)]
    args = (lengths, inputs, gains) + tuple(weights)
    specs += [whole(w.shape) for w in weights]
    outs, out_specs = [], []
    if first:
        last = seq // PAIR - 1
        args += (buckets, buckets)
        specs += [
            pl.BlockSpec((seq, PAIR), lambda p: (0, 0)),
            pl.BlockSpec((seq, PAIR), lambda p: (0, last)),
        ]
        outs = [shape_of((pairs * 3 * PAIR, width), BF16), shape_of((2 * pairs, 2 * seq), F32)]
        out_specs = [whole(o.shape) for o in outs]
    outs += [
        shape_of((seq, width), BF16),
        shape_of((seq, pairs * 3 * PAIR), BF16),
        shape_of((2 * pairs, seq, seq), BF16),
        shape_of((seq, pairs * PAIR), BF16),
    ]
    out_specs += [
        whole((seq, width)),
        pl.BlockSpec((seq, 3 * PAIR), lambda p: (0, p)),
        pl.BlockSpec((2, seq, seq), lambda p: (p, 0, 0)),
        pl.BlockSpec((seq, PAIR), lambda p: (0, p)),
    ]
    return call(
        functools.partial(attn_fwd_kernel, first, doc, docs, seq),
        "attn_fwd",
        ids,
        args,
        specs,
        outs,
        out_specs,
        grid=(pairs,),
    )


TILE = 256


def ffn_kernel(first, *refs):
    (
        src_ref, att_own_ref, att_oth_ref, wo_a_ref, wo_b_ref, wo_x_ref, wo_xc_ref, gains_ref, cot_ref,
        in_a_ref, in_b_ref, back_a_ref, back_b_ref, *refs,
    ) = refs
    if not first:
        gback_a_in, gback_b_in, gin_a_in, gin_b_in, *refs = refs
    (
        middle_ref, gsend_ref, hsend_ref, gback_a_ref, gback_b_ref, gin_a_ref, gin_b_ref,
        normed_ref, normed_t_ref, acc_ref, gacc_ref,
    ) = refs
    rows = src_ref.shape[0]
    step = pl.program_id(0)
    half = pl.num_programs(0) // 2

    @pl.when(step == 0)
    def _():
        swapped = lax.axis_index("x") != 0
        wo_own = jnp.concatenate([wo_a_ref[...], wo_b_ref[...]], axis=0)
        wo_oth = jnp.concatenate([wo_x_ref[...], wo_xc_ref[...]], axis=0)
        wo_0 = jnp.where(swapped, wo_oth, wo_own)
        wo_1 = jnp.where(swapped, wo_own, wo_oth)
        for start in range(0, rows, CHUNK):
            at = slice(start, start + CHUNK)
            own, oth = att_own_ref[at, :], att_oth_ref[at, :]
            terms = dot_nn(jnp.where(swapped, oth, own), wo_0) + dot_nn(jnp.where(swapped, own, oth), wo_1)
            m = src_ref[at, :].astype(F32) + terms
            middle_ref[at, :] = m
            normed = (m * rms_rows(m) * gains_ref[1:, :]).astype(BF16)
            normed_ref[at, :] = normed
            normed_t_ref[:, at] = normed.T
        acc_ref[...] = jnp.zeros(acc_ref.shape, F32)
        gacc_ref[...] = jnp.zeros(gacc_ref.shape, F32)

    mine = step < half
    w_in = jnp.where(mine, in_a_ref[...], in_b_ref[...])
    w_back = jnp.where(mine, back_a_ref[...], back_b_ref[...])
    hiddens, gpres = [], []
    for start in range(0, rows, 2 * CHUNK):
        at = slice(start, start + 2 * CHUNK)
        pre = dot_nn(normed_ref[at, :], w_in)
        ghid = dot_nt(cot_ref[at, :], w_back)
        sq = pre * pre
        t = jnp.tanh(pre * (GELU_C + (GELU_C * GELU_A) * sq))
        half_t = 0.5 + 0.5 * t
        act = pre * half_t
        hidden = act.astype(BF16)
        slope = half_t + (act * (1.0 - t)) * (GELU_C + (3.0 * GELU_C * GELU_A) * sq)
        gpre = (ghid * slope).astype(BF16)
        acc_ref[at, :] += dot_nn(hidden, w_back)
        gacc_ref[at, :] += dot_nt(gpre, w_in)
        hiddens.append(hidden)
        gpres.append(gpre)
    gback = dot_tn(jnp.concatenate(hiddens, axis=0), cot_ref[...])
    gin = dot_nn(normed_t_ref[...], jnp.concatenate(gpres, axis=0))

    @pl.when(mine)
    def _():
        if first:
            gback_a_ref[...] = gback.astype(BF16)
            gin_a_ref[...] = gin.astype(BF16)
        else:
            gback_a_ref[...] = (gback + gback_a_in[...].astype(F32)).astype(BF16)
            gin_a_ref[...] = (gin + gin_a_in[...].astype(F32)).astype(BF16)

    @pl.when(jnp.logical_not(mine))
    def _():
        if first:
            gback_b_ref[...] = gback.astype(BF16)
            gin_b_ref[...] = gin.astype(BF16)
        else:
            gback_b_ref[...] = (gback + gback_b_in[...].astype(F32)).astype(BF16)
            gin_b_ref[...] = (gin + gin_b_in[...].astype(F32)).astype(BF16)

    @pl.when(step == 2 * half - 1)
    def _():
        hsend_ref[...] = acc_ref[...].astype(BF16)
        gsend_ref[...] = gacc_ref[...].astype(BF16)


def ffn(ids, inputs, att_own, att_oth, wos, gains, cotangent, w_ins, w_backs, grads, doc, docs):
    seq = att_own.shape[0]
    width = inputs.shape[1]
    units = w_ins[0].shape[1]
    tiles = units // TILE
    mine = doc_rows(seq, width, docs, doc)

    def first_half(i):
        return jnp.minimum(i, tiles - 1)

    def second_half(i):
        return jnp.maximum(i - tiles, 0)

    def back_spec(of):
        return pl.BlockSpec((TILE, width), lambda i: (of(i), 0))

    def in_spec(of):
        return pl.BlockSpec((width, TILE), lambda i: (0, of(i)))

    grad_specs = [back_spec(first_half), back_spec(second_half), in_spec(first_half), in_spec(second_half)]
    outs = [
        shape_of((seq, width), F32),
        shape_of((seq, width), BF16),
        shape_of((seq, width), BF16),
        shape_of((units, width), BF16),
        shape_of((units, width), BF16),
        shape_of((width, units), BF16),
        shape_of((width, units), BF16),
    ]
    return call(
        functools.partial(ffn_kernel, grads is None),
        "ffn",
        ids,
        (inputs, att_own, att_oth) + wos + (gains, cotangent) + w_ins + w_backs + tuple(grads or ()),
        [mine, whole(att_own.shape), whole(att_oth.shape)]
        + [whole(w.shape) for w in wos]
        + [whole(gains.shape), mine]
        + [in_spec(first_half), in_spec(second_half), back_spec(first_half), back_spec(second_half)]
        + (grad_specs if grads else []),
        outs,
        [whole(o.shape) for o in outs[:3]] + grad_specs,
        grid=(2 * tiles,),
        vmem=56 * 1024 * 1024,
        scratch=[
            pltpu.VMEM((seq, width), BF16),
            pltpu.VMEM((width, seq), BF16),
            pltpu.VMEM((seq, width), F32),
            pltpu.VMEM((seq, width), F32),
        ],
    )


def fold_diagonals(g, seq):
    g = jnp.concatenate([g, jnp.zeros_like(g)], axis=1)
    n = seq
    while n > 8:
        n //= 2
        g = g[:n] + pltpu.roll(g[n:], 2 * seq - n, 1)
    while n > 1:
        n //= 2
        g = g[:n] + jnp.concatenate([g[n:, n:], g[n:, :n]], axis=1)
    return g


def attn_bwd_kernel(
    seq, middle_ref, gown_ref, goth_ref, gains_ref, cot_ref, wo_a_ref, wo_b_ref, w_ref, packed_ref, probs_ref,
    gmid_ref, low_ref, ggain_ref, gp_ref, nsend_ref, diag_ref, dout_ref, acc_ref,
):
    step = pl.program_id(0)
    pairs = pl.num_programs(0)

    @pl.when(step == 0)
    def _():
        wo_own = jnp.concatenate([wo_a_ref[...], wo_b_ref[...]], axis=0)
        ggain = jnp.zeros(ggain_ref.shape, F32)
        for start in range(0, seq, CHUNK):
            at = slice(start, start + CHUNK)
            m = middle_ref[at, :]
            gnorm = gown_ref[at, :].astype(F32) + goth_ref[at, :].astype(F32)
            r = rms_rows(m)
            ggain = ggain + jnp.sum(gnorm * m * r, axis=0, keepdims=True)
            back = gains_ref[1:, :] * gnorm
            inner = jnp.mean(back * m, axis=-1, keepdims=True)
            gm = cot_ref[at, :].astype(F32) + r * back - m * (r * r * r * inner)
            gmid_ref[at, :] = gm
            low = gm.astype(BF16)
            low_ref[at, :] = low
            dout = dot_nt(low, wo_own).astype(BF16)
            for p in range(dout_ref.shape[0]):
                dout_ref[p, at, :] = dout[:, p * PAIR : (p + 1) * PAIR]
        ggain_ref[...] = ggain

    lane = lax.broadcasted_iota(jnp.int32, (seq, PAIR), 1)
    scale = 1.0 / math.sqrt(HD)
    q = packed_ref[:, :PAIR]
    k = packed_ref[:, PAIR : 2 * PAIR]
    v = packed_ref[:, 2 * PAIR :]
    do = dout_ref[step]
    kt = k.T
    dqs, dks, dvs = [], [], []
    for head in range(2):
        mine = (lane >= HD) if head else (lane < HD)
        vm = jnp.where(mine, v, jnp.zeros_like(v))
        dp = dot_nt(vm, do)
        p_low = probs_ref[head]
        p = p_low.astype(F32)
        mean = jnp.sum(dp * p, axis=0, keepdims=True)
        ds = (p * (dp - mean)).astype(BF16)
        diag_ref[0, head : head + 1, :] = fold_diagonals(ds.astype(F32), seq)
        dvs.append(dot_nn(p_low, do))
        dks.append(dot_nn(ds, q))
        dqs.append(dot_nn(kt[head * HD : (head + 1) * HD, :], ds))
    dq = jnp.concatenate(dqs, axis=0).T * scale
    first = lane < HD
    gp_ref[:, :PAIR] = dq.astype(BF16)
    gp_ref[:, PAIR : 2 * PAIR] = jnp.where(first, dks[0], dks[1]).astype(BF16)
    gp_ref[:, 2 * PAIR :] = jnp.where(first, dvs[0], dvs[1]).astype(BF16)
    terms = dot_nn(gp_ref[...], w_ref[...])

    @pl.when(step == 0)
    def _():
        acc_ref[...] = terms

    @pl.when(step != 0)
    def _():
        acc_ref[...] += terms

    @pl.when(step == pairs - 1)
    def _():
        nsend_ref[...] = acc_ref[...].astype(BF16)


def attn_bwd(ids, middle, gown, goth, gains, cotangent, wo_a, wo_b, w_own, packed, probs, doc, docs):
    seq, width = middle.shape
    pairs = packed.shape[1] // (3 * PAIR)
    mine = doc_rows(seq, width, docs, doc)
    outs = [
        shape_of((seq, width), F32),
        shape_of((seq, width), BF16),
        shape_of((1, width), F32),
        shape_of(packed.shape, BF16),
        shape_of((seq, width), BF16),
        shape_of((pairs, 2, 2 * seq), F32),
    ]
    return call(
        functools.partial(attn_bwd_kernel, seq),
        "attn_bwd",
        ids,
        (middle, gown, goth, gains, cotangent, wo_a, wo_b, w_own, packed, probs),
        [whole(middle.shape), whole(gown.shape), whole(goth.shape), whole(gains.shape), mine]
        + [whole(wo_a.shape), whole(wo_b.shape)]
        + [
            pl.BlockSpec((3 * PAIR, width), lambda p: (p, 0)),
            pl.BlockSpec((seq, 3 * PAIR), lambda p: (0, p)),
            pl.BlockSpec((2, seq, seq), lambda p: (p, 0, 0)),
        ],
        outs,
        [
            whole((seq, width)),
            whole((seq, width)),
            whole((1, width)),
            pl.BlockSpec((seq, 3 * PAIR), lambda p: (0, p)),
            whole((seq, width)),
            pl.BlockSpec((1, 2, 2 * seq), lambda p: (p, 0, 0)),
        ],
        grid=(pairs,),
        scratch=[pltpu.VMEM((pairs, seq, PAIR), BF16), pltpu.VMEM((seq, width), F32)],
    )


def grad_attn_kernel(docs, pairs, *refs):
    groups = [refs[i * docs : (i + 1) * docs] for i in range(4)]
    mine_ref, other_ref = refs[4 * docs :]
    normed, gp, low, att = (jnp.concatenate([r[...] for r in g], axis=0) for g in groups)
    step = pl.program_id(0)
    cols = mine_ref.shape[0] // 4
    heads = cols // HD
    grads = dot_tn(gp, normed).astype(BF16)
    outer = dot_tn(att, low).astype(BF16)
    for p in range(pairs):

        @pl.when(step == p)
        def _(p=p):
            for i in range(2):
                head = 2 * p + i
                ref = mine_ref if head < heads else other_ref
                at = (head % heads) * HD
                for part in range(3):
                    piece = grads[part * PAIR + i * HD : part * PAIR + (i + 1) * HD, :]
                    ref[part * cols + at : part * cols + at + HD, :] = piece
                ref[3 * cols + at : 3 * cols + at + HD, :] = outer[i * HD : (i + 1) * HD, :]


def grad_attn(ids, normeds, gps, lows, atts, docs):
    seq, width = normeds[0].shape
    pairs = atts[0].shape[1] // PAIR
    outs = [shape_of((width, width), BF16)] * 2
    return call(
        functools.partial(grad_attn_kernel, docs, pairs),
        "grad_attn",
        ids,
        tuple(normeds) + tuple(gps) + tuple(lows) + tuple(atts),
        [whole((seq, width))] * docs
        + [pl.BlockSpec((seq, 3 * PAIR), lambda p: (0, p))] * docs
        + [whole((seq, width))] * docs
        + [pl.BlockSpec((seq, PAIR), lambda p: (0, p))] * docs,
        outs,
        [whole((width, width))] * 2,
        grid=(pairs,),
    )


def grad_input_kernel(docs, src_ref, gains_ref, *refs):
    gmid_refs, own_refs, oth_refs = (refs[i * docs : (i + 1) * docs] for i in range(3))
    full_ref, send_ref, ggain_ref = refs[3 * docs :]
    seq = gmid_refs[0].shape[0]
    ggain = jnp.zeros(ggain_ref.shape, F32)
    for doc in range(docs):
        for start in range(0, seq, CHUNK):
            here = slice(start, start + CHUNK)
            at = slice(doc * seq + start, doc * seq + start + CHUNK)
            gnorm = own_refs[doc][here, :].astype(F32) + oth_refs[doc][here, :].astype(F32)
            v = src_ref[at, :].astype(F32)
            r = rms_rows(v)
            ggain = ggain + jnp.sum(gnorm * v * r, axis=0, keepdims=True)
            back = gains_ref[:1, :] * gnorm
            inner = jnp.mean(back * v, axis=-1, keepdims=True)
            out = gmid_refs[doc][here, :] + r * back - v * (r * r * r * inner)
            full_ref[at, :] = out
            send_ref[at, :] = out
    ggain_ref[...] = ggain


def grad_input(ids, inputs, gains, gmids, owns, oths, docs):
    seq, width = gmids[0].shape
    rows = docs * seq
    mine = pl.BlockSpec((rows, width), lambda i: (lax.axis_index("core"), 0))
    return call(
        functools.partial(grad_input_kernel, docs),
        "grad_input",
        ids,
        (inputs, gains) + tuple(gmids) + tuple(owns) + tuple(oths),
        [mine, whole(gains.shape)] + [whole((seq, width))] * (3 * docs),
        [shape_of((2 * rows, width), F32), shape_of((rows, width), F32), shape_of((1, width), F32)],
        [mine, whole((rows, width)), whole((1, width))],
    )


def mix_kernel(docs, *refs):
    middle_refs, own_refs, oth_refs = (refs[i * docs : (i + 1) * docs] for i in range(3))
    full_ref, send_ref = refs[3 * docs :]
    seq = middle_refs[0].shape[0]
    for doc in range(docs):
        at = slice(doc * seq, (doc + 1) * seq)
        terms = own_refs[doc][...].astype(F32) + oth_refs[doc][...].astype(F32)
        out = (middle_refs[doc][...] + terms).astype(BF16)
        full_ref[at, :] = out
        send_ref[at, :] = out


def mix(ids, middles, owns, oths, docs):
    seq, width = middles[0].shape
    rows = docs * seq
    return call(
        functools.partial(mix_kernel, docs),
        "mix",
        ids,
        tuple(middles) + tuple(owns) + tuple(oths),
        [whole((seq, width))] * (3 * docs),
        [shape_of((2 * rows, width), BF16), shape_of((rows, width), BF16)],
        [pl.BlockSpec((rows, width), lambda i: (lax.axis_index("core"), 0)), whole((rows, width))],
    )


def place_kernel(full_ref, got_ref, out_ref):
    out_ref[...] = got_ref[...]


def place(ids, full, got):
    rows, width = got.shape
    steps = 4
    part = rows // steps
    return call(
        place_kernel,
        "place",
        ids,
        (full, got),
        [pl.BlockSpec(memory_space=pl.ANY), pl.BlockSpec((part, width), lambda i: (i, 0))],
        [shape_of(full.shape, full.dtype)],
        [pl.BlockSpec((part, width), lambda i: ((1 - lax.axis_index("core")) * steps + i, 0))],
        grid=(steps,),
        aliases={1: 1},
    )


def gate(ids, *arrays):
    anywhere = [pl.BlockSpec(memory_space=pl.ANY)] * len(arrays)
    shapes = [shape_of(v.shape, v.dtype) for v in arrays]
    aliases = {i + 1: i + 1 for i in range(len(arrays))}
    return call(lambda *refs: None, "gate", ids, arrays, anywhere, shapes, anywhere, aliases=aliases)


def need(ids, *arrays):
    anywhere = pl.BlockSpec(memory_space=pl.ANY)
    return call(lambda *refs: None, "need", ids, arrays, [anywhere] * len(arrays), [], [])[1]


def sum_core_kernel(*refs):
    for i, out_ref in enumerate(refs[2 * len(refs) // 3 :]):
        out_ref[...] = (refs[2 * i][...].astype(F32) + refs[2 * i + 1][...].astype(F32)).astype(BF16)


def sum_core(ids, *arrays):
    steps = 2
    specs = [pl.BlockSpec((v.shape[0] // steps, v.shape[1]), lambda i: (i, 0)) for v in arrays]
    outs = [shape_of(v.shape, BF16) for v in arrays[::2]]
    return call(sum_core_kernel, "sum_core", ids, arrays, specs, outs, specs[::2], grid=(steps,))


def widen_kernel(*refs):
    half = len(refs) // 2
    for src, dst in zip(refs[:half], refs[half:]):
        dst[...] = src[...].astype(F32)


def widen_attn(ids, total):
    steps = 4
    width = total.shape[1]
    part = total.shape[0] // (4 * steps)
    specs = [
        pl.BlockSpec((3 * part, width), lambda i: (i, 0)),
        pl.BlockSpec((part, width), lambda i: (3 * steps + i, 0)),
    ]
    return call(
        widen_kernel,
        "widen_attn",
        ids,
        (total, total),
        specs,
        [shape_of((12 * part, width), F32), shape_of((4 * part, width), F32)],
        [pl.BlockSpec((n * part, width), lambda i: (i, 0)) for n in (3, 1)],
        grid=(steps,),
    )


def widen(ids, *arrays):
    steps = 4
    specs = [pl.BlockSpec((v.shape[0] // steps, v.shape[1]), lambda i: (i, 0)) for v in arrays]
    return call(
        widen_kernel, "widen", ids, arrays, specs, [shape_of(v.shape, F32) for v in arrays], specs, grid=(steps,)
    )


def sum_kernel(got_ref, out_ref):
    rows = out_ref.shape[0]
    parts = got_ref.shape[0] // rows
    total = got_ref[:rows, :].astype(F32)
    for i in range(1, parts):
        total = total + got_ref[i * rows : (i + 1) * rows, :].astype(F32)
    out_ref[...] = total.astype(BF16)


def sum_parts(token, got, dp):
    width = got.shape[1]
    rows = got.shape[0] // dp
    if rows % 16:
        total = jnp.sum(got.reshape(dp, rows, width).astype(F32), axis=0).astype(BF16)
        return [jnp.tile(total, (dp, 1))], token
    return call(
        sum_kernel,
        "sum_parts",
        token,
        (got,),
        [whole(got.shape)],
        [shape_of((dp * rows, width), BF16)],
        [pl.BlockSpec((rows, width), lambda i: (i, 0))],
        grid=(dp,),
    )


def region(always, fn, ids):
    outs = jax.eval_shape(fn, ids)
    return lax.cond(always, fn, lambda _: jax.tree.map(lambda o: jnp.zeros(o.shape, o.dtype), outs), ids)


def per_device(dp, inputs, gain_attn, w_qkv, w_out, gain_ffn, w_in, w_back, bias_table, lengths, buckets, cotangent):
    width = inputs.shape[1]
    seq = buckets.shape[0]
    docs = lengths.shape[0] // 2
    table_rows, heads = bias_table.shape
    gains = jnp.stack([gain_attn, gain_ffn]).astype(F32)
    ids = jnp.zeros((8, 128), F32)

    def from_core(v):
        return lax.ppermute(v, "core", [(0, 1), (1, 0)])

    def from_x(v):
        return lax.ppermute(v, "x", [(0, 1), (1, 0)])

    def spread(v):
        return lax.all_to_all(v, "dp", 0, 0, tiled=True)

    bias = jnp.pad(bias_table.T, ((0, BIAS_ROWS - heads), (0, width - table_rows)))
    attn_w = jnp.concatenate([w_qkv.transpose(0, 2, 1).reshape(-1, width), bias], axis=0)
    attn_w = jnp.concatenate([attn_w[: 3 * width // 4], w_out, attn_w[3 * width // 4 :]], axis=0)
    attn_c = from_core(attn_w)
    wo_x = from_x(w_out)
    wo_c = from_core(w_out)
    in_c = from_core(w_in)
    back_c = from_core(w_back)

    every = range(docs)
    normed, packed, probs, att, att_x = [], [], [], [], []
    for doc in every:
        if doc == 0:
            (w_own, u, n, a, b, c), ids = attn_fwd(
                ids, lengths, inputs, gains, (attn_w, attn_c), buckets, doc, docs
            )
            (wo_x,), ids = gate(ids, wo_x)
            wo_xc = from_core(wo_x)
        else:
            (n, a, b, c), ids = attn_fwd(ids, lengths, inputs, gains, (w_own, u), buckets, doc, docs)
        normed.append(n)
        packed.append(a)
        probs.append(b)
        att.append(c)
        att_x.append(from_x(c))

    middle, gown, hown, goth, grads = [], [], [], [], None
    for doc in every:
        (m, g, h, *grads), ids = ffn(
            ids, inputs, att[doc], att_x[doc], (w_out, wo_c, wo_x, wo_xc), gains, cotangent,
            (w_in, in_c), (w_back, back_c), grads, doc, docs,
        )
        middle.append(m)
        hown.append(h)
        if doc + 1 < docs:
            ids = need(ids, att_x[doc + 1])
        (g,), ids = gate(ids, g)
        gown.append(g)
        goth.append(from_x(g))
    always = lengths[0] > 0

    def ffn_grads(ids):
        gback, gback_c, gin, gin_c = grads
        return sum_core(ids, gback, from_core(gback_c), gin, from_core(gin_c))[::-1]

    ids = need(ids, goth[0])
    ids, (gback, gin) = region(always, ffn_grads, ids)
    gback, gin = lax.psum((gback, gin), "dp")

    def back_of(doc, ids):
        res, ids = attn_bwd(
            ids, middle[doc], gown[doc], goth[doc], gains, cotangent, w_out, wo_c, w_own, packed[doc], probs[doc],
            doc, docs,
        )
        return ids, res

    ids, first = back_of(0, ids)
    ids = need(ids, *goth[1:])

    def attention_back(ids):
        (nown_0,), ids = gate(ids, first[4])
        noth = [from_x(nown_0)]

        def others(ids):
            results = [first]
            for doc in range(1, docs):
                ids, res = back_of(doc, ids)
                results.append(res)
            gp, low = [r[3] for r in results], [r[1] for r in results]
            (gattn, gattn_c), ids = grad_attn(ids, normed, gp, low, att, docs)
            return ids, results[1:], gattn, gattn_c

        ids, results, gattn, gattn_c = region(always, others, ids)
        gmid, low, ggain_two, gp, nown, diag = zip(first, *results)
        ids = need(ids, noth[0])
        (gattn_c,), ids = gate(ids, gattn_c)
        (gattn,), ids = sum_core(ids, gattn, from_core(gattn_c))
        gattn = spread(gattn)

        def rows_back(ids):
            mine, got = [nown_0] + list(nown[1:]), list(noth)
            for doc in range(1, docs):
                (mine[doc],), ids = gate(ids, mine[doc])
                got.append(from_x(mine[doc]))
            sent, hoth = list(hown), []
            for doc in range(docs // 2):
                (sent[doc],), ids = gate(ids, sent[doc])
                hoth.append(from_x(sent[doc]))
            (gsrc, gsrc_send, ggain_one), ids = grad_input(ids, inputs, gains, gmid, mine, got, docs)
            diag_bucket = jnp.concatenate([buckets[:, 0], buckets[:1, -1], buckets[:-1, -1]])
            one_hot = (diag_bucket[:, None] == jnp.arange(table_rows)[None, :]).astype(F32)
            diags = sum(diag).reshape(2 * heads, 2 * seq)
            table = lax.dot_general(
                diags, one_hot, (((1,), (0,)), ((), ())), precision=lax.Precision.HIGHEST, preferred_element_type=F32
            )
            ggain_ffn = sum(ggain_two)
            small = jnp.concatenate([ggain_one.reshape(-1), ggain_ffn.reshape(-1), table[:heads].reshape(-1)])
            small_send = jnp.concatenate([ggain_one.reshape(-1), ggain_ffn.reshape(-1), table[heads:].reshape(-1)])
            small = small + from_core(small_send)
            for s in range(dp.bit_length() - 1):
                small = small + lax.ppermute(small, "dp", [(i, i ^ (1 << s)) for i in range(dp)])
            grad_gain_attn, grad_gain_ffn = small[:width], small[width : 2 * width]
            grad_table = small[2 * width :].reshape(heads, table_rows).T
            ids = need(ids, grad_gain_attn, grad_gain_ffn, grad_table)
            (gsrc,), ids = place(ids, gsrc, from_core(gsrc_send))
            ids = need(ids, *hoth)
            return ids, gsrc, (grad_gain_attn, grad_gain_ffn, grad_table), sent, hoth

        ids, gsrc, smalls, hsent, hoth = region(always, rows_back, ids)
        (gattn,), ids = sum_parts(ids, gattn, dp)
        return ids, gattn, gsrc, smalls, hsent, hoth

    ids, gattn, gsrc, smalls, hsent, hoth = region(always, attention_back, ids)
    grad_gain_attn, grad_gain_ffn, grad_table = smalls
    for doc in range(docs // 2, docs):
        (hsent[doc],), ids = gate(ids, hsent[doc])
        hoth.append(from_x(hsent[doc]))
    gattn = spread(gattn)
    (grad_w_back, grad_w_in), ids = widen(ids, gback, gin)
    (mixed, mixed_send), ids = mix(ids, middle, hsent, hoth, docs)
    mixed_got = from_core(mixed_send)
    (mixed,), ids = place(ids, mixed, mixed_got)
    (grad_w_qkv, grad_w_out), ids = widen_attn(ids, gattn)
    grad_w_qkv = grad_w_qkv.reshape(3, width // 4, width).transpose(0, 2, 1)
    return (
        mixed,
        gsrc,
        grad_gain_attn,
        grad_w_qkv,
        grad_w_out,
        grad_gain_ffn,
        grad_w_in,
        grad_w_back,
        grad_table,
    )


def solution(mesh):
    dp = mesh.shape["dp"]
    devices = mesh.devices.reshape(mesh.shape["tensor"] // 2, 2, dp)
    mesh = jax.sharding.Mesh(devices, ("x", "core", "dp"))
    return jax.shard_map(
        functools.partial(per_device, dp),
        mesh=mesh,
        in_specs=(
            P("dp", None),
            P(),
            P(None, None, ("x", "core")),
            P(("x", "core"), None),
            P(),
            P(None, ("x", "core")),
            P(("x", "core"), None),
            P(None, ("x", "core")),
            P("dp"),
            P(),
            P("dp", None),
        ),
        out_specs=(
            P("dp", None),
            P("dp", None),
            P(),
            P(None, None, ("x", "core")),
            P(("x", "core"), None),
            P(),
            P(None, ("x", "core")),
            P(("x", "core"), None),
            P(None, ("x", "core")),
        ),
        check_vma=False,
    )
```

```python
import functools
import math

import jax
import jax.numpy as jnp
from jax import lax
from jax.experimental import pallas as pl
from jax.experimental.pallas import tpu as pltpu
from jax.sharding import PartitionSpec as P

HD = 64
PAIR = 2 * HD
EPS = 1e-06
MASKED = -1000000000.0
GELU_C = 0.7978845608028654
GELU_A = 0.044715
CHUNK = 256
VMEM_BYTES = 18 * 1024 * 1024

F32 = jnp.float32
BF16 = jnp.bfloat16


def dot_nn(a, b):
    return lax.dot_general(a, b, (((1,), (0,)), ((), ())), preferred_element_type=F32)


def dot_nt(a, b):
    return lax.dot_general(a, b, (((1,), (1,)), ((), ())), preferred_element_type=F32)


def dot_tn(a, b):
    return lax.dot_general(a, b, (((0,), (0,)), ((), ())), preferred_element_type=F32)


def whole(shape):
    return pl.BlockSpec(shape, lambda *_: (0,) * len(shape))


def shape_of(shape, dtype):
    return jax.ShapeDtypeStruct(shape, dtype)


def call(kernel, name, token, args, in_specs, outs, out_specs, grid=(1,), scratch=(), aliases=None, vmem=VMEM_BYTES):
    n_in, n_out = len(args), len(outs)

    def body(token_ref, *refs):
        del token_ref
        kernel(*refs[:n_in], *refs[n_in + 1 :])

    anywhere = pl.BlockSpec(memory_space=pl.ANY)
    res = pl.pallas_call(
        body,
        grid=grid,
        in_specs=[anywhere] + list(in_specs),
        out_specs=[anywhere] + list(out_specs),
        scratch_shapes=list(scratch),
        out_shape=[shape_of(token.shape, token.dtype)] + list(outs),
        input_output_aliases={0: 0, **(aliases or {})},
        compiler_params=pltpu.CompilerParams(vmem_limit_bytes=vmem),
        name=name,
    )(token, *args)
    return res[1:], res[0]


def rms_rows(v):
    return lax.rsqrt(jnp.mean(v * v, axis=-1, keepdims=True) + EPS)


def doc_rows(seq, width, docs, doc):
    return pl.BlockSpec((seq, width), lambda i: (lax.axis_index("core") * docs + doc, 0))


BIAS_ROWS = 16


def assemble(first_ref, second_ref, w_ref, width):
    cols = width // 4
    heads = cols // HD
    sources = [(first_ref, h) for h in range(heads)] + [(second_ref, h) for h in range(heads)]
    for p in range(heads):
        for part in range(3):
            for i in range(2):
                ref, head = sources[2 * p + i]
                src = part * cols + head * HD
                dst = (3 * p + part) * PAIR + i * HD
                w_ref[dst : dst + HD, :] = ref[src : src + HD, :]


def bias_along(first_ref, second_ref, left_ref, right_ref, u_ref, width):
    seq = left_ref.shape[0]
    left = left_ref[...].astype(F32).T[:1, :]
    right = right_ref[...].astype(F32).T[PAIR - 1 :, :]
    bucket = jnp.concatenate([left, pltpu.roll(right, 1, 1)], axis=1)
    index = lax.broadcasted_iota(jnp.int32, (PAIR, 2 * seq), 0).astype(F32)
    one_hot = (index == bucket).astype(BF16)
    heads = width // 4 // HD
    for at, ref in ((0, first_ref), (heads, second_ref)):
        u = dot_nn(ref[width:, :PAIR], one_hot)
        u_ref[at : at + heads, :] = u[:heads]


def attn_fwd_kernel(
    first, doc, docs, seq, len_ref, src_ref, gains_ref, *refs
):
    step = pl.program_id(0)
    if first:
        first_ref, second_ref, left_ref, right_ref, w_ref, u_ref, *refs = refs
    else:
        w_ref, u_ref, *refs = refs
    normed_ref, packed_ref, probs_ref, att_ref = refs

    @pl.when(step == 0)
    def _():
        if first:
            assemble(first_ref, second_ref, w_ref, src_ref.shape[1])
            bias_along(first_ref, second_ref, left_ref, right_ref, u_ref, src_ref.shape[1])
        for start in range(0, src_ref.shape[0], CHUNK):
            at = slice(start, start + CHUNK)
            v = src_ref[at, :].astype(F32)
            normed_ref[at, :] = (v * rms_rows(v) * gains_ref[:1, :]).astype(BF16)

    at = pl.multiple_of(step * 3 * PAIR, 3 * PAIR)
    packed = dot_nt(normed_ref[...], w_ref[pl.ds(at, 3 * PAIR), :])
    lane = lax.broadcasted_iota(jnp.int32, (seq, PAIR), 1)
    scale = 1.0 / math.sqrt(HD)
    packed_ref[:, :PAIR] = (packed[:, :PAIR].astype(BF16).astype(F32) * scale).astype(BF16)
    packed_ref[:, PAIR:] = packed[:, PAIR:].astype(BF16)
    key_pos = lax.broadcasted_iota(jnp.int32, (seq, 1), 0)
    length = len_ref[lax.axis_index("core") * docs + doc]
    for head in range(2):
        row = jnp.broadcast_to(u_ref[pl.ds(2 * step + head, 1), :], (seq, 2 * seq))
        rel = pltpu.roll(row, 0, 1, stride=1, stride_axis=0)[:, :seq]
        mine = (lane >= HD) if head else (lane < HD)
        q = packed_ref[:, :PAIR]
        k = packed_ref[:, PAIR : 2 * PAIR]
        v = packed_ref[:, 2 * PAIR :]
        k = jnp.where(mine, k, jnp.zeros_like(k))
        scores = dot_nt(k, q) + rel
        scores = jnp.where(key_pos < length, scores, MASKED)
        top = jnp.max(scores, axis=0, keepdims=True)
        e = jnp.exp(scores - top)
        total = jnp.sum(e, axis=0, keepdims=True)
        p = (e * (1.0 / total)).astype(BF16)
        probs_ref[head] = p
        vt = v.T[head * HD : (head + 1) * HD, :]
        o = dot_nn(vt, p)
        att_ref[:, head * HD : (head + 1) * HD] = o.T.astype(BF16)


def attn_fwd(ids, lengths, inputs, gains, weights, buckets, doc, docs):
    seq = buckets.shape[0]
    width = inputs.shape[1]
    pairs = width // (4 * HD)
    first = doc == 0
    specs = [pl.BlockSpec(memory_space=pltpu.SMEM), doc_rows(seq, width, docs, doc), whole(gains.shape)]
    args = (lengths, inputs, gains) + tuple(weights)
    specs += [whole(w.shape) for w in weights]
    outs, out_specs = [], []
    if first:
        last = seq // PAIR - 1
        args += (buckets, buckets)
        specs += [
            pl.BlockSpec((seq, PAIR), lambda p: (0, 0)),
            pl.BlockSpec((seq, PAIR), lambda p: (0, last)),
        ]
        outs = [shape_of((pairs * 3 * PAIR, width), BF16), shape_of((2 * pairs, 2 * seq), F32)]
        out_specs = [whole(o.shape) for o in outs]
    outs += [
        shape_of((seq, width), BF16),
        shape_of((seq, pairs * 3 * PAIR), BF16),
        shape_of((2 * pairs, seq, seq), BF16),
        shape_of((seq, pairs * PAIR), BF16),
    ]
    out_specs += [
        whole((seq, width)),
        pl.BlockSpec((seq, 3 * PAIR), lambda p: (0, p)),
        pl.BlockSpec((2, seq, seq), lambda p: (p, 0, 0)),
        pl.BlockSpec((seq, PAIR), lambda p: (0, p)),
    ]
    return call(
        functools.partial(attn_fwd_kernel, first, doc, docs, seq),
        "attn_fwd",
        ids,
        args,
        specs,
        outs,
        out_specs,
        grid=(pairs,),
    )


TILE = 256


def ffn_kernel(first, *refs):
    (
        src_ref, att_own_ref, att_oth_ref, wo_a_ref, wo_b_ref, wo_x_ref, wo_xc_ref, gains_ref, cot_ref,
        in_a_ref, in_b_ref, back_a_ref, back_b_ref, *refs,
    ) = refs
    if not first:
        gback_a_in, gback_b_in, gin_a_in, gin_b_in, *refs = refs
    (
        middle_ref, gsend_ref, hsend_ref, gback_a_ref, gback_b_ref, gin_a_ref, gin_b_ref,
        normed_ref, normed_t_ref, acc_ref, gacc_ref,
    ) = refs
    rows = src_ref.shape[0]
    step = pl.program_id(0)
    half = pl.num_programs(0) // 2

    @pl.when(step == 0)
    def _():
        swapped = lax.axis_index("x") != 0
        wo_own = jnp.concatenate([wo_a_ref[...], wo_b_ref[...]], axis=0)
        wo_oth = jnp.concatenate([wo_x_ref[...], wo_xc_ref[...]], axis=0)
        wo_0 = jnp.where(swapped, wo_oth, wo_own)
        wo_1 = jnp.where(swapped, wo_own, wo_oth)
        for start in range(0, rows, CHUNK):
            at = slice(start, start + CHUNK)
            own, oth = att_own_ref[at, :], att_oth_ref[at, :]
            terms = dot_nn(jnp.where(swapped, oth, own), wo_0) + dot_nn(jnp.where(swapped, own, oth), wo_1)
            m = src_ref[at, :].astype(F32) + terms
            middle_ref[at, :] = m
            normed = (m * rms_rows(m) * gains_ref[1:, :]).astype(BF16)
            normed_ref[at, :] = normed
            normed_t_ref[:, at] = normed.T
        acc_ref[...] = jnp.zeros(acc_ref.shape, F32)
        gacc_ref[...] = jnp.zeros(gacc_ref.shape, F32)

    mine = step < half
    w_in = jnp.where(mine, in_a_ref[...], in_b_ref[...])
    w_back = jnp.where(mine, back_a_ref[...], back_b_ref[...])
    hiddens, gpres = [], []
    for start in range(0, rows, 2 * CHUNK):
        at = slice(start, start + 2 * CHUNK)
        pre = dot_nn(normed_ref[at, :], w_in)
        ghid = dot_nt(cot_ref[at, :], w_back)
        sq = pre * pre
        t = jnp.tanh(pre * (GELU_C + (GELU_C * GELU_A) * sq))
        half_t = 0.5 + 0.5 * t
        act = pre * half_t
        hidden = act.astype(BF16)
        slope = half_t + (act * (1.0 - t)) * (GELU_C + (3.0 * GELU_C * GELU_A) * sq)
        gpre = (ghid * slope).astype(BF16)
        acc_ref[at, :] += dot_nn(hidden, w_back)
        gacc_ref[at, :] += dot_nt(gpre, w_in)
        hiddens.append(hidden)
        gpres.append(gpre)
    gback = dot_tn(jnp.concatenate(hiddens, axis=0), cot_ref[...])
    gin = dot_nn(normed_t_ref[...], jnp.concatenate(gpres, axis=0))

    @pl.when(mine)
    def _():
        if first:
            gback_a_ref[...] = gback.astype(BF16)
            gin_a_ref[...] = gin.astype(BF16)
        else:
            gback_a_ref[...] = (gback + gback_a_in[...].astype(F32)).astype(BF16)
            gin_a_ref[...] = (gin + gin_a_in[...].astype(F32)).astype(BF16)

    @pl.when(jnp.logical_not(mine))
    def _():
        if first:
            gback_b_ref[...] = gback.astype(BF16)
            gin_b_ref[...] = gin.astype(BF16)
        else:
            gback_b_ref[...] = (gback + gback_b_in[...].astype(F32)).astype(BF16)
            gin_b_ref[...] = (gin + gin_b_in[...].astype(F32)).astype(BF16)

    @pl.when(step == 2 * half - 1)
    def _():
        hsend_ref[...] = acc_ref[...].astype(BF16)
        gsend_ref[...] = gacc_ref[...].astype(BF16)


def ffn(ids, inputs, att_own, att_oth, wos, gains, cotangent, w_ins, w_backs, grads, doc, docs):
    seq = att_own.shape[0]
    width = inputs.shape[1]
    units = w_ins[0].shape[1]
    tiles = units // TILE
    mine = doc_rows(seq, width, docs, doc)

    def first_half(i):
        return jnp.minimum(i, tiles - 1)

    def second_half(i):
        return jnp.maximum(i - tiles, 0)

    def back_spec(of):
        return pl.BlockSpec((TILE, width), lambda i: (of(i), 0))

    def in_spec(of):
        return pl.BlockSpec((width, TILE), lambda i: (0, of(i)))

    grad_specs = [back_spec(first_half), back_spec(second_half), in_spec(first_half), in_spec(second_half)]
    outs = [
        shape_of((seq, width), F32),
        shape_of((seq, width), BF16),
        shape_of((seq, width), BF16),
        shape_of((units, width), BF16),
        shape_of((units, width), BF16),
        shape_of((width, units), BF16),
        shape_of((width, units), BF16),
    ]
    return call(
        functools.partial(ffn_kernel, grads is None),
        "ffn",
        ids,
        (inputs, att_own, att_oth) + wos + (gains, cotangent) + w_ins + w_backs + tuple(grads or ()),
        [mine, whole(att_own.shape), whole(att_oth.shape)]
        + [whole(w.shape) for w in wos]
        + [whole(gains.shape), mine]
        + [in_spec(first_half), in_spec(second_half), back_spec(first_half), back_spec(second_half)]
        + (grad_specs if grads else []),
        outs,
        [whole(o.shape) for o in outs[:3]] + grad_specs,
        grid=(2 * tiles,),
        vmem=56 * 1024 * 1024,
        scratch=[
            pltpu.VMEM((seq, width), BF16),
            pltpu.VMEM((width, seq), BF16),
            pltpu.VMEM((seq, width), F32),
            pltpu.VMEM((seq, width), F32),
        ],
    )


def fold_diagonals(g, seq):
    g = jnp.concatenate([g, jnp.zeros_like(g)], axis=1)
    n = seq
    while n > 8:
        n //= 2
        g = g[:n] + pltpu.roll(g[n:], 2 * seq - n, 1)
    while n > 1:
        n //= 2
        g = g[:n] + jnp.concatenate([g[n:, n:], g[n:, :n]], axis=1)
    return g


def attn_bwd_kernel(
    seq, middle_ref, gown_ref, goth_ref, gains_ref, cot_ref, wo_a_ref, wo_b_ref, w_ref, packed_ref, probs_ref,
    gmid_ref, low_ref, ggain_ref, gp_ref, nsend_ref, diag_ref, dout_ref, acc_ref,
):
    step = pl.program_id(0)
    pairs = pl.num_programs(0)

    @pl.when(step == 0)
    def _():
        wo_own = jnp.concatenate([wo_a_ref[...], wo_b_ref[...]], axis=0)
        ggain = jnp.zeros(ggain_ref.shape, F32)
        for start in range(0, seq, CHUNK):
            at = slice(start, start + CHUNK)
            m = middle_ref[at, :]
            gnorm = gown_ref[at, :].astype(F32) + goth_ref[at, :].astype(F32)
            r = rms_rows(m)
            ggain = ggain + jnp.sum(gnorm * m * r, axis=0, keepdims=True)
            back = gains_ref[1:, :] * gnorm
            inner = jnp.mean(back * m, axis=-1, keepdims=True)
            gm = cot_ref[at, :].astype(F32) + r * back - m * (r * r * r * inner)
            gmid_ref[at, :] = gm
            low = gm.astype(BF16)
            low_ref[at, :] = low
            dout = dot_nt(low, wo_own).astype(BF16)
            for p in range(dout_ref.shape[0]):
                dout_ref[p, at, :] = dout[:, p * PAIR : (p + 1) * PAIR]
        ggain_ref[...] = ggain

    lane = lax.broadcasted_iota(jnp.int32, (seq, PAIR), 1)
    scale = 1.0 / math.sqrt(HD)
    q = packed_ref[:, :PAIR]
    k = packed_ref[:, PAIR : 2 * PAIR]
    v = packed_ref[:, 2 * PAIR :]
    do = dout_ref[step]
    kt = k.T
    dqs, dks, dvs = [], [], []
    for head in range(2):
        mine = (lane >= HD) if head else (lane < HD)
        vm = jnp.where(mine, v, jnp.zeros_like(v))
        dp = dot_nt(vm, do)
        p_low = probs_ref[head]
        p = p_low.astype(F32)
        mean = jnp.sum(dp * p, axis=0, keepdims=True)
        ds = (p * (dp - mean)).astype(BF16)
        diag_ref[0, head : head + 1, :] = fold_diagonals(ds.astype(F32), seq)
        dvs.append(dot_nn(p_low, do))
        dks.append(dot_nn(ds, q))
        dqs.append(dot_nn(kt[head * HD : (head + 1) * HD, :], ds))
    dq = jnp.concatenate(dqs, axis=0).T * scale
    first = lane < HD
    gp_ref[:, :PAIR] = dq.astype(BF16)
    gp_ref[:, PAIR : 2 * PAIR] = jnp.where(first, dks[0], dks[1]).astype(BF16)
    gp_ref[:, 2 * PAIR :] = jnp.where(first, dvs[0], dvs[1]).astype(BF16)
    terms = dot_nn(gp_ref[...], w_ref[...])

    @pl.when(step == 0)
    def _():
        acc_ref[...] = terms

    @pl.when(step != 0)
    def _():
        acc_ref[...] += terms

    @pl.when(step == pairs - 1)
    def _():
        nsend_ref[...] = acc_ref[...].astype(BF16)


def attn_bwd(ids, middle, gown, goth, gains, cotangent, wo_a, wo_b, w_own, packed, probs, doc, docs):
    seq, width = middle.shape
    pairs = packed.shape[1] // (3 * PAIR)
    mine = doc_rows(seq, width, docs, doc)
    outs = [
        shape_of((seq, width), F32),
        shape_of((seq, width), BF16),
        shape_of((1, width), F32),
        shape_of(packed.shape, BF16),
        shape_of((seq, width), BF16),
        shape_of((pairs, 2, 2 * seq), F32),
    ]
    return call(
        functools.partial(attn_bwd_kernel, seq),
        "attn_bwd",
        ids,
        (middle, gown, goth, gains, cotangent, wo_a, wo_b, w_own, packed, probs),
        [whole(middle.shape), whole(gown.shape), whole(goth.shape), whole(gains.shape), mine]
        + [whole(wo_a.shape), whole(wo_b.shape)]
        + [
            pl.BlockSpec((3 * PAIR, width), lambda p: (p, 0)),
            pl.BlockSpec((seq, 3 * PAIR), lambda p: (0, p)),
            pl.BlockSpec((2, seq, seq), lambda p: (p, 0, 0)),
        ],
        outs,
        [
            whole((seq, width)),
            whole((seq, width)),
            whole((1, width)),
            pl.BlockSpec((seq, 3 * PAIR), lambda p: (0, p)),
            whole((seq, width)),
            pl.BlockSpec((1, 2, 2 * seq), lambda p: (p, 0, 0)),
        ],
        grid=(pairs,),
        scratch=[pltpu.VMEM((pairs, seq, PAIR), BF16), pltpu.VMEM((seq, width), F32)],
    )


def grad_attn_kernel(docs, pairs, *refs):
    groups = [refs[i * docs : (i + 1) * docs] for i in range(4)]
    mine_ref, other_ref = refs[4 * docs :]
    normed, gp, low, att = (jnp.concatenate([r[...] for r in g], axis=0) for g in groups)
    step = pl.program_id(0)
    cols = mine_ref.shape[0] // 4
    heads = cols // HD
    grads = dot_tn(gp, normed).astype(BF16)
    outer = dot_tn(att, low).astype(BF16)
    for p in range(pairs):

        @pl.when(step == p)
        def _(p=p):
            for i in range(2):
                head = 2 * p + i
                ref = mine_ref if head < heads else other_ref
                at = (head % heads) * HD
                for part in range(3):
                    piece = grads[part * PAIR + i * HD : part * PAIR + (i + 1) * HD, :]
                    ref[part * cols + at : part * cols + at + HD, :] = piece
                ref[3 * cols + at : 3 * cols + at + HD, :] = outer[i * HD : (i + 1) * HD, :]


def grad_attn(ids, normeds, gps, lows, atts, docs):
    seq, width = normeds[0].shape
    pairs = atts[0].shape[1] // PAIR
    outs = [shape_of((width, width), BF16)] * 2
    return call(
        functools.partial(grad_attn_kernel, docs, pairs),
        "grad_attn",
        ids,
        tuple(normeds) + tuple(gps) + tuple(lows) + tuple(atts),
        [whole((seq, width))] * docs
        + [pl.BlockSpec((seq, 3 * PAIR), lambda p: (0, p))] * docs
        + [whole((seq, width))] * docs
        + [pl.BlockSpec((seq, PAIR), lambda p: (0, p))] * docs,
        outs,
        [whole((width, width))] * 2,
        grid=(pairs,),
    )


def grad_input_kernel(docs, src_ref, gains_ref, *refs):
    gmid_refs, own_refs, oth_refs = (refs[i * docs : (i + 1) * docs] for i in range(3))
    full_ref, send_ref, ggain_ref = refs[3 * docs :]
    seq = gmid_refs[0].shape[0]
    ggain = jnp.zeros(ggain_ref.shape, F32)
    for doc in range(docs):
        for start in range(0, seq, CHUNK):
            here = slice(start, start + CHUNK)
            at = slice(doc * seq + start, doc * seq + start + CHUNK)
            gnorm = own_refs[doc][here, :].astype(F32) + oth_refs[doc][here, :].astype(F32)
            v = src_ref[at, :].astype(F32)
            r = rms_rows(v)
            ggain = ggain + jnp.sum(gnorm * v * r, axis=0, keepdims=True)
            back = gains_ref[:1, :] * gnorm
            inner = jnp.mean(back * v, axis=-1, keepdims=True)
            out = gmid_refs[doc][here, :] + r * back - v * (r * r * r * inner)
            full_ref[at, :] = out
            send_ref[at, :] = out
    ggain_ref[...] = ggain


def grad_input(ids, inputs, gains, gmids, owns, oths, docs):
    seq, width = gmids[0].shape
    rows = docs * seq
    mine = pl.BlockSpec((rows, width), lambda i: (lax.axis_index("core"), 0))
    return call(
        functools.partial(grad_input_kernel, docs),
        "grad_input",
        ids,
        (inputs, gains) + tuple(gmids) + tuple(owns) + tuple(oths),
        [mine, whole(gains.shape)] + [whole((seq, width))] * (3 * docs),
        [shape_of((2 * rows, width), F32), shape_of((rows, width), F32), shape_of((1, width), F32)],
        [mine, whole((rows, width)), whole((1, width))],
    )


def mix_kernel(docs, *refs):
    middle_refs, own_refs, oth_refs = (refs[i * docs : (i + 1) * docs] for i in range(3))
    full_ref, send_ref = refs[3 * docs :]
    seq = middle_refs[0].shape[0]
    for doc in range(docs):
        at = slice(doc * seq, (doc + 1) * seq)
        terms = own_refs[doc][...].astype(F32) + oth_refs[doc][...].astype(F32)
        out = (middle_refs[doc][...] + terms).astype(BF16)
        full_ref[at, :] = out
        send_ref[at, :] = out


def mix(ids, middles, owns, oths, docs):
    seq, width = middles[0].shape
    rows = docs * seq
    return call(
        functools.partial(mix_kernel, docs),
        "mix",
        ids,
        tuple(middles) + tuple(owns) + tuple(oths),
        [whole((seq, width))] * (3 * docs),
        [shape_of((2 * rows, width), BF16), shape_of((rows, width), BF16)],
        [pl.BlockSpec((rows, width), lambda i: (lax.axis_index("core"), 0)), whole((rows, width))],
    )


def place_kernel(full_ref, got_ref, out_ref):
    out_ref[...] = got_ref[...]


def place(ids, full, got):
    rows, width = got.shape
    steps = 4
    part = rows // steps
    return call(
        place_kernel,
        "place",
        ids,
        (full, got),
        [pl.BlockSpec(memory_space=pl.ANY), pl.BlockSpec((part, width), lambda i: (i, 0))],
        [shape_of(full.shape, full.dtype)],
        [pl.BlockSpec((part, width), lambda i: ((1 - lax.axis_index("core")) * steps + i, 0))],
        grid=(steps,),
        aliases={1: 1},
    )


def gate(ids, *arrays):
    anywhere = [pl.BlockSpec(memory_space=pl.ANY)] * len(arrays)
    shapes = [shape_of(v.shape, v.dtype) for v in arrays]
    aliases = {i + 1: i + 1 for i in range(len(arrays))}
    return call(lambda *refs: None, "gate", ids, arrays, anywhere, shapes, anywhere, aliases=aliases)


def need(ids, *arrays):
    anywhere = pl.BlockSpec(memory_space=pl.ANY)
    return call(lambda *refs: None, "need", ids, arrays, [anywhere] * len(arrays), [], [])[1]


def sum_core_kernel(*refs):
    for i, out_ref in enumerate(refs[2 * len(refs) // 3 :]):
        out_ref[...] = (refs[2 * i][...].astype(F32) + refs[2 * i + 1][...].astype(F32)).astype(BF16)


def sum_core(ids, *arrays):
    steps = 2
    specs = [pl.BlockSpec((v.shape[0] // steps, v.shape[1]), lambda i: (i, 0)) for v in arrays]
    outs = [shape_of(v.shape, BF16) for v in arrays[::2]]
    return call(sum_core_kernel, "sum_core", ids, arrays, specs, outs, specs[::2], grid=(steps,))


def widen_kernel(*refs):
    half = len(refs) // 2
    for src, dst in zip(refs[:half], refs[half:]):
        dst[...] = src[...].astype(F32)


def widen_attn(ids, total):
    steps = 4
    width = total.shape[1]
    part = total.shape[0] // (4 * steps)
    specs = [
        pl.BlockSpec((3 * part, width), lambda i: (i, 0)),
        pl.BlockSpec((part, width), lambda i: (3 * steps + i, 0)),
    ]
    return call(
        widen_kernel,
        "widen_attn",
        ids,
        (total, total),
        specs,
        [shape_of((12 * part, width), F32), shape_of((4 * part, width), F32)],
        [pl.BlockSpec((n * part, width), lambda i: (i, 0)) for n in (3, 1)],
        grid=(steps,),
    )


def widen(ids, *arrays):
    steps = 4
    specs = [pl.BlockSpec((v.shape[0] // steps, v.shape[1]), lambda i: (i, 0)) for v in arrays]
    return call(
        widen_kernel, "widen", ids, arrays, specs, [shape_of(v.shape, F32) for v in arrays], specs, grid=(steps,)
    )


def sum_kernel(got_ref, out_ref):
    rows = out_ref.shape[0]
    parts = got_ref.shape[0] // rows
    total = got_ref[:rows, :].astype(F32)
    for i in range(1, parts):
        total = total + got_ref[i * rows : (i + 1) * rows, :].astype(F32)
    out_ref[...] = total.astype(BF16)


def sum_parts(token, got, dp):
    width = got.shape[1]
    rows = got.shape[0] // dp
    if rows % 16:
        total = jnp.sum(got.reshape(dp, rows, width).astype(F32), axis=0).astype(BF16)
        return [jnp.tile(total, (dp, 1))], token
    return call(
        sum_kernel,
        "sum_parts",
        token,
        (got,),
        [whole(got.shape)],
        [shape_of((dp * rows, width), BF16)],
        [pl.BlockSpec((rows, width), lambda i: (i, 0))],
        grid=(dp,),
    )


def region(always, fn, ids):
    outs = jax.eval_shape(fn, ids)
    return lax.cond(always, fn, lambda _: jax.tree.map(lambda o: jnp.zeros(o.shape, o.dtype), outs), ids)


def per_device(dp, inputs, gain_attn, w_qkv, w_out, gain_ffn, w_in, w_back, bias_table, lengths, buckets, cotangent):
    width = inputs.shape[1]
    seq = buckets.shape[0]
    docs = lengths.shape[0] // 2
    table_rows, heads = bias_table.shape
    gains = jnp.stack([gain_attn, gain_ffn]).astype(F32)
    ids = jnp.zeros((8, 128), F32)

    def from_core(v):
        return lax.ppermute(v, "core", [(0, 1), (1, 0)])

    def from_x(v):
        return lax.ppermute(v, "x", [(0, 1), (1, 0)])

    def spread(v):
        return lax.all_to_all(v, "dp", 0, 0, tiled=True)

    bias = jnp.pad(bias_table.T, ((0, BIAS_ROWS - heads), (0, width - table_rows)))
    attn_w = jnp.concatenate([w_qkv.transpose(0, 2, 1).reshape(-1, width), bias], axis=0)
    attn_w = jnp.concatenate([attn_w[: 3 * width // 4], w_out, attn_w[3 * width // 4 :]], axis=0)
    attn_c = from_core(attn_w)
    wo_x = from_x(w_out)
    wo_c = from_core(w_out)
    in_c = from_core(w_in)
    back_c = from_core(w_back)

    every = range(docs)
    normed, packed, probs, att, att_x = [], [], [], [], []
    for doc in every:
        if doc == 0:
            (w_own, u, n, a, b, c), ids = attn_fwd(
                ids, lengths, inputs, gains, (attn_w, attn_c), buckets, doc, docs
            )
            (wo_x,), ids = gate(ids, wo_x)
            wo_xc = from_core(wo_x)
        else:
            (n, a, b, c), ids = attn_fwd(ids, lengths, inputs, gains, (w_own, u), buckets, doc, docs)
        normed.append(n)
        packed.append(a)
        probs.append(b)
        att.append(c)
        att_x.append(from_x(c))

    middle, gown, hown, goth, grads = [], [], [], [], None
    for doc in every:
        (m, g, h, *grads), ids = ffn(
            ids, inputs, att[doc], att_x[doc], (w_out, wo_c, wo_x, wo_xc), gains, cotangent,
            (w_in, in_c), (w_back, back_c), grads, doc, docs,
        )
        middle.append(m)
        hown.append(h)
        if doc + 1 < docs:
            ids = need(ids, att_x[doc + 1])
        (g,), ids = gate(ids, g)
        gown.append(g)
        goth.append(from_x(g))
    always = lengths[0] > 0

    def ffn_grads(ids):
        gback, gback_c, gin, gin_c = grads
        return sum_core(ids, gback, from_core(gback_c), gin, from_core(gin_c))[::-1]

    ids = need(ids, goth[0])
    ids, (gback, gin) = region(always, ffn_grads, ids)
    gback, gin = lax.psum((gback, gin), "dp")

    def back_of(doc, ids):
        res, ids = attn_bwd(
            ids, middle[doc], gown[doc], goth[doc], gains, cotangent, w_out, wo_c, w_own, packed[doc], probs[doc],
            doc, docs,
        )
        return ids, res

    ids, first = back_of(0, ids)
    ids = need(ids, *goth[1:])

    def attention_back(ids):
        (nown_0,), ids = gate(ids, first[4])
        noth = [from_x(nown_0)]

        def others(ids):
            results = [first]
            for doc in range(1, docs):
                ids, res = back_of(doc, ids)
                results.append(res)
            gp, low = [r[3] for r in results], [r[1] for r in results]
            (gattn, gattn_c), ids = grad_attn(ids, normed, gp, low, att, docs)
            return ids, results[1:], gattn, gattn_c

        ids, results, gattn, gattn_c = region(always, others, ids)
        gmid, low, ggain_two, gp, nown, diag = zip(first, *results)
        ids = need(ids, noth[0])
        (gattn_c,), ids = gate(ids, gattn_c)
        (gattn,), ids = sum_core(ids, gattn, from_core(gattn_c))
        gattn = spread(gattn)

        def rows_back(ids):
            mine, got = [nown_0] + list(nown[1:]), list(noth)
            for doc in range(1, docs):
                (mine[doc],), ids = gate(ids, mine[doc])
                got.append(from_x(mine[doc]))
            sent, hoth = list(hown), []
            for doc in range(docs // 2):
                (sent[doc],), ids = gate(ids, sent[doc])
                hoth.append(from_x(sent[doc]))
            (gsrc, gsrc_send, ggain_one), ids = grad_input(ids, inputs, gains, gmid, mine, got, docs)
            diag_bucket = jnp.concatenate([buckets[:, 0], buckets[:1, -1], buckets[:-1, -1]])
            one_hot = (diag_bucket[:, None] == jnp.arange(table_rows)[None, :]).astype(F32)
            diags = sum(diag).reshape(2 * heads, 2 * seq)
            table = lax.dot_general(
                diags, one_hot, (((1,), (0,)), ((), ())), precision=lax.Precision.HIGHEST, preferred_element_type=F32
            )
            ggain_ffn = sum(ggain_two)
            small = jnp.concatenate([ggain_one.reshape(-1), ggain_ffn.reshape(-1), table[:heads].reshape(-1)])
            small_send = jnp.concatenate([ggain_one.reshape(-1), ggain_ffn.reshape(-1), table[heads:].reshape(-1)])
            small = small + from_core(small_send)
            for s in range(dp.bit_length() - 1):
                small = small + lax.ppermute(small, "dp", [(i, i ^ (1 << s)) for i in range(dp)])
            grad_gain_attn, grad_gain_ffn = small[:width], small[width : 2 * width]
            grad_table = small[2 * width :].reshape(heads, table_rows).T
            ids = need(ids, grad_gain_attn, grad_gain_ffn, grad_table)
            gsrc_got = from_core(gsrc_send)
            ids = need(ids, gsrc_got, *hoth)
            return ids, gsrc, gsrc_got, (grad_gain_attn, grad_gain_ffn, grad_table), sent, hoth

        ids, gsrc, gsrc_got, smalls, hsent, hoth = region(always, rows_back, ids)
        (gattn,), ids = sum_parts(ids, gattn, dp)
        return ids, gattn, gsrc, gsrc_got, smalls, hsent, hoth

    ids, gattn, gsrc, gsrc_got, smalls, hsent, hoth = region(always, attention_back, ids)
    grad_gain_attn, grad_gain_ffn, grad_table = smalls
    for doc in range(docs // 2, docs):
        (hsent[doc],), ids = gate(ids, hsent[doc])
        hoth.append(from_x(hsent[doc]))
    gattn = spread(gattn)
    (gsrc,), ids = place(ids, gsrc, gsrc_got)
    (grad_w_back, grad_w_in), ids = widen(ids, gback, gin)
    (mixed, mixed_send), ids = mix(ids, middle, hsent, hoth, docs)
    mixed_got = from_core(mixed_send)
    (mixed,), ids = place(ids, mixed, mixed_got)
    (grad_w_qkv, grad_w_out), ids = widen_attn(ids, gattn)
    grad_w_qkv = grad_w_qkv.reshape(3, width // 4, width).transpose(0, 2, 1)
    return (
        mixed,
        gsrc,
        grad_gain_attn,
        grad_w_qkv,
        grad_w_out,
        grad_gain_ffn,
        grad_w_in,
        grad_w_back,
        grad_table,
    )


def solution(mesh):
    dp = mesh.shape["dp"]
    devices = mesh.devices.reshape(mesh.shape["tensor"] // 2, 2, dp)
    mesh = jax.sharding.Mesh(devices, ("x", "core", "dp"))
    return jax.shard_map(
        functools.partial(per_device, dp),
        mesh=mesh,
        in_specs=(
            P("dp", None),
            P(),
            P(None, None, ("x", "core")),
            P(("x", "core"), None),
            P(),
            P(None, ("x", "core")),
            P(("x", "core"), None),
            P(None, ("x", "core")),
            P("dp"),
            P(),
            P("dp", None),
        ),
        out_specs=(
            P("dp", None),
            P("dp", None),
            P(),
            P(None, None, ("x", "core")),
            P(("x", "core"), None),
            P(),
            P(None, ("x", "core")),
            P(("x", "core"), None),
            P(None, ("x", "core")),
        ),
        check_vma=False,
    )
```

```python
import functools
import math

import jax
import jax.numpy as jnp
from jax import lax
from jax.experimental import pallas as pl
from jax.experimental.pallas import tpu as pltpu
from jax.sharding import PartitionSpec as P

HD = 64
PAIR = 2 * HD
EPS = 1e-06
MASKED = -1000000000.0
GELU_C = 0.7978845608028654
GELU_A = 0.044715
CHUNK = 256
VMEM_BYTES = 18 * 1024 * 1024

F32 = jnp.float32
BF16 = jnp.bfloat16


def dot_nn(a, b):
    return lax.dot_general(a, b, (((1,), (0,)), ((), ())), preferred_element_type=F32)


def dot_nt(a, b):
    return lax.dot_general(a, b, (((1,), (1,)), ((), ())), preferred_element_type=F32)


def dot_tn(a, b):
    return lax.dot_general(a, b, (((0,), (0,)), ((), ())), preferred_element_type=F32)


def whole(shape):
    return pl.BlockSpec(shape, lambda *_: (0,) * len(shape))


def shape_of(shape, dtype):
    return jax.ShapeDtypeStruct(shape, dtype)


def call(kernel, name, token, args, in_specs, outs, out_specs, grid=(1,), scratch=(), aliases=None, vmem=VMEM_BYTES):
    n_in, n_out = len(args), len(outs)

    def body(token_ref, *refs):
        del token_ref
        kernel(*refs[:n_in], *refs[n_in + 1 :])

    anywhere = pl.BlockSpec(memory_space=pl.ANY)
    res = pl.pallas_call(
        body,
        grid=grid,
        in_specs=[anywhere] + list(in_specs),
        out_specs=[anywhere] + list(out_specs),
        scratch_shapes=list(scratch),
        out_shape=[shape_of(token.shape, token.dtype)] + list(outs),
        input_output_aliases={0: 0, **(aliases or {})},
        compiler_params=pltpu.CompilerParams(vmem_limit_bytes=vmem),
        name=name,
    )(token, *args)
    return res[1:], res[0]


def rms_rows(v):
    return lax.rsqrt(jnp.mean(v * v, axis=-1, keepdims=True) + EPS)


def doc_rows(seq, width, docs, doc):
    return pl.BlockSpec((seq, width), lambda i: (lax.axis_index("core") * docs + doc, 0))


BIAS_ROWS = 16


def assemble(first_ref, second_ref, w_ref, width):
    cols = width // 4
    heads = cols // HD
    sources = [(first_ref, h) for h in range(heads)] + [(second_ref, h) for h in range(heads)]
    for p in range(heads):
        for part in range(3):
            for i in range(2):
                ref, head = sources[2 * p + i]
                src = part * cols + head * HD
                dst = (3 * p + part) * PAIR + i * HD
                w_ref[dst : dst + HD, :] = ref[src : src + HD, :]


def bias_along(first_ref, second_ref, left_ref, right_ref, u_ref, width):
    seq = left_ref.shape[0]
    left = left_ref[...].astype(F32).T[:1, :]
    right = right_ref[...].astype(F32).T[PAIR - 1 :, :]
    bucket = jnp.concatenate([left, pltpu.roll(right, 1, 1)], axis=1)
    index = lax.broadcasted_iota(jnp.int32, (PAIR, 2 * seq), 0).astype(F32)
    one_hot = (index == bucket).astype(BF16)
    heads = width // 4 // HD
    for at, ref in ((0, first_ref), (heads, second_ref)):
        u = dot_nn(ref[width:, :PAIR], one_hot)
        u_ref[at : at + heads, :] = u[:heads]


def attn_fwd_kernel(
    first, doc, docs, seq, len_ref, src_ref, gains_ref, *refs
):
    step = pl.program_id(0)
    if first:
        first_ref, second_ref, left_ref, right_ref, w_ref, u_ref, *refs = refs
    else:
        w_ref, u_ref, *refs = refs
    normed_ref, packed_ref, probs_ref, att_ref = refs

    @pl.when(step == 0)
    def _():
        if first:
            assemble(first_ref, second_ref, w_ref, src_ref.shape[1])
            bias_along(first_ref, second_ref, left_ref, right_ref, u_ref, src_ref.shape[1])
        for start in range(0, src_ref.shape[0], CHUNK):
            at = slice(start, start + CHUNK)
            v = src_ref[at, :].astype(F32)
            normed_ref[at, :] = (v * rms_rows(v) * gains_ref[:1, :]).astype(BF16)

    at = pl.multiple_of(step * 3 * PAIR, 3 * PAIR)
    packed = dot_nt(normed_ref[...], w_ref[pl.ds(at, 3 * PAIR), :])
    lane = lax.broadcasted_iota(jnp.int32, (seq, PAIR), 1)
    scale = 1.0 / math.sqrt(HD)
    packed_ref[:, :PAIR] = (packed[:, :PAIR].astype(BF16).astype(F32) * scale).astype(BF16)
    packed_ref[:, PAIR:] = packed[:, PAIR:].astype(BF16)
    key_pos = lax.broadcasted_iota(jnp.int32, (seq, 1), 0)
    length = len_ref[lax.axis_index("core") * docs + doc]
    for head in range(2):
        row = jnp.broadcast_to(u_ref[pl.ds(2 * step + head, 1), :], (seq, 2 * seq))
        rel = pltpu.roll(row, 0, 1, stride=1, stride_axis=0)[:, :seq]
        mine = (lane >= HD) if head else (lane < HD)
        q = packed_ref[:, :PAIR]
        k = packed_ref[:, PAIR : 2 * PAIR]
        v = packed_ref[:, 2 * PAIR :]
        k = jnp.where(mine, k, jnp.zeros_like(k))
        scores = dot_nt(k, q) + rel
        scores = jnp.where(key_pos < length, scores, MASKED)
        top = jnp.max(scores, axis=0, keepdims=True)
        e = jnp.exp(scores - top)
        total = jnp.sum(e, axis=0, keepdims=True)
        p = (e * (1.0 / total)).astype(BF16)
        probs_ref[head] = p
        vt = v.T[head * HD : (head + 1) * HD, :]
        o = dot_nn(vt, p)
        att_ref[:, head * HD : (head + 1) * HD] = o.T.astype(BF16)


def attn_fwd(ids, lengths, inputs, gains, weights, buckets, doc, docs):
    seq = buckets.shape[0]
    width = inputs.shape[1]
    pairs = width // (4 * HD)
    first = doc == 0
    specs = [pl.BlockSpec(memory_space=pltpu.SMEM), doc_rows(seq, width, docs, doc), whole(gains.shape)]
    args = (lengths, inputs, gains) + tuple(weights)
    specs += [whole(w.shape) for w in weights]
    outs, out_specs = [], []
    if first:
        last = seq // PAIR - 1
        args += (buckets, buckets)
        specs += [
            pl.BlockSpec((seq, PAIR), lambda p: (0, 0)),
            pl.BlockSpec((seq, PAIR), lambda p: (0, last)),
        ]
        outs = [shape_of((pairs * 3 * PAIR, width), BF16), shape_of((2 * pairs, 2 * seq), F32)]
        out_specs = [whole(o.shape) for o in outs]
    outs += [
        shape_of((seq, width), BF16),
        shape_of((seq, pairs * 3 * PAIR), BF16),
        shape_of((2 * pairs, seq, seq), BF16),
        shape_of((seq, pairs * PAIR), BF16),
    ]
    out_specs += [
        whole((seq, width)),
        pl.BlockSpec((seq, 3 * PAIR), lambda p: (0, p)),
        pl.BlockSpec((2, seq, seq), lambda p: (p, 0, 0)),
        pl.BlockSpec((seq, PAIR), lambda p: (0, p)),
    ]
    return call(
        functools.partial(attn_fwd_kernel, first, doc, docs, seq),
        "attn_fwd",
        ids,
        args,
        specs,
        outs,
        out_specs,
        grid=(pairs,),
    )


TILE = 256


def ffn_kernel(first, *refs):
    (
        src_ref, att_own_ref, att_oth_ref, wo_a_ref, wo_b_ref, wo_x_ref, wo_xc_ref, gains_ref, cot_ref,
        in_a_ref, in_b_ref, back_a_ref, back_b_ref, *refs,
    ) = refs
    if not first:
        gback_a_in, gback_b_in, gin_a_in, gin_b_in, *refs = refs
    (
        middle_ref, gsend_ref, hsend_ref, gback_a_ref, gback_b_ref, gin_a_ref, gin_b_ref,
        normed_ref, normed_t_ref, acc_ref, gacc_ref,
    ) = refs
    rows = src_ref.shape[0]
    step = pl.program_id(0)
    half = pl.num_programs(0) // 2

    @pl.when(step == 0)
    def _():
        swapped = lax.axis_index("x") != 0
        wo_own = jnp.concatenate([wo_a_ref[...], wo_b_ref[...]], axis=0)
        wo_oth = jnp.concatenate([wo_x_ref[...], wo_xc_ref[...]], axis=0)
        wo_0 = jnp.where(swapped, wo_oth, wo_own)
        wo_1 = jnp.where(swapped, wo_own, wo_oth)
        for start in range(0, rows, CHUNK):
            at = slice(start, start + CHUNK)
            own, oth = att_own_ref[at, :], att_oth_ref[at, :]
            terms = dot_nn(jnp.where(swapped, oth, own), wo_0) + dot_nn(jnp.where(swapped, own, oth), wo_1)
            m = src_ref[at, :].astype(F32) + terms
            middle_ref[at, :] = m
            normed = (m * rms_rows(m) * gains_ref[1:, :]).astype(BF16)
            normed_ref[at, :] = normed
            normed_t_ref[:, at] = normed.T
        acc_ref[...] = jnp.zeros(acc_ref.shape, F32)
        gacc_ref[...] = jnp.zeros(gacc_ref.shape, F32)

    mine = step < half
    w_in = jnp.where(mine, in_a_ref[...], in_b_ref[...])
    w_back = jnp.where(mine, back_a_ref[...], back_b_ref[...])
    hiddens, gpres = [], []
    for start in range(0, rows, 2 * CHUNK):
        at = slice(start, start + 2 * CHUNK)
        pre = dot_nn(normed_ref[at, :], w_in)
        ghid = dot_nt(cot_ref[at, :], w_back)
        sq = pre * pre
        t = jnp.tanh(pre * (GELU_C + (GELU_C * GELU_A) * sq))
        half_t = 0.5 + 0.5 * t
        act = pre * half_t
        hidden = act.astype(BF16)
        slope = half_t + (act * (1.0 - t)) * (GELU_C + (3.0 * GELU_C * GELU_A) * sq)
        gpre = (ghid * slope).astype(BF16)
        acc_ref[at, :] += dot_nn(hidden, w_back)
        gacc_ref[at, :] += dot_nt(gpre, w_in)
        hiddens.append(hidden)
        gpres.append(gpre)
    gback = dot_tn(jnp.concatenate(hiddens, axis=0), cot_ref[...])
    gin = dot_nn(normed_t_ref[...], jnp.concatenate(gpres, axis=0))

    @pl.when(mine)
    def _():
        if first:
            gback_a_ref[...] = gback.astype(BF16)
            gin_a_ref[...] = gin.astype(BF16)
        else:
            gback_a_ref[...] = (gback + gback_a_in[...].astype(F32)).astype(BF16)
            gin_a_ref[...] = (gin + gin_a_in[...].astype(F32)).astype(BF16)

    @pl.when(jnp.logical_not(mine))
    def _():
        if first:
            gback_b_ref[...] = gback.astype(BF16)
            gin_b_ref[...] = gin.astype(BF16)
        else:
            gback_b_ref[...] = (gback + gback_b_in[...].astype(F32)).astype(BF16)
            gin_b_ref[...] = (gin + gin_b_in[...].astype(F32)).astype(BF16)

    @pl.when(step == 2 * half - 1)
    def _():
        hsend_ref[...] = acc_ref[...].astype(BF16)
        gsend_ref[...] = gacc_ref[...].astype(BF16)


def ffn(ids, inputs, att_own, att_oth, wos, gains, cotangent, w_ins, w_backs, grads, doc, docs):
    seq = att_own.shape[0]
    width = inputs.shape[1]
    units = w_ins[0].shape[1]
    tiles = units // TILE
    mine = doc_rows(seq, width, docs, doc)

    def first_half(i):
        return jnp.minimum(i, tiles - 1)

    def second_half(i):
        return jnp.maximum(i - tiles, 0)

    def back_spec(of):
        return pl.BlockSpec((TILE, width), lambda i: (of(i), 0))

    def in_spec(of):
        return pl.BlockSpec((width, TILE), lambda i: (0, of(i)))

    grad_specs = [back_spec(first_half), back_spec(second_half), in_spec(first_half), in_spec(second_half)]
    outs = [
        shape_of((seq, width), F32),
        shape_of((seq, width), BF16),
        shape_of((seq, width), BF16),
        shape_of((units, width), BF16),
        shape_of((units, width), BF16),
        shape_of((width, units), BF16),
        shape_of((width, units), BF16),
    ]
    return call(
        functools.partial(ffn_kernel, grads is None),
        "ffn",
        ids,
        (inputs, att_own, att_oth) + wos + (gains, cotangent) + w_ins + w_backs + tuple(grads or ()),
        [mine, whole(att_own.shape), whole(att_oth.shape)]
        + [whole(w.shape) for w in wos]
        + [whole(gains.shape), mine]
        + [in_spec(first_half), in_spec(second_half), back_spec(first_half), back_spec(second_half)]
        + (grad_specs if grads else []),
        outs,
        [whole(o.shape) for o in outs[:3]] + grad_specs,
        grid=(2 * tiles,),
        vmem=56 * 1024 * 1024,
        scratch=[
            pltpu.VMEM((seq, width), BF16),
            pltpu.VMEM((width, seq), BF16),
            pltpu.VMEM((seq, width), F32),
            pltpu.VMEM((seq, width), F32),
        ],
    )


def fold_diagonals(g, seq):
    g = jnp.concatenate([g, jnp.zeros_like(g)], axis=1)
    n = seq
    while n > 8:
        n //= 2
        g = g[:n] + pltpu.roll(g[n:], 2 * seq - n, 1)
    while n > 1:
        n //= 2
        g = g[:n] + jnp.concatenate([g[n:, n:], g[n:, :n]], axis=1)
    return g


def attn_bwd_kernel(
    seq, middle_ref, gown_ref, goth_ref, gains_ref, cot_ref, wo_a_ref, wo_b_ref, w_ref, packed_ref, probs_ref,
    gmid_ref, low_ref, ggain_ref, gp_ref, nsend_ref, diag_ref, dout_ref, acc_ref,
):
    step = pl.program_id(0)
    pairs = pl.num_programs(0)

    @pl.when(step == 0)
    def _():
        wo_own = jnp.concatenate([wo_a_ref[...], wo_b_ref[...]], axis=0)
        ggain = jnp.zeros(ggain_ref.shape, F32)
        for start in range(0, seq, CHUNK):
            at = slice(start, start + CHUNK)
            m = middle_ref[at, :]
            gnorm = gown_ref[at, :].astype(F32) + goth_ref[at, :].astype(F32)
            r = rms_rows(m)
            ggain = ggain + jnp.sum(gnorm * m * r, axis=0, keepdims=True)
            back = gains_ref[1:, :] * gnorm
            inner = jnp.mean(back * m, axis=-1, keepdims=True)
            gm = cot_ref[at, :].astype(F32) + r * back - m * (r * r * r * inner)
            gmid_ref[at, :] = gm
            low = gm.astype(BF16)
            low_ref[at, :] = low
            dout = dot_nt(low, wo_own).astype(BF16)
            for p in range(dout_ref.shape[0]):
                dout_ref[p, at, :] = dout[:, p * PAIR : (p + 1) * PAIR]
        ggain_ref[...] = ggain

    lane = lax.broadcasted_iota(jnp.int32, (seq, PAIR), 1)
    scale = 1.0 / math.sqrt(HD)
    q = packed_ref[:, :PAIR]
    k = packed_ref[:, PAIR : 2 * PAIR]
    v = packed_ref[:, 2 * PAIR :]
    do = dout_ref[step]
    kt = k.T
    dqs, dks, dvs = [], [], []
    for head in range(2):
        mine = (lane >= HD) if head else (lane < HD)
        vm = jnp.where(mine, v, jnp.zeros_like(v))
        dp = dot_nt(vm, do)
        p_low = probs_ref[head]
        p = p_low.astype(F32)
        mean = jnp.sum(dp * p, axis=0, keepdims=True)
        ds = (p * (dp - mean)).astype(BF16)
        diag_ref[0, head : head + 1, :] = fold_diagonals(ds.astype(F32), seq)
        dvs.append(dot_nn(p_low, do))
        dks.append(dot_nn(ds, q))
        dqs.append(dot_nn(kt[head * HD : (head + 1) * HD, :], ds))
    dq = jnp.concatenate(dqs, axis=0).T * scale
    first = lane < HD
    gp_ref[:, :PAIR] = dq.astype(BF16)
    gp_ref[:, PAIR : 2 * PAIR] = jnp.where(first, dks[0], dks[1]).astype(BF16)
    gp_ref[:, 2 * PAIR :] = jnp.where(first, dvs[0], dvs[1]).astype(BF16)
    terms = dot_nn(gp_ref[...], w_ref[...])

    @pl.when(step == 0)
    def _():
        acc_ref[...] = terms

    @pl.when(step != 0)
    def _():
        acc_ref[...] += terms

    @pl.when(step == pairs - 1)
    def _():
        nsend_ref[...] = acc_ref[...].astype(BF16)


def attn_bwd(ids, middle, gown, goth, gains, cotangent, wo_a, wo_b, w_own, packed, probs, doc, docs):
    seq, width = middle.shape
    pairs = packed.shape[1] // (3 * PAIR)
    mine = doc_rows(seq, width, docs, doc)
    outs = [
        shape_of((seq, width), F32),
        shape_of((seq, width), BF16),
        shape_of((1, width), F32),
        shape_of(packed.shape, BF16),
        shape_of((seq, width), BF16),
        shape_of((pairs, 2, 2 * seq), F32),
    ]
    return call(
        functools.partial(attn_bwd_kernel, seq),
        "attn_bwd",
        ids,
        (middle, gown, goth, gains, cotangent, wo_a, wo_b, w_own, packed, probs),
        [whole(middle.shape), whole(gown.shape), whole(goth.shape), whole(gains.shape), mine]
        + [whole(wo_a.shape), whole(wo_b.shape)]
        + [
            pl.BlockSpec((3 * PAIR, width), lambda p: (p, 0)),
            pl.BlockSpec((seq, 3 * PAIR), lambda p: (0, p)),
            pl.BlockSpec((2, seq, seq), lambda p: (p, 0, 0)),
        ],
        outs,
        [
            whole((seq, width)),
            whole((seq, width)),
            whole((1, width)),
            pl.BlockSpec((seq, 3 * PAIR), lambda p: (0, p)),
            whole((seq, width)),
            pl.BlockSpec((1, 2, 2 * seq), lambda p: (p, 0, 0)),
        ],
        grid=(pairs,),
        scratch=[pltpu.VMEM((pairs, seq, PAIR), BF16), pltpu.VMEM((seq, width), F32)],
    )


def grad_attn_kernel(docs, pairs, *refs):
    groups = [refs[i * docs : (i + 1) * docs] for i in range(4)]
    mine_ref, other_ref = refs[4 * docs :]
    normed, gp, low, att = (jnp.concatenate([r[...] for r in g], axis=0) for g in groups)
    step = pl.program_id(0)
    cols = mine_ref.shape[0] // 4
    heads = cols // HD
    grads = dot_tn(gp, normed).astype(BF16)
    outer = dot_tn(att, low).astype(BF16)
    for p in range(pairs):

        @pl.when(step == p)
        def _(p=p):
            for i in range(2):
                head = 2 * p + i
                ref = mine_ref if head < heads else other_ref
                at = (head % heads) * HD
                for part in range(3):
                    piece = grads[part * PAIR + i * HD : part * PAIR + (i + 1) * HD, :]
                    ref[part * cols + at : part * cols + at + HD, :] = piece
                ref[3 * cols + at : 3 * cols + at + HD, :] = outer[i * HD : (i + 1) * HD, :]


def grad_attn(ids, normeds, gps, lows, atts, docs):
    seq, width = normeds[0].shape
    pairs = atts[0].shape[1] // PAIR
    outs = [shape_of((width, width), BF16)] * 2
    return call(
        functools.partial(grad_attn_kernel, docs, pairs),
        "grad_attn",
        ids,
        tuple(normeds) + tuple(gps) + tuple(lows) + tuple(atts),
        [whole((seq, width))] * docs
        + [pl.BlockSpec((seq, 3 * PAIR), lambda p: (0, p))] * docs
        + [whole((seq, width))] * docs
        + [pl.BlockSpec((seq, PAIR), lambda p: (0, p))] * docs,
        outs,
        [whole((width, width))] * 2,
        grid=(pairs,),
    )


def grad_input_kernel(docs, src_ref, gains_ref, *refs):
    gmid_refs, own_refs, oth_refs = (refs[i * docs : (i + 1) * docs] for i in range(3))
    full_ref, send_ref, ggain_ref = refs[3 * docs :]
    seq = gmid_refs[0].shape[0]
    ggain = jnp.zeros(ggain_ref.shape, F32)
    for doc in range(docs):
        for start in range(0, seq, CHUNK):
            here = slice(start, start + CHUNK)
            at = slice(doc * seq + start, doc * seq + start + CHUNK)
            gnorm = own_refs[doc][here, :].astype(F32) + oth_refs[doc][here, :].astype(F32)
            v = src_ref[at, :].astype(F32)
            r = rms_rows(v)
            ggain = ggain + jnp.sum(gnorm * v * r, axis=0, keepdims=True)
            back = gains_ref[:1, :] * gnorm
            inner = jnp.mean(back * v, axis=-1, keepdims=True)
            out = gmid_refs[doc][here, :] + r * back - v * (r * r * r * inner)
            full_ref[at, :] = out
            send_ref[at, :] = out
    ggain_ref[...] = ggain


def grad_input(ids, inputs, gains, gmids, owns, oths, docs):
    seq, width = gmids[0].shape
    rows = docs * seq
    mine = pl.BlockSpec((rows, width), lambda i: (lax.axis_index("core"), 0))
    return call(
        functools.partial(grad_input_kernel, docs),
        "grad_input",
        ids,
        (inputs, gains) + tuple(gmids) + tuple(owns) + tuple(oths),
        [mine, whole(gains.shape)] + [whole((seq, width))] * (3 * docs),
        [shape_of((2 * rows, width), F32), shape_of((rows, width), F32), shape_of((1, width), F32)],
        [mine, whole((rows, width)), whole((1, width))],
    )


def mix_kernel(docs, *refs):
    middle_refs, own_refs, oth_refs = (refs[i * docs : (i + 1) * docs] for i in range(3))
    full_ref, send_ref = refs[3 * docs :]
    seq = middle_refs[0].shape[0]
    for doc in range(docs):
        at = slice(doc * seq, (doc + 1) * seq)
        terms = own_refs[doc][...].astype(F32) + oth_refs[doc][...].astype(F32)
        out = (middle_refs[doc][...] + terms).astype(BF16)
        full_ref[at, :] = out
        send_ref[at, :] = out


def mix(ids, middles, owns, oths, docs):
    seq, width = middles[0].shape
    rows = docs * seq
    return call(
        functools.partial(mix_kernel, docs),
        "mix",
        ids,
        tuple(middles) + tuple(owns) + tuple(oths),
        [whole((seq, width))] * (3 * docs),
        [shape_of((2 * rows, width), BF16), shape_of((rows, width), BF16)],
        [pl.BlockSpec((rows, width), lambda i: (lax.axis_index("core"), 0)), whole((rows, width))],
    )


def place_kernel(full_ref, got_ref, out_ref):
    out_ref[...] = got_ref[...]


def place(ids, full, got):
    rows, width = got.shape
    steps = 4
    part = rows // steps
    return call(
        place_kernel,
        "place",
        ids,
        (full, got),
        [pl.BlockSpec(memory_space=pl.ANY), pl.BlockSpec((part, width), lambda i: (i, 0))],
        [shape_of(full.shape, full.dtype)],
        [pl.BlockSpec((part, width), lambda i: ((1 - lax.axis_index("core")) * steps + i, 0))],
        grid=(steps,),
        aliases={1: 1},
    )


def gate(ids, *arrays):
    anywhere = [pl.BlockSpec(memory_space=pl.ANY)] * len(arrays)
    shapes = [shape_of(v.shape, v.dtype) for v in arrays]
    aliases = {i + 1: i + 1 for i in range(len(arrays))}
    return call(lambda *refs: None, "gate", ids, arrays, anywhere, shapes, anywhere, aliases=aliases)


def need(ids, *arrays):
    anywhere = pl.BlockSpec(memory_space=pl.ANY)
    return call(lambda *refs: None, "need", ids, arrays, [anywhere] * len(arrays), [], [])[1]


def sum_core_kernel(*refs):
    for i, out_ref in enumerate(refs[2 * len(refs) // 3 :]):
        out_ref[...] = (refs[2 * i][...].astype(F32) + refs[2 * i + 1][...].astype(F32)).astype(BF16)


def sum_core(ids, *arrays):
    steps = 2
    specs = [pl.BlockSpec((v.shape[0] // steps, v.shape[1]), lambda i: (i, 0)) for v in arrays]
    outs = [shape_of(v.shape, BF16) for v in arrays[::2]]
    return call(sum_core_kernel, "sum_core", ids, arrays, specs, outs, specs[::2], grid=(steps,))


def widen_kernel(*refs):
    half = len(refs) // 2
    for src, dst in zip(refs[:half], refs[half:]):
        dst[...] = src[...].astype(F32)


def widen_attn(ids, total):
    steps = 4
    width = total.shape[1]
    part = total.shape[0] // (4 * steps)
    specs = [
        pl.BlockSpec((3 * part, width), lambda i: (i, 0)),
        pl.BlockSpec((part, width), lambda i: (3 * steps + i, 0)),
    ]
    return call(
        widen_kernel,
        "widen_attn",
        ids,
        (total, total),
        specs,
        [shape_of((12 * part, width), F32), shape_of((4 * part, width), F32)],
        [pl.BlockSpec((n * part, width), lambda i: (i, 0)) for n in (3, 1)],
        grid=(steps,),
    )


def widen(ids, *arrays):
    steps = 4
    specs = [pl.BlockSpec((v.shape[0] // steps, v.shape[1]), lambda i: (i, 0)) for v in arrays]
    return call(
        widen_kernel, "widen", ids, arrays, specs, [shape_of(v.shape, F32) for v in arrays], specs, grid=(steps,)
    )


def sum_kernel(got_ref, out_ref, total_ref):
    rows = out_ref.shape[0]
    parts = got_ref.shape[0] // rows

    @pl.when(pl.program_id(0) == 0)
    def _():
        total = got_ref[:rows, :].astype(F32)
        for i in range(1, parts):
            total = total + got_ref[i * rows : (i + 1) * rows, :].astype(F32)
        total_ref[...] = total.astype(BF16)

    out_ref[...] = total_ref[...]


def sum_parts(token, got, dp):
    width = got.shape[1]
    rows = got.shape[0] // dp
    if rows % 16:
        total = jnp.sum(got.reshape(dp, rows, width).astype(F32), axis=0).astype(BF16)
        return [jnp.tile(total, (dp, 1))], token
    return call(
        sum_kernel,
        "sum_parts",
        token,
        (got,),
        [whole(got.shape)],
        [shape_of((dp * rows, width), BF16)],
        [pl.BlockSpec((rows, width), lambda i: (i, 0))],
        grid=(dp,),
        scratch=[pltpu.VMEM((rows, width), BF16)],
    )


def region(always, fn, ids):
    outs = jax.eval_shape(fn, ids)
    return lax.cond(always, fn, lambda _: jax.tree.map(lambda o: jnp.zeros(o.shape, o.dtype), outs), ids)


def per_device(dp, inputs, gain_attn, w_qkv, w_out, gain_ffn, w_in, w_back, bias_table, lengths, buckets, cotangent):
    width = inputs.shape[1]
    seq = buckets.shape[0]
    docs = lengths.shape[0] // 2
    table_rows, heads = bias_table.shape
    gains = jnp.stack([gain_attn, gain_ffn]).astype(F32)
    ids = jnp.zeros((8, 128), F32)

    def from_core(v):
        return lax.ppermute(v, "core", [(0, 1), (1, 0)])

    def from_x(v):
        return lax.ppermute(v, "x", [(0, 1), (1, 0)])

    def spread(v):
        return lax.all_to_all(v, "dp", 0, 0, tiled=True)

    bias = jnp.pad(bias_table.T, ((0, BIAS_ROWS - heads), (0, width - table_rows)))
    attn_w = jnp.concatenate([w_qkv.transpose(0, 2, 1).reshape(-1, width), bias], axis=0)
    attn_w = jnp.concatenate([attn_w[: 3 * width // 4], w_out, attn_w[3 * width // 4 :]], axis=0)
    attn_c = from_core(attn_w)
    wo_x = from_x(w_out)
    wo_c = from_core(w_out)
    in_c = from_core(w_in)
    back_c = from_core(w_back)

    every = range(docs)
    normed, packed, probs, att, att_x = [], [], [], [], []
    for doc in every:
        if doc == 0:
            (w_own, u, n, a, b, c), ids = attn_fwd(
                ids, lengths, inputs, gains, (attn_w, attn_c), buckets, doc, docs
            )
            (wo_x,), ids = gate(ids, wo_x)
            wo_xc = from_core(wo_x)
        else:
            (n, a, b, c), ids = attn_fwd(ids, lengths, inputs, gains, (w_own, u), buckets, doc, docs)
        normed.append(n)
        packed.append(a)
        probs.append(b)
        att.append(c)
        att_x.append(from_x(c))

    middle, gown, hown, goth, grads = [], [], [], [], None
    for doc in every:
        (m, g, h, *grads), ids = ffn(
            ids, inputs, att[doc], att_x[doc], (w_out, wo_c, wo_x, wo_xc), gains, cotangent,
            (w_in, in_c), (w_back, back_c), grads, doc, docs,
        )
        middle.append(m)
        hown.append(h)
        if doc + 1 < docs:
            ids = need(ids, att_x[doc + 1])
        (g,), ids = gate(ids, g)
        gown.append(g)
        goth.append(from_x(g))
    always = lengths[0] > 0

    def ffn_grads(ids):
        gback, gback_c, gin, gin_c = grads
        return sum_core(ids, gback, from_core(gback_c), gin, from_core(gin_c))[::-1]

    ids = need(ids, goth[0])
    ids, (gback, gin) = region(always, ffn_grads, ids)
    gback, gin = lax.psum((gback, gin), "dp")

    def back_of(doc, ids):
        res, ids = attn_bwd(
            ids, middle[doc], gown[doc], goth[doc], gains, cotangent, w_out, wo_c, w_own, packed[doc], probs[doc],
            doc, docs,
        )
        return ids, res

    ids, first = back_of(0, ids)
    ids = need(ids, *goth[1:])

    def attention_back(ids):
        (nown_0,), ids = gate(ids, first[4])
        noth = [from_x(nown_0)]

        def others(ids):
            results = [first]
            for doc in range(1, docs):
                ids, res = back_of(doc, ids)
                results.append(res)
            gp, low = [r[3] for r in results], [r[1] for r in results]
            (gattn, gattn_c), ids = grad_attn(ids, normed, gp, low, att, docs)
            return ids, results[1:], gattn, gattn_c

        ids, results, gattn, gattn_c = region(always, others, ids)
        gmid, low, ggain_two, gp, nown, diag = zip(first, *results)
        ids = need(ids, noth[0])
        (gattn_c,), ids = gate(ids, gattn_c)
        (gattn,), ids = sum_core(ids, gattn, from_core(gattn_c))
        gattn = spread(gattn)

        def rows_back(ids):
            mine, got = [nown_0] + list(nown[1:]), list(noth)
            for doc in range(1, docs):
                (mine[doc],), ids = gate(ids, mine[doc])
                got.append(from_x(mine[doc]))
            sent, hoth = list(hown), []
            for doc in range(docs // 2):
                (sent[doc],), ids = gate(ids, sent[doc])
                hoth.append(from_x(sent[doc]))
            (gsrc, gsrc_send, ggain_one), ids = grad_input(ids, inputs, gains, gmid, mine, got, docs)
            diag_bucket = jnp.concatenate([buckets[:, 0], buckets[:1, -1], buckets[:-1, -1]])
            one_hot = (diag_bucket[:, None] == jnp.arange(table_rows)[None, :]).astype(F32)
            diags = sum(diag).reshape(2 * heads, 2 * seq)
            table = lax.dot_general(
                diags, one_hot, (((1,), (0,)), ((), ())), precision=lax.Precision.HIGHEST, preferred_element_type=F32
            )
            ggain_ffn = sum(ggain_two)
            small = jnp.concatenate([ggain_one.reshape(-1), ggain_ffn.reshape(-1), table[:heads].reshape(-1)])
            small_send = jnp.concatenate([ggain_one.reshape(-1), ggain_ffn.reshape(-1), table[heads:].reshape(-1)])
            small = small + from_core(small_send)
            for s in range(dp.bit_length() - 1):
                small = small + lax.ppermute(small, "dp", [(i, i ^ (1 << s)) for i in range(dp)])
            grad_gain_attn, grad_gain_ffn = small[:width], small[width : 2 * width]
            grad_table = small[2 * width :].reshape(heads, table_rows).T
            ids = need(ids, grad_gain_attn, grad_gain_ffn, grad_table)
            (gsrc,), ids = place(ids, gsrc, from_core(gsrc_send))
            ids = need(ids, *hoth)
            return ids, gsrc, (grad_gain_attn, grad_gain_ffn, grad_table), sent, hoth

        ids, gsrc, smalls, hsent, hoth = region(always, rows_back, ids)
        (gattn,), ids = sum_parts(ids, gattn, dp)
        return ids, gattn, gsrc, smalls, hsent, hoth

    ids, gattn, gsrc, smalls, hsent, hoth = region(always, attention_back, ids)
    grad_gain_attn, grad_gain_ffn, grad_table = smalls
    for doc in range(docs // 2, docs):
        (hsent[doc],), ids = gate(ids, hsent[doc])
        hoth.append(from_x(hsent[doc]))
    gattn = spread(gattn)
    (grad_w_back, grad_w_in), ids = widen(ids, gback, gin)
    (mixed, mixed_send), ids = mix(ids, middle, hsent, hoth, docs)
    mixed_got = from_core(mixed_send)
    (mixed,), ids = place(ids, mixed, mixed_got)
    (grad_w_qkv, grad_w_out), ids = widen_attn(ids, gattn)
    grad_w_qkv = grad_w_qkv.reshape(3, width // 4, width).transpose(0, 2, 1)
    return (
        mixed,
        gsrc,
        grad_gain_attn,
        grad_w_qkv,
        grad_w_out,
        grad_gain_ffn,
        grad_w_in,
        grad_w_back,
        grad_table,
    )


def solution(mesh):
    dp = mesh.shape["dp"]
    devices = mesh.devices.reshape(mesh.shape["tensor"] // 2, 2, dp)
    mesh = jax.sharding.Mesh(devices, ("x", "core", "dp"))
    return jax.shard_map(
        functools.partial(per_device, dp),
        mesh=mesh,
        in_specs=(
            P("dp", None),
            P(),
            P(None, None, ("x", "core")),
            P(("x", "core"), None),
            P(),
            P(None, ("x", "core")),
            P(("x", "core"), None),
            P(None, ("x", "core")),
            P("dp"),
            P(),
            P("dp", None),
        ),
        out_specs=(
            P("dp", None),
            P("dp", None),
            P(),
            P(None, None, ("x", "core")),
            P(("x", "core"), None),
            P(),
            P(None, ("x", "core")),
            P(("x", "core"), None),
            P(None, ("x", "core")),
        ),
        check_vma=False,
    )
```
